512 devices in a mesh: row: 32 (over z_lo, y, core), col: 4 (over z_hi), rep: 4 (over x).
Axes of the slice: x: 4, y: 4, z: 16 (z_hi: 4, z_lo: 4; z = z_hi * 4 + z_lo), core: 2. Of those that a mesh axis runs over, the one named last changes fastest.
Arguments:
- images: bfloat16 [4, 96, 512, 512], P('rep', None, 'row', 'col'), may hold values from -6 to 6
- gain_first: float32 [96], replicated, may hold values from 0.1 to 1.9
- filter_first: float32 [2, 96, 512, 512], P(None, 'row', 'col'), may hold values from -6 to 6
- reduce_weight: bfloat16 [192, 384], replicated, may hold values from -0.3125 to 0.3125
- gain_second: float32 [192], replicated, may hold values from 0.1 to 1.9
- filter_second: float32 [2, 192, 256, 256], P(None, 'row', 'col'), may hold values from -6 to 6
- grad_out: bfloat16 [4, 192, 256, 256], P('rep', None, 'row', 'col'), may hold values from -6 to 6
Outputs:
- grad_images: bfloat16 [4, 96, 512, 512], P('rep', None, 'row', 'col')
- grad_filter_first: float32 [2, 96, 512, 512], P(None, 'row', 'col', 'rep')
- grad_filter_second: float32 [2, 192, 256, 256], P(None, 'row', 'col', 'rep')
The draws below stay inside these ranges and needn't reach their ends.
All inputs are finite; a program needn't handle non-finite values.
Results may differ from the reference program's by a relative error of at most 0.022.
Values may be sent and summed in bfloat16 or wider, within the bound.
No kernel may reach another device: no remote copies, remote signals or barrier semaphores. Data moves between devices by JAX's collectives and lax.ppermute only.
A program may use at most 64 MiB of HBM per device.

```python
import math
import jax
import jax.numpy as jnp
from jax import lax

C1 = 96
C2 = 192
H1 = 512
W1 = 512
H2 = 256
W2 = 256
B = 4


def steps_of(key, dims, pieces, smallest, top_value):
    factor_of, own = 1.0, jax.random.fold_in(key, 6)
    for axis_at, blocks in pieces:
        draws = jnp.exp(jax.random.uniform(jax.random.fold_in(own, axis_at), (blocks,), jnp.float32, smallest / len(pieces), top_value / len(pieces)))
        factor_of = factor_of * jnp.repeat(draws, dims[axis_at] // blocks).reshape([-1 if axis == axis_at else 1 for axis in range(len(dims))])
    return factor_of


def normal_values(key, shape, scale, reach, shards=(), held_as=jnp.bfloat16):
    gain = steps_of(key, shape, shards, -0.22, 0.18) if shards else 1.0
    array = jax.random.normal(key, shape, jnp.float32) * scale * gain
    return jnp.minimum(jnp.maximum(array, -reach), reach).astype(held_as)


def setup_inputs(seed: int = 0) -> dict:
    arg_keys = jax.random.split(jax.random.key(seed), 8)
    return {
        "images": normal_values(arg_keys[0], (B, C1, H1, W1), 1.0, 6.0, ((0, 4), (2, 32), (3, 4))),
        "gain_first": jnp.clip(1.0 + 0.18 * jax.random.normal(arg_keys[1], (C1,), jnp.float32), 0.1, 1.9),
        "filter_first": normal_values(arg_keys[2], (2, C1, H1, W1), 1.0, 6.0, ((1, 32), (2, 4)), jnp.float32),
        "reduce_weight": normal_values(arg_keys[3], (C2, 4 * C1), (4 * C1) ** -0.5, 0.3125),
        "gain_second": jnp.clip(1.0 + 0.18 * jax.random.normal(arg_keys[4], (C2,), jnp.float32), 0.1, 1.9),
        "filter_second": normal_values(arg_keys[5], (2, C2, H2, W2), 1.0, 6.0, ((1, 32), (2, 4)), jnp.float32),
        "grad_out": normal_values(arg_keys[6], (B, C2, H2, W2), 1.0, 6.0, ((0, 4), (2, 32), (3, 4))),
    }


epsilon = 1e-06

def tables(length):
    indices = jnp.arange(length, dtype=jnp.int32)
    product = indices[:, None] * indices[None, :] % length
    angles = product.astype(jnp.float32) * (2.0 * math.pi / length)
    factor = 1.0 / math.sqrt(length)
    return ((jnp.cos(angles) * factor).astype(jnp.bfloat16), (jnp.sin(angles) * factor).astype(jnp.bfloat16))

def contract(pattern, first_op, second_op):
    return jnp.einsum(pattern, first_op.astype(jnp.float32), second_op.astype(jnp.float32), precision=lax.Precision.HIGHEST)

def layer_normalize(entry_values, gains):
    center = entry_values - lax.optimization_barrier(jnp.mean(entry_values, axis=0, keepdims=True))
    spread = lax.optimization_barrier(jnp.mean(center * center, axis=0, keepdims=True))
    return center * lax.rsqrt(spread + epsilon) * gains[:, None, None]

def norm_pullback_step(entry_values, gains, upstream):
    _, pullback = jax.vjp(lambda inner_vals: layer_normalize(inner_vals, gains), entry_values)
    return pullback(upstream.astype(jnp.float32))[0]

def spectrum(entry_values, row_tab, col_tab):
    row_cos, row_sin = row_tab
    col_cos, col_sin = col_tab
    half_real = contract('kh,chw->ckw', row_cos, entry_values).astype(jnp.bfloat16)
    half_imag = (-contract('kh,chw->ckw', row_sin, entry_values)).astype(jnp.bfloat16)
    spec_real = contract('chw,wk->chk', half_real, col_cos) + contract('chw,wk->chk', half_imag, col_sin)
    spec_imag = contract('chw,wk->chk', half_imag, col_cos) - contract('chw,wk->chk', half_real, col_sin)
    return (spec_real, spec_imag)

def inverse(real_part, imag_part, row_tab, col_tab):
    row_cos, row_sin = row_tab
    col_cos, col_sin = col_tab
    rot_real = (contract('chk,kw->chw', real_part, col_cos) - contract('chk,kw->chw', imag_part, col_sin)).astype(jnp.bfloat16)
    rot_imag = (contract('chk,kw->chw', imag_part, col_cos) + contract('chk,kw->chw', real_part, col_sin)).astype(jnp.bfloat16)
    result = contract('hk,ckw->chw', row_cos, rot_real) - contract('hk,ckw->chw', row_sin, rot_imag)
    return result.astype(jnp.bfloat16)

def filtered(weights, spec_real, spec_imag):
    return ((weights[0] * spec_real - weights[1] * spec_imag).astype(jnp.bfloat16), (weights[0] * spec_imag + weights[1] * spec_real).astype(jnp.bfloat16))

def filtered_back(weights, grad_real, grad_imag):
    return ((weights[0] * grad_real + weights[1] * grad_imag).astype(jnp.bfloat16), (weights[0] * grad_imag - weights[1] * grad_real).astype(jnp.bfloat16))

def filter_grad(grad_real, grad_imag, spec_real, spec_imag):
    return jnp.stack([grad_real * spec_real + grad_imag * spec_imag, grad_imag * spec_real - grad_real * spec_imag])

def strided_reduce(entry_values, weight_matrix):
    patches = entry_values.reshape(C1, H2, 2, W2, 2).transpose(2, 4, 0, 1, 3).reshape(4 * C1, H2, W2)
    return contract('ok,kij->oij', weight_matrix, patches).astype(jnp.bfloat16)

def upsample(upstream, weight_matrix):
    patches = contract('ok,oij->kij', weight_matrix, upstream)
    return patches.reshape(2, 2, C1, H2, W2).transpose(2, 3, 0, 4, 1).reshape(C1, H1, W1).astype(jnp.bfloat16)

def reference(images, gain_first, filter_first, reduce_weight, gain_second, filter_second, grad_out):
    rows_one = tables(H1)
    cols_one = tables(W1)
    rows_two = tables(H2)
    cols_two = tables(W2)

    def per_image(totals, item):
        pixels, upstream = item
        pixels_wide = pixels.astype(jnp.float32)
        norm_one = layer_normalize(pixels_wide, gain_first).astype(jnp.bfloat16)
        spec_one_r, spec_one_i = spectrum(norm_one, rows_one, cols_one)
        mixed_r, mixed_i = filtered(filter_first, spec_one_r, spec_one_i)
        mixed_one = inverse(mixed_r, mixed_i, rows_one, cols_one)
        first_filter_section = (pixels_wide + mixed_one.astype(jnp.float32)).astype(jnp.bfloat16)
        reduced_grid = strided_reduce(first_filter_section, reduce_weight)
        down_wide = reduced_grid.astype(jnp.float32)
        norm_two = layer_normalize(down_wide, gain_second).astype(jnp.bfloat16)
        spec_two_r, spec_two_i = spectrum(norm_two, rows_two, cols_two)
        grad_two_r, grad_two_i = spectrum(upstream, rows_two, cols_two)
        term_two = filter_grad(grad_two_r, grad_two_i, spec_two_r, spec_two_i)
        dspec_r, dspec_i = filtered_back(filter_second, grad_two_r, grad_two_i)
        grad_norm_two = inverse(dspec_r, dspec_i, rows_two, cols_two)
        grad_down = (upstream.astype(jnp.float32) + norm_pullback_step(down_wide, gain_second, grad_norm_two)).astype(jnp.bfloat16)
        grad_section = upsample(grad_down, reduce_weight)
        grad_one_r, grad_one_i = spectrum(grad_section, rows_one, cols_one)
        term_one = filter_grad(grad_one_r, grad_one_i, spec_one_r, spec_one_i)
        dspec_one_r, dspec_one_i = filtered_back(filter_first, grad_one_r, grad_one_i)
        grad_norm_one = inverse(dspec_one_r, dspec_one_i, rows_one, cols_one)
        grad_pixels = (grad_section.astype(jnp.float32) + norm_pullback_step(pixels_wide, gain_first, grad_norm_one)).astype(jnp.bfloat16)
        return ((totals[0] + term_one, totals[1] + term_two), grad_pixels)
    start = (jnp.zeros((2, C1, H1, W1), jnp.float32), jnp.zeros((2, C2, H2, W2), jnp.float32))
    sums, grad_images = lax.scan(per_image, start, (images, grad_out))
    return (grad_images, sums[0], sums[1])
```

```python
import functools
import math

import jax
import jax.numpy as jnp
import numpy as np
from jax import lax
from jax.experimental import pallas as pl
from jax.experimental.pallas import tpu as pltpu
from jax.sharding import PartitionSpec as P

H1 = 512
H2 = 256
GROUPS = 3
COLS = 4
ROWS = 32
LANES = 128

epsilon = 1e-06

ORDER = (0, 2, 3, 1)
SWAP = ((0, 3), (3, 0), (1, 2), (2, 1))


def cos_sin(n):
    index = np.arange(n)
    angles = (index[:, None] * index[None, :] % n) * (2.0 * math.pi / n)
    factor = 1.0 / math.sqrt(n)
    return np.cos(angles) * factor, np.sin(angles) * factor


def row_table(n):
    cos, sin = cos_sin(n)
    slots = n // 8
    parts = []
    for c in range(COLS):
        k = ORDER[c] * slots + np.arange(slots)
        real, imag = cos[k], -sin[k]
        if c == 0:
            imag[0] = cos[n // 2]
        parts += [real, imag]
    return np.concatenate(parts, axis=0)


def col_tables(n):
    cos, sin = cos_sin(n)
    pair = 512 // n
    width = LANES // pair
    if pair == 1:
        return cos, sin
    out = []
    for table in (cos, sin):
        blocks = table.reshape(COLS, width, COLS, width)
        full = np.zeros((COLS, pair, width, COLS, pair, width))
        for p in range(pair):
            full[:, p, :, :, p, :] = blocks
        out.append(full.reshape(512, 512))
    return tuple(out)


def mirror_matrix(slots):
    matrix = np.zeros((2 * slots, 2 * slots))
    for s in range(slots):
        matrix[s, slots - s] = 1.0
        matrix[slots + s, (2 * slots - s) % (2 * slots)] = 1.0
    return matrix


def constant(values):
    return jnp.asarray(np.asarray(values, np.float32).astype(jnp.bfloat16))


def dot(a, b):
    return jnp.dot(a, b, preferred_element_type=jnp.float32)


def params(flops, traffic):
    return dict(
        compiler_params=pltpu.CompilerParams(vmem_limit_bytes=40 * 1024 * 1024),
        cost_estimate=pl.CostEstimate(flops=flops, bytes_accessed=traffic, transcendentals=0),
    )


def gather_rows(block, rows):
    parts = []
    for g in range(GROUPS):
        part = block[:, g * rows : (g + 1) * rows, :]
        if rows % 16:
            part = part.astype(jnp.float32)
        parts.append(part.reshape(ROWS * rows, LANES).astype(jnp.bfloat16))
    return jnp.concatenate(parts, axis=1)


def forward_rows_kernel(layout, *refs):
    x_ref, tables, out_ref = refs[0], refs[1:-1], refs[-1]
    for (n, first_in, first_out), table in zip(layout, tables):
        rows = n // ROWS
        slots = n // 8
        block = x_ref[:, first_in : first_in + GROUPS * rows, :]
        half = dot(table[...], gather_rows(block, rows)).astype(jnp.bfloat16)
        half = half.reshape(COLS, 2, slots, GROUPS * LANES)
        for part in range(2):
            for g in range(GROUPS):
                at = first_out + (part * GROUPS + g) * slots
                out_ref[:, at : at + slots, :] = half[:, part, :, g * LANES : (g + 1) * LANES]


def forward_rows(entries, sizes):
    layout, first_in, first_out = [], 0, 0
    for n in sizes:
        layout.append((n, first_in, first_out))
        first_in += GROUPS * n // ROWS
        first_out += 2 * GROUPS * n // 8
    flops = sum(2 * n * n * GROUPS * LANES for n in sizes)
    return pl.pallas_call(
        functools.partial(forward_rows_kernel, tuple(layout)),
        out_shape=jax.ShapeDtypeStruct((COLS, first_out, LANES), jnp.bfloat16),
        name="forward_rows_" + "_".join(str(n) for n in sizes),
        **params(flops, 2 << 20),
    )(entries, *[constant(row_table(n)) for n in sizes])


def inverse_rows_kernel(n, x_ref, table, out_ref):
    rows = n // ROWS
    slots = n // 8
    parts = []
    for g in range(GROUPS):
        both = [
            x_ref[:, (part * GROUPS + g) * slots : (part * GROUPS + g + 1) * slots, :].reshape(
                COLS, 1, slots, LANES
            )
            for part in range(2)
        ]
        parts.append(jnp.concatenate(both, axis=1).reshape(n, LANES))
    result = dot(table[...], jnp.concatenate(parts, axis=1))
    pieces = [
        result[:, g * LANES : (g + 1) * LANES].reshape(ROWS, rows, LANES) for g in range(GROUPS)
    ]
    out_ref[...] = jnp.concatenate(pieces, axis=1).astype(jnp.bfloat16)


def inverse_rows(entries, n):
    return pl.pallas_call(
        functools.partial(inverse_rows_kernel, n),
        out_shape=jax.ShapeDtypeStruct((ROWS, GROUPS * n // ROWS, LANES), jnp.bfloat16),
        name="inverse_rows_" + str(n),
        **params(2 * n * n * GROUPS * LANES, 2 << 20),
    )(entries, constant(row_table(n).T))


def wide(ref, first, count):
    return jnp.concatenate([ref[q, first : first + count, :] for q in range(COLS)], axis=1)


def spectrum(ref, first, slots, special, cos, sin):
    count = GROUPS * slots
    real, imag = wide(ref, first, count), wide(ref, first + count, count)
    real_cos, real_sin = dot(real, cos), dot(real, sin)
    imag_cos, imag_sin = dot(imag, cos), dot(imag, sin)
    return (
        jnp.where(special, real_cos, real_cos + imag_sin),
        jnp.where(special, -real_sin, imag_cos - real_sin),
        jnp.where(special, imag_cos, real_cos - imag_sin),
        jnp.where(special, -imag_sin, -imag_cos - real_sin),
    )


def filters(near, kept_ref, recv_ref, first, slots):
    count = GROUPS * slots
    out = []
    for part in range(2):
        kept = wide(kept_ref, first + part * count, count).astype(jnp.float32)
        recv = wide(recv_ref, first + part * count, count).astype(jnp.float32)
        out.append((jnp.where(near, kept, recv), jnp.where(near, recv, kept)))
    return out


def put_inverse(out_ref, slots, special, up, down, cos, sin):
    count = GROUPS * slots
    (up_r, up_i), (down_r, down_i) = up, down
    bf16 = jnp.bfloat16
    sum_r = jnp.where(special, up_r, up_r + down_r).astype(bf16)
    sum_i = jnp.where(special, up_i, up_i + down_i).astype(bf16)
    dif_i = jnp.where(special, down_r, up_i - down_i).astype(bf16)
    dif_r = jnp.where(special, -down_i, up_r - down_r).astype(bf16)
    rot_real = (dot(sum_r, cos) - dot(sum_i, sin)).astype(bf16)
    rot_imag = (dot(dif_i, cos) + dot(dif_r, sin)).astype(bf16)
    for q in range(COLS):
        out_ref[q, :count, :] = rot_real[:, q * LANES : (q + 1) * LANES]
        out_ref[q, count:, :] = rot_imag[:, q * LANES : (q + 1) * LANES]


def masks(col_ref, slots):
    col = col_ref[0]
    row = lax.broadcasted_iota(jnp.int32, (GROUPS * slots, 512), 0)
    return (lax.rem(row, slots) + col * slots) == 0, col < 2


def mix_forward_kernel(n, first_filter, col_ref, x_ref, kept_ref, recv_ref, cos, sin, out_ref):
    slots = n // 8
    special, near = masks(col_ref, slots)
    up_r, up_i, down_r, down_i = spectrum(x_ref, 0, slots, special, cos[...], sin[...])
    real, imag = filters(near, kept_ref, recv_ref, first_filter, slots)
    up = (real[0] * up_r - imag[0] * up_i, real[0] * up_i + imag[0] * up_r)
    down = (real[1] * down_r - imag[1] * down_i, real[1] * down_i + imag[1] * down_r)
    put_inverse(out_ref, slots, special, up, down, cos[...], sin[...])


def mix_back_kernel(
    n, first_filter, first_field, first_grad, col_ref, x_ref, g_ref, kept_ref, recv_ref,
    cos, sin, cos_back, sin_back, out_ref, grad_ref,
):
    slots = n // 8
    count = GROUPS * slots
    special, near = masks(col_ref, slots)
    field = spectrum(x_ref, first_field, slots, special, cos[...], sin[...])
    grad = spectrum(g_ref, first_grad, slots, special, cos[...], sin[...])
    real, imag = filters(near, kept_ref, recv_ref, first_filter, slots)
    sides, terms = [], []
    for side in range(2):
        g_r, g_i = grad[2 * side], grad[2 * side + 1]
        s_r, s_i = field[2 * side], field[2 * side + 1]
        sides.append((real[side] * g_r + imag[side] * g_i, real[side] * g_i - imag[side] * g_r))
        terms.append((g_r * s_r + g_i * s_i, g_i * s_r - g_r * s_i))
    put_inverse(out_ref, slots, special, sides[0], sides[1], cos_back[...], sin_back[...])
    for part in range(2):
        up, down = terms[0][part], terms[1][part]
        kept = jnp.where(near, up, down).astype(jnp.bfloat16)
        sent = jnp.where(near, down, up).astype(jnp.bfloat16)
        for q in range(COLS):
            lanes = slice(q * LANES, (q + 1) * LANES)
            grad_ref[q, part * count : (part + 1) * count, :] = kept[:, lanes]
            grad_ref[q, (2 + part) * count : (3 + part) * count, :] = sent[:, lanes]


def smem():
    return pl.BlockSpec(memory_space=pltpu.SMEM)


def vmem(count):
    return [pl.BlockSpec(memory_space=pltpu.VMEM)] * count


def mix_forward(n, col, entries, kept, recv, first_filter):
    rows = 2 * GROUPS * n // 8
    cos, sin = col_tables(n)
    return pl.pallas_call(
        functools.partial(mix_forward_kernel, n, first_filter),
        out_shape=jax.ShapeDtypeStruct((COLS, rows, LANES), jnp.bfloat16),
        in_specs=[smem()] + vmem(5),
        name="mix_forward_" + str(n),
        **params(8 * rows * 512 * 512, 4 << 20),
    )(col, entries, kept, recv, constant(cos), constant(sin))


def mix_back(n, col, entries, first_field, upstream, first_grad, kept, recv, first_filter):
    rows = 2 * GROUPS * n // 8
    cos, sin = col_tables(n)
    return pl.pallas_call(
        functools.partial(mix_back_kernel, n, first_filter, first_field, first_grad),
        out_shape=(
            jax.ShapeDtypeStruct((COLS, rows, LANES), jnp.bfloat16),
            jax.ShapeDtypeStruct((COLS, 2 * rows, LANES), jnp.bfloat16),
        ),
        in_specs=[smem()] + vmem(8),
        name="mix_back_" + str(n),
        **params(12 * rows * 512 * 512, 6 << 20),
    )(
        col, entries, upstream, kept, recv,
        constant(cos), constant(sin), constant(cos.T), constant(sin.T),
    )


def pair_lanes():
    matrix = np.zeros((2, COLS, 64, COLS, 2, 64))
    for p in range(2):
        for q in range(COLS):
            matrix[p, q, :, q, p, :] = np.eye(64)
    return matrix.reshape(512, 512)


def take_filters_kernel(first_ref, second_ref, pick_first, pick_second, lanes, kept_ref, sent_ref):
    at = 0
    for n, pick in ((H1, pick_first), (H2, pick_second)):
        slots = n // 8
        for part in range(2):
            for g in range(GROUPS):
                if n == H1:
                    rows = first_ref[part, g].astype(jnp.bfloat16)
                else:
                    pair = [second_ref[part, 2 * g + i].astype(jnp.bfloat16) for i in range(2)]
                    rows = dot(jnp.concatenate(pair, axis=1), lanes[...]).astype(jnp.bfloat16)
                rows = dot(pick[...], rows).astype(jnp.bfloat16)
                for q in range(COLS):
                    cut = slice(q * LANES, (q + 1) * LANES)
                    kept_ref[q, at : at + slots, :] = rows[:slots, cut]
                    sent_ref[q, at : at + slots, :] = rows[slots:, cut]
                at += slots


def slot_zero(block, first, slots):
    count = 2 * GROUPS * slots
    return block[first : first + count].reshape(2 * GROUPS, slots, LANES)[:, :1]


def put_slot_zero(block, zero, take, slots):
    shaped = block.reshape(2 * GROUPS, slots, LANES)
    here = (jnp.arange(slots) == 0)[None, :, None] & take
    return jnp.where(here, zero, shaped).reshape(2 * GROUPS * slots, LANES)


def take_filters(filter_first, filter_second, col, pick_first, pick_second):
    rows = 2 * GROUPS * (H1 + H2) // 8
    shape = jax.ShapeDtypeStruct((COLS, rows, LANES), jnp.bfloat16)
    kept, sent = pl.pallas_call(
        take_filters_kernel,
        out_shape=(shape, shape),
        name="take_filters",
        **params(12 * 128 * 128 * 512 * 2, 4 << 20),
    )(filter_first, filter_second, pick_first, pick_second, constant(pair_lanes()))
    quarter = lax.dynamic_index_in_dim(sent, lax.axis_index("rep"), 0, keepdims=False)
    recv = lax.ppermute(quarter, "col", SWAP)
    split = 2 * GROUPS * H1 // 8
    zero = jnp.concatenate(
        [slot_zero(quarter, 0, H1 // 8), slot_zero(quarter, split, H2 // 8)], axis=1
    )
    zero = lax.ppermute(zero, "col", ((2, 0), (3, 1)))
    near = col < 2
    recv = jnp.concatenate(
        [
            put_slot_zero(recv[:split], zero[:, :1], near, H1 // 8),
            put_slot_zero(recv[split:], zero[:, 1:], near, H2 // 8),
        ],
        axis=0,
    )
    return kept, lax.all_gather(recv, "rep", axis=0, tiled=False)


def place_grads_kernel(
    kept_first, recv_first, kept_second, recv_second, pick_first, pick_second, lanes,
    first_ref, second_ref,
):
    for n, pick, kept, recv in (
        (H1, pick_first, kept_first, recv_first),
        (H2, pick_second, kept_second, recv_second),
    ):
        slots = n // 8
        for part in range(2):
            for g in range(GROUPS):
                at = (part * GROUPS + g) * slots
                both = jnp.concatenate([kept[at : at + slots], recv[at : at + slots]], axis=0)
                rows = dot(pick[...], both)
                if n == H1:
                    first_ref[part, g] = rows
                else:
                    rows = rows.astype(jnp.bfloat16)
                    for i in range(2):
                        second_ref[part, 2 * g + i] = dot(rows, lanes[i])


def summed(terms):
    return lax.psum_scatter(terms, "rep", scatter_dimension=0, tiled=False)


def place_grads(sum_first, sum_second, col, pick_first, pick_second):
    count_first, count_second = 2 * GROUPS * H1 // 8, 2 * GROUPS * H2 // 8
    sent = jnp.concatenate([sum_first[count_first:], sum_second[count_second:]], axis=0)
    zero = jnp.concatenate(
        [slot_zero(sent, 0, H1 // 8), slot_zero(sent, count_first, H2 // 8)], axis=1
    )
    recv = lax.ppermute(sent, "col", SWAP)
    zero = lax.ppermute(zero, "col", ((0, 2), (1, 3)))
    far = col >= 2
    recv_first = put_slot_zero(recv[:count_first], zero[:, :1], far, H1 // 8)
    recv_second = put_slot_zero(recv[count_first:], zero[:, 1:], far, H2 // 8)
    lanes = np.zeros((2, 128, 64))
    lanes[0, :64] = np.eye(64)
    lanes[1, 64:] = np.eye(64)
    return pl.pallas_call(
        place_grads_kernel,
        out_shape=(
            jax.ShapeDtypeStruct((2, GROUPS, H1 // 4, LANES), jnp.float32),
            jax.ShapeDtypeStruct((2, 2 * GROUPS, H2 // 4, LANES // 2), jnp.float32),
        ),
        name="place_grads",
        **params(12 * 128 * 128 * 128 * 2, 2 << 20),
    )(
        sum_first[:count_first], recv_first, sum_second[:count_second], recv_second,
        pick_first.T, pick_second.T, constant(lanes),
    )


def layer_normalize(entry_values, gains):
    center = entry_values - jnp.mean(entry_values, axis=1, keepdims=True)
    spread = jnp.mean(center * center, axis=1, keepdims=True)
    return center * lax.rsqrt(spread + epsilon) * gains[None, :, None, None]


def norm_pullback_step(entry_values, gains, upstream):
    _, pullback = jax.vjp(lambda inner_vals: layer_normalize(inner_vals, gains), entry_values)
    return pullback(upstream.astype(jnp.float32))[0]


def offset_table(cols_dev):
    half_cols = cols_dev // 2
    target = np.arange(2 * cols_dev)
    row_off = target // cols_dev
    rest = target % cols_dev
    source = row_off * cols_dev + 2 * (rest % half_cols) + rest // half_cols
    place = np.arange(2 * cols_dev)
    return constant(place[:, None] == source[None, :])


def strided_reduce(entry_values, weight_matrix):
    images_dev, channels, rows_dev, cols_dev = entry_values.shape
    outputs = weight_matrix.shape[0]
    merged = entry_values.reshape(images_dev, channels, rows_dev // 2, 2 * cols_dev)
    placed = jnp.einsum(
        "bcis,st->bcit", merged, offset_table(cols_dev), preferred_element_type=jnp.float32
    ).astype(jnp.bfloat16)
    placed = placed.reshape(images_dev, channels, rows_dev // 2, 4, cols_dev // 2)
    kernel = weight_matrix.reshape(outputs, 4, channels)
    return jnp.einsum("oqc,bciqj->boij", kernel, placed, preferred_element_type=jnp.float32).astype(
        jnp.bfloat16
    )


def upsample(upstream, weight_matrix):
    images_dev, outputs, rows_half, cols_half = upstream.shape
    channels = weight_matrix.shape[1] // 4
    kernel = weight_matrix.reshape(outputs, 4, channels)
    patches = jnp.einsum(
        "oqc,boij->bciqj", kernel, upstream, preferred_element_type=jnp.float32
    ).astype(jnp.bfloat16)
    patches = patches.reshape(images_dev, channels, rows_half, 8 * cols_half // 2)
    spread_back = jnp.einsum(
        "bcit,st->bcis", patches, offset_table(2 * cols_half), preferred_element_type=jnp.float32
    )
    return spread_back.reshape(images_dev, channels, 2 * rows_half, 2 * cols_half).astype(
        jnp.bfloat16
    )


def pack_first(field):
    return field.reshape(ROWS, GROUPS * 16, LANES)


def unpack_first(blocks):
    return blocks.reshape(1, 96, 16, LANES)


def pack_second(field):
    pairs = field.reshape(96, 2, 8, 64).transpose(0, 2, 1, 3)
    return pairs.reshape(ROWS, GROUPS * 8, LANES)


def unpack_second(blocks):
    return blocks.reshape(96, 8, 2, 64).transpose(0, 2, 1, 3).reshape(1, 192, 8, 64)


def exchange(blocks, axis):
    return lax.all_to_all(blocks, axis, split_axis=0, concat_axis=0, tiled=True)


def shards(images, gain_first, filter_first, reduce_weight, gain_second, filter_second, grad_out):
    col = lax.axis_index("col")
    col_word = col.astype(jnp.int32).reshape(1)
    picks = [
        jnp.where(col < 2, constant(np.eye(n // 4)), constant(mirror_matrix(n // 8)))
        for n in (H1, H2)
    ]
    kept, recv = take_filters(filter_first, filter_second, col, *picks)
    second_rows = 2 * GROUPS * H1 // 8

    pixels_wide = images.astype(jnp.float32)
    norm_one = layer_normalize(pixels_wide, gain_first).astype(jnp.bfloat16)
    both = jnp.concatenate([pack_first(norm_one), pack_second(grad_out)], axis=1)
    both = exchange(forward_rows(exchange(both, "row"), (H1, H2)), "col")
    mixed = exchange(mix_forward(H1, col_word, both, kept, recv, 0), "col")
    mixed_one = unpack_first(exchange(inverse_rows(mixed, H1), "row"))

    section_one = (pixels_wide + mixed_one.astype(jnp.float32)).astype(jnp.bfloat16)
    down_wide = strided_reduce(section_one, reduce_weight).astype(jnp.float32)
    norm_two = layer_normalize(down_wide, gain_second).astype(jnp.bfloat16)
    half_two = exchange(forward_rows(exchange(pack_second(norm_two), "row"), (H2,)), "col")
    dspec_two, terms_two = mix_back(
        H2, col_word, half_two, 0, both, second_rows, kept, recv, second_rows
    )
    sum_two = summed(terms_two)
    back_two = inverse_rows(exchange(dspec_two, "col"), H2)
    grad_norm_two = unpack_second(exchange(back_two, "row"))

    grad_down = (
        grad_out.astype(jnp.float32) + norm_pullback_step(down_wide, gain_second, grad_norm_two)
    ).astype(jnp.bfloat16)
    grad_section = upsample(grad_down, reduce_weight)
    half_grad = exchange(forward_rows(exchange(pack_first(grad_section), "row"), (H1,)), "col")
    dspec_one, terms_one = mix_back(H1, col_word, both, 0, half_grad, 0, kept, recv, 0)
    sum_one = summed(terms_one)
    back_one = inverse_rows(exchange(dspec_one, "col"), H1)
    grad_norm_one = unpack_first(exchange(back_one, "row"))
    grad_images = (
        grad_section.astype(jnp.float32)
        + norm_pullback_step(pixels_wide, gain_first, grad_norm_one)
    ).astype(jnp.bfloat16)
    grad_first, grad_second = place_grads(sum_one, sum_two, col, *picks)
    return (grad_images, grad_first, grad_second)


def solution(mesh):
    placed = (
        P("rep", None, "row", "col"),
        P(),
        P(None, "row", "col", None),
        P(),
        P(),
        P(None, "row", "col", None),
        P("rep", None, "row", "col"),
    )
    return jax.shard_map(
        shards,
        mesh=mesh,
        in_specs=placed,
        out_specs=(
            P("rep", None, "row", "col"),
            P(None, "row", "col", "rep"),
            P(None, "row", "col", "rep"),
        ),
        check_vma=False,
    )
```

```python
import functools
import math

import jax
import jax.numpy as jnp
import numpy as np
from jax import lax
from jax.experimental import pallas as pl
from jax.experimental.pallas import tpu as pltpu
from jax.sharding import PartitionSpec as P

H1 = 512
H2 = 256
GROUPS = 3
COLS = 4
ROWS = 32
LANES = 128

epsilon = 1e-06

ORDER = (0, 2, 3, 1)
SWAP = ((0, 3), (3, 0), (1, 2), (2, 1))


def cos_sin(n):
    index = np.arange(n)
    angles = (index[:, None] * index[None, :] % n) * (2.0 * math.pi / n)
    factor = 1.0 / math.sqrt(n)
    return np.cos(angles) * factor, np.sin(angles) * factor


def row_table(n):
    cos, sin = cos_sin(n)
    slots = n // 8
    parts = []
    for c in range(COLS):
        k = ORDER[c] * slots + np.arange(slots)
        real, imag = cos[k], -sin[k]
        if c == 0:
            imag[0] = cos[n // 2]
        parts += [real, imag]
    return np.concatenate(parts, axis=0)


def col_tables(n):
    cos, sin = cos_sin(n)
    pair = 512 // n
    width = LANES // pair
    if pair == 1:
        return cos, sin
    out = []
    for table in (cos, sin):
        blocks = table.reshape(COLS, width, COLS, width)
        full = np.zeros((COLS, pair, width, COLS, pair, width))
        for p in range(pair):
            full[:, p, :, :, p, :] = blocks
        out.append(full.reshape(512, 512))
    return tuple(out)


def mirror_matrix(slots):
    matrix = np.zeros((2 * slots, 2 * slots))
    for s in range(slots):
        matrix[s, slots - s] = 1.0
        matrix[slots + s, (2 * slots - s) % (2 * slots)] = 1.0
    return matrix


def constant(values):
    return jnp.asarray(np.asarray(values, np.float32).astype(jnp.bfloat16))


def dot(a, b):
    return jnp.dot(a, b, preferred_element_type=jnp.float32)


def params(flops, traffic):
    return dict(
        compiler_params=pltpu.CompilerParams(vmem_limit_bytes=40 * 1024 * 1024),
        cost_estimate=pl.CostEstimate(flops=flops, bytes_accessed=traffic, transcendentals=0),
    )


def gather_rows(block, rows):
    parts = []
    for g in range(GROUPS):
        part = block[:, g * rows : (g + 1) * rows, :]
        if rows % 16:
            part = part.astype(jnp.float32)
        parts.append(part.reshape(ROWS * rows, LANES).astype(jnp.bfloat16))
    return jnp.concatenate(parts, axis=1)


def forward_rows_kernel(layout, *refs):
    x_ref, tables, out_ref = refs[0], refs[1:-1], refs[-1]
    for (n, first_in, first_out), table in zip(layout, tables):
        rows = n // ROWS
        slots = n // 8
        block = x_ref[:, first_in : first_in + GROUPS * rows, :]
        half = dot(table[...], gather_rows(block, rows)).astype(jnp.bfloat16)
        half = half.reshape(COLS, 2, slots, GROUPS * LANES)
        for part in range(2):
            for g in range(GROUPS):
                at = first_out + (part * GROUPS + g) * slots
                out_ref[:, at : at + slots, :] = half[:, part, :, g * LANES : (g + 1) * LANES]


def forward_rows(entries, sizes):
    layout, first_in, first_out = [], 0, 0
    for n in sizes:
        layout.append((n, first_in, first_out))
        first_in += GROUPS * n // ROWS
        first_out += 2 * GROUPS * n // 8
    flops = sum(2 * n * n * GROUPS * LANES for n in sizes)
    return pl.pallas_call(
        functools.partial(forward_rows_kernel, tuple(layout)),
        out_shape=jax.ShapeDtypeStruct((COLS, first_out, LANES), jnp.bfloat16),
        name="forward_rows_" + "_".join(str(n) for n in sizes),
        **params(flops, 2 << 20),
    )(entries, *[constant(row_table(n)) for n in sizes])


def inverse_rows_kernel(n, x_ref, table, out_ref):
    rows = n // ROWS
    slots = n // 8
    parts = []
    for g in range(GROUPS):
        both = [
            x_ref[:, (part * GROUPS + g) * slots : (part * GROUPS + g + 1) * slots, :].reshape(
                COLS, 1, slots, LANES
            )
            for part in range(2)
        ]
        parts.append(jnp.concatenate(both, axis=1).reshape(n, LANES))
    result = dot(table[...], jnp.concatenate(parts, axis=1))
    pieces = [
        result[:, g * LANES : (g + 1) * LANES].reshape(ROWS, rows, LANES) for g in range(GROUPS)
    ]
    out_ref[...] = jnp.concatenate(pieces, axis=1).astype(jnp.bfloat16)


def inverse_rows(entries, n):
    return pl.pallas_call(
        functools.partial(inverse_rows_kernel, n),
        out_shape=jax.ShapeDtypeStruct((ROWS, GROUPS * n // ROWS, LANES), jnp.bfloat16),
        name="inverse_rows_" + str(n),
        **params(2 * n * n * GROUPS * LANES, 2 << 20),
    )(entries, constant(row_table(n).T))


def wide(ref, first, count):
    return jnp.concatenate([ref[q, first : first + count, :] for q in range(COLS)], axis=1)


def spectrum(ref, first, slots, special, cos, sin):
    count = GROUPS * slots
    real, imag = wide(ref, first, count), wide(ref, first + count, count)
    real_cos, real_sin = dot(real, cos), dot(real, sin)
    imag_cos, imag_sin = dot(imag, cos), dot(imag, sin)
    return (
        jnp.where(special, real_cos, real_cos + imag_sin),
        jnp.where(special, -real_sin, imag_cos - real_sin),
        jnp.where(special, imag_cos, real_cos - imag_sin),
        jnp.where(special, -imag_sin, -imag_cos - real_sin),
    )


def filters(near, kept_ref, recv_ref, first, slots):
    count = GROUPS * slots
    out = []
    for part in range(2):
        kept = wide(kept_ref, first + part * count, count).astype(jnp.float32)
        recv = wide(recv_ref, first + part * count, count).astype(jnp.float32)
        out.append((jnp.where(near, kept, recv), jnp.where(near, recv, kept)))
    return out


def put_inverse(out_ref, slots, special, up, down, cos, sin):
    count = GROUPS * slots
    (up_r, up_i), (down_r, down_i) = up, down
    bf16 = jnp.bfloat16
    sum_r = jnp.where(special, up_r, up_r + down_r).astype(bf16)
    sum_i = jnp.where(special, up_i, up_i + down_i).astype(bf16)
    dif_i = jnp.where(special, down_r, up_i - down_i).astype(bf16)
    dif_r = jnp.where(special, -down_i, up_r - down_r).astype(bf16)
    rot_real = (dot(sum_r, cos) - dot(sum_i, sin)).astype(bf16)
    rot_imag = (dot(dif_i, cos) + dot(dif_r, sin)).astype(bf16)
    for q in range(COLS):
        out_ref[q, :count, :] = rot_real[:, q * LANES : (q + 1) * LANES]
        out_ref[q, count:, :] = rot_imag[:, q * LANES : (q + 1) * LANES]


def masks(col_ref, slots):
    col = col_ref[0]
    row = lax.broadcasted_iota(jnp.int32, (GROUPS * slots, 512), 0)
    return (lax.rem(row, slots) + col * slots) == 0, col < 2


def mix_forward_kernel(n, first_filter, col_ref, x_ref, kept_ref, recv_ref, cos, sin, out_ref):
    slots = n // 8
    special, near = masks(col_ref, slots)
    up_r, up_i, down_r, down_i = spectrum(x_ref, 0, slots, special, cos[...], sin[...])
    real, imag = filters(near, kept_ref, recv_ref, first_filter, slots)
    up = (real[0] * up_r - imag[0] * up_i, real[0] * up_i + imag[0] * up_r)
    down = (real[1] * down_r - imag[1] * down_i, real[1] * down_i + imag[1] * down_r)
    put_inverse(out_ref, slots, special, up, down, cos[...], sin[...])


def mix_back_kernel(
    n, first_filter, first_field, first_grad, col_ref, x_ref, g_ref, kept_ref, recv_ref,
    cos, sin, cos_back, sin_back, out_ref, grad_ref,
):
    slots = n // 8
    count = GROUPS * slots
    special, near = masks(col_ref, slots)
    field = spectrum(x_ref, first_field, slots, special, cos[...], sin[...])
    grad = spectrum(g_ref, first_grad, slots, special, cos[...], sin[...])
    real, imag = filters(near, kept_ref, recv_ref, first_filter, slots)
    sides, terms = [], []
    for side in range(2):
        g_r, g_i = grad[2 * side], grad[2 * side + 1]
        s_r, s_i = field[2 * side], field[2 * side + 1]
        sides.append((real[side] * g_r + imag[side] * g_i, real[side] * g_i - imag[side] * g_r))
        terms.append((g_r * s_r + g_i * s_i, g_i * s_r - g_r * s_i))
    put_inverse(out_ref, slots, special, sides[0], sides[1], cos_back[...], sin_back[...])
    for part in range(2):
        up, down = terms[0][part], terms[1][part]
        kept = jnp.where(near, up, down).astype(jnp.bfloat16)
        sent = jnp.where(near, down, up).astype(jnp.bfloat16)
        for q in range(COLS):
            lanes = slice(q * LANES, (q + 1) * LANES)
            grad_ref[q, part * count : (part + 1) * count, :] = kept[:, lanes]
            grad_ref[q, (2 + part) * count : (3 + part) * count, :] = sent[:, lanes]


def smem():
    return pl.BlockSpec(memory_space=pltpu.SMEM)


def vmem(count):
    return [pl.BlockSpec(memory_space=pltpu.VMEM)] * count


def mix_forward(n, col, entries, kept, recv, first_filter):
    rows = 2 * GROUPS * n // 8
    cos, sin = col_tables(n)
    return pl.pallas_call(
        functools.partial(mix_forward_kernel, n, first_filter),
        out_shape=jax.ShapeDtypeStruct((COLS, rows, LANES), jnp.bfloat16),
        in_specs=[smem()] + vmem(5),
        name="mix_forward_" + str(n),
        **params(8 * rows * 512 * 512, 4 << 20),
    )(col, entries, kept, recv, constant(cos), constant(sin))


def mix_back(n, col, entries, first_field, upstream, first_grad, kept, recv, first_filter):
    rows = 2 * GROUPS * n // 8
    cos, sin = col_tables(n)
    return pl.pallas_call(
        functools.partial(mix_back_kernel, n, first_filter, first_field, first_grad),
        out_shape=(
            jax.ShapeDtypeStruct((COLS, rows, LANES), jnp.bfloat16),
            jax.ShapeDtypeStruct((COLS, 2 * rows, LANES), jnp.bfloat16),
        ),
        in_specs=[smem()] + vmem(8),
        name="mix_back_" + str(n),
        **params(12 * rows * 512 * 512, 6 << 20),
    )(
        col, entries, upstream, kept, recv,
        constant(cos), constant(sin), constant(cos.T), constant(sin.T),
    )


def pair_lanes():
    matrix = np.zeros((2, COLS, 64, COLS, 2, 64))
    for p in range(2):
        for q in range(COLS):
            matrix[p, q, :, q, p, :] = np.eye(64)
    return matrix.reshape(512, 512)


def take_filters_kernel(first_ref, second_ref, pick_first, pick_second, lanes, kept_ref, sent_ref):
    at = 0
    for n, pick in ((H1, pick_first), (H2, pick_second)):
        slots = n // 8
        for part in range(2):
            for g in range(GROUPS):
                if n == H1:
                    rows = first_ref[part, g].astype(jnp.bfloat16)
                else:
                    pair = [second_ref[part, 2 * g + i].astype(jnp.bfloat16) for i in range(2)]
                    rows = dot(jnp.concatenate(pair, axis=1), lanes[...]).astype(jnp.bfloat16)
                rows = dot(pick[...], rows).astype(jnp.bfloat16)
                for q in range(COLS):
                    cut = slice(q * LANES, (q + 1) * LANES)
                    kept_ref[q, at : at + slots, :] = rows[:slots, cut]
                    sent_ref[q, at : at + slots, :] = rows[slots:, cut]
                at += slots


def slot_zero(block, first, slots):
    count = 2 * GROUPS * slots
    return block[first : first + count].reshape(2 * GROUPS, slots, LANES)[:, :1]


def put_slot_zero(block, zero, take, slots):
    shaped = block.reshape(2 * GROUPS, slots, LANES)
    here = (jnp.arange(slots) == 0)[None, :, None] & take
    return jnp.where(here, zero, shaped).reshape(2 * GROUPS * slots, LANES)


def take_filters(filter_first, filter_second, pick_first, pick_second):
    rows = 2 * GROUPS * (H1 + H2) // 8
    shape = jax.ShapeDtypeStruct((COLS, rows, LANES), jnp.bfloat16)
    kept, sent = pl.pallas_call(
        take_filters_kernel,
        out_shape=(shape, shape),
        name="take_filters",
        **params(12 * 128 * 128 * 512 * 2, 4 << 20),
    )(filter_first, filter_second, pick_first, pick_second, constant(pair_lanes()))
    quarter = lax.dynamic_index_in_dim(sent, lax.axis_index("rep"), 0, keepdims=False)
    split = 2 * GROUPS * H1 // 8
    zero = jnp.concatenate(
        [slot_zero(quarter, 0, H1 // 8), slot_zero(quarter, split, H2 // 8)], axis=1
    )
    return kept, quarter, zero


def swap_filters(quarter, zero):
    return lax.ppermute(quarter, "col", SWAP), lax.ppermute(zero, "col", ((2, 0), (3, 1)))


def patch_filters(recv, zero, col):
    split = 2 * GROUPS * H1 // 8
    near = col < 2
    recv = jnp.concatenate(
        [
            put_slot_zero(recv[:split], zero[:, :1], near, H1 // 8),
            put_slot_zero(recv[split:], zero[:, 1:], near, H2 // 8),
        ],
        axis=0,
    )
    return lax.all_gather(recv, "rep", axis=0, tiled=False)


def place_grads_kernel(
    kept_first, recv_first, kept_second, recv_second, pick_first, pick_second, lanes,
    first_ref, second_ref,
):
    for n, pick, kept, recv in (
        (H1, pick_first, kept_first, recv_first),
        (H2, pick_second, kept_second, recv_second),
    ):
        slots = n // 8
        for part in range(2):
            for g in range(GROUPS):
                at = (part * GROUPS + g) * slots
                both = jnp.concatenate([kept[at : at + slots], recv[at : at + slots]], axis=0)
                rows = dot(pick[...], both)
                if n == H1:
                    first_ref[part, g] = rows
                else:
                    rows = rows.astype(jnp.bfloat16)
                    for i in range(2):
                        second_ref[part, 2 * g + i] = dot(rows, lanes[i])


def summed(terms):
    return lax.psum_scatter(terms, "rep", scatter_dimension=0, tiled=False)


def swap_grads(total, n):
    count = 2 * GROUPS * n // 8
    sent = total[count:]
    zero = slot_zero(sent, 0, n // 8)
    return lax.ppermute(sent, "col", SWAP), lax.ppermute(zero, "col", ((0, 2), (1, 3)))


def place_grads(sum_first, swap_first, sum_second, swap_second, col, pick_first, pick_second):
    count_first, count_second = 2 * GROUPS * H1 // 8, 2 * GROUPS * H2 // 8
    far = col >= 2
    recv_first = put_slot_zero(*swap_first, far, H1 // 8)
    recv_second = put_slot_zero(*swap_second, far, H2 // 8)
    lanes = np.zeros((2, 128, 64))
    lanes[0, :64] = np.eye(64)
    lanes[1, 64:] = np.eye(64)
    return pl.pallas_call(
        place_grads_kernel,
        out_shape=(
            jax.ShapeDtypeStruct((2, GROUPS, H1 // 4, LANES), jnp.float32),
            jax.ShapeDtypeStruct((2, 2 * GROUPS, H2 // 4, LANES // 2), jnp.float32),
        ),
        name="place_grads",
        **params(12 * 128 * 128 * 128 * 2, 2 << 20),
    )(
        sum_first[:count_first], recv_first, sum_second[:count_second], recv_second,
        pick_first.T, pick_second.T, constant(lanes),
    )


def layer_normalize(entry_values, gains):
    center = entry_values - jnp.mean(entry_values, axis=1, keepdims=True)
    spread = jnp.mean(center * center, axis=1, keepdims=True)
    return center * lax.rsqrt(spread + epsilon) * gains[None, :, None, None]


def norm_pullback_step(entry_values, gains, upstream):
    _, pullback = jax.vjp(lambda inner_vals: layer_normalize(inner_vals, gains), entry_values)
    return pullback(upstream.astype(jnp.float32))[0]


def offset_table(cols_dev):
    half_cols = cols_dev // 2
    target = np.arange(2 * cols_dev)
    row_off = target // cols_dev
    rest = target % cols_dev
    source = row_off * cols_dev + 2 * (rest % half_cols) + rest // half_cols
    place = np.arange(2 * cols_dev)
    return constant(place[:, None] == source[None, :])


def strided_reduce(entry_values, weight_matrix):
    images_dev, channels, rows_dev, cols_dev = entry_values.shape
    outputs = weight_matrix.shape[0]
    merged = entry_values.reshape(images_dev, channels, rows_dev // 2, 2 * cols_dev)
    placed = jnp.einsum(
        "bcis,st->bcit", merged, offset_table(cols_dev), preferred_element_type=jnp.float32
    ).astype(jnp.bfloat16)
    placed = placed.reshape(images_dev, channels, rows_dev // 2, 4, cols_dev // 2)
    kernel = weight_matrix.reshape(outputs, 4, channels)
    return jnp.einsum("oqc,bciqj->boij", kernel, placed, preferred_element_type=jnp.float32).astype(
        jnp.bfloat16
    )


def upsample(upstream, weight_matrix):
    images_dev, outputs, rows_half, cols_half = upstream.shape
    channels = weight_matrix.shape[1] // 4
    kernel = weight_matrix.reshape(outputs, 4, channels)
    patches = jnp.einsum(
        "oqc,boij->bciqj", kernel, upstream, preferred_element_type=jnp.float32
    ).astype(jnp.bfloat16)
    patches = patches.reshape(images_dev, channels, rows_half, 8 * cols_half // 2)
    spread_back = jnp.einsum(
        "bcit,st->bcis", patches, offset_table(2 * cols_half), preferred_element_type=jnp.float32
    )
    return spread_back.reshape(images_dev, channels, 2 * rows_half, 2 * cols_half).astype(
        jnp.bfloat16
    )


def pack_first(field):
    return field.reshape(ROWS, GROUPS * 16, LANES)


def unpack_first(blocks):
    return blocks.reshape(1, 96, 16, LANES)


def pack_second(field):
    pairs = field.reshape(96, 2, 8, 64).transpose(0, 2, 1, 3)
    return pairs.reshape(ROWS, GROUPS * 8, LANES)


def unpack_second(blocks):
    return blocks.reshape(96, 8, 2, 64).transpose(0, 2, 1, 3).reshape(1, 192, 8, 64)


def exchange(blocks, axis):
    return lax.all_to_all(blocks, axis, split_axis=0, concat_axis=0, tiled=True)


def shards(images, gain_first, filter_first, reduce_weight, gain_second, filter_second, grad_out):
    col = lax.axis_index("col")
    col_word = col.astype(jnp.int32).reshape(1)
    picks = [
        jnp.where(col < 2, constant(np.eye(n // 4)), constant(mirror_matrix(n // 8)))
        for n in (H1, H2)
    ]
    kept, quarter, zero = take_filters(filter_first, filter_second, *picks)
    second_rows = 2 * GROUPS * H1 // 8

    pixels_wide = images.astype(jnp.float32)
    norm_one = layer_normalize(pixels_wide, gain_first).astype(jnp.bfloat16)
    both = jnp.concatenate([pack_first(norm_one), pack_second(grad_out)], axis=1)
    both, quarter, zero = lax.optimization_barrier((both, quarter, zero))
    swapped = swap_filters(quarter, zero)
    half = forward_rows(exchange(both, "row"), (H1, H2))
    half, swapped = lax.optimization_barrier((half, swapped))
    recv = patch_filters(*swapped, col)
    both = exchange(half, "col")
    mixed = exchange(mix_forward(H1, col_word, both, kept, recv, 0), "col")
    mixed_one = unpack_first(exchange(inverse_rows(mixed, H1), "row"))

    section_one = (pixels_wide + mixed_one.astype(jnp.float32)).astype(jnp.bfloat16)
    down_wide = strided_reduce(section_one, reduce_weight).astype(jnp.float32)
    norm_two = layer_normalize(down_wide, gain_second).astype(jnp.bfloat16)
    half_two = exchange(forward_rows(exchange(pack_second(norm_two), "row"), (H2,)), "col")
    dspec_two, terms_two = mix_back(
        H2, col_word, half_two, 0, both, second_rows, kept, recv, second_rows
    )
    sum_two = summed(terms_two)
    rot_two = exchange(dspec_two, "col")
    back_two = inverse_rows(rot_two, H2)
    grad_norm_two = unpack_second(exchange(back_two, "row"))

    grad_down = (
        grad_out.astype(jnp.float32) + norm_pullback_step(down_wide, gain_second, grad_norm_two)
    ).astype(jnp.bfloat16)
    grad_section = upsample(grad_down, reduce_weight)
    packed = pack_first(grad_section)
    packed, sum_two = lax.optimization_barrier((packed, sum_two))
    swap_two = swap_grads(sum_two, H2)
    half_grad = forward_rows(exchange(packed, "row"), (H1,))
    half_grad, swap_two = lax.optimization_barrier((half_grad, swap_two))
    half_grad = exchange(half_grad, "col")
    dspec_one, terms_one = mix_back(H1, col_word, both, 0, half_grad, 0, kept, recv, 0)
    sum_one = summed(terms_one)
    rot_one = exchange(dspec_one, "col")
    rot_one, sum_one = lax.optimization_barrier((rot_one, sum_one))
    swap_one = swap_grads(sum_one, H1)
    back_one = inverse_rows(rot_one, H1)
    grad_norm_one = unpack_first(exchange(back_one, "row"))
    grad_images = (
        grad_section.astype(jnp.float32)
        + norm_pullback_step(pixels_wide, gain_first, grad_norm_one)
    ).astype(jnp.bfloat16)
    grad_first, grad_second = place_grads(
        sum_one, swap_one, sum_two, swap_two, col, *picks
    )
    return (grad_images, grad_first, grad_second)


def solution(mesh):
    placed = (
        P("rep", None, "row", "col"),
        P(),
        P(None, "row", "col", None),
        P(),
        P(),
        P(None, "row", "col", None),
        P("rep", None, "row", "col"),
    )
    return jax.shard_map(
        shards,
        mesh=mesh,
        in_specs=placed,
        out_specs=(
            P("rep", None, "row", "col"),
            P(None, "row", "col", "rep"),
            P(None, "row", "col", "rep"),
        ),
        check_vma=False,
    )
```

```python
import functools
import math

import jax
import jax.numpy as jnp
import numpy as np
from jax import lax
from jax.experimental import pallas as pl
from jax.experimental.pallas import tpu as pltpu
from jax.sharding import PartitionSpec as P

H1 = 512
H2 = 256
GROUPS = 3
COLS = 4
ROWS = 32
LANES = 128

epsilon = 1e-06

ORDER = (0, 2, 3, 1)
SWAP = ((0, 3), (3, 0), (1, 2), (2, 1))


def cos_sin(n):
    index = np.arange(n)
    angles = (index[:, None] * index[None, :] % n) * (2.0 * math.pi / n)
    factor = 1.0 / math.sqrt(n)
    return np.cos(angles) * factor, np.sin(angles) * factor


def row_table(n):
    cos, sin = cos_sin(n)
    slots = n // 8
    parts = []
    for c in range(COLS):
        k = ORDER[c] * slots + np.arange(slots)
        real, imag = cos[k], -sin[k]
        if c == 0:
            imag[0] = cos[n // 2]
        parts += [real, imag]
    return np.concatenate(parts, axis=0)


def col_tables(n):
    cos, sin = cos_sin(n)
    pair = 512 // n
    width = LANES // pair
    if pair == 1:
        return cos, sin
    out = []
    for table in (cos, sin):
        blocks = table.reshape(COLS, width, COLS, width)
        full = np.zeros((COLS, pair, width, COLS, pair, width))
        for p in range(pair):
            full[:, p, :, :, p, :] = blocks
        out.append(full.reshape(512, 512))
    return tuple(out)


def mirror_matrix(slots):
    matrix = np.zeros((2 * slots, 2 * slots))
    for s in range(slots):
        matrix[s, slots - s] = 1.0
        matrix[slots + s, (2 * slots - s) % (2 * slots)] = 1.0
    return matrix


def constant(values):
    return jnp.asarray(np.asarray(values, np.float32).astype(jnp.bfloat16))


def dot(a, b):
    return jnp.dot(a, b, preferred_element_type=jnp.float32)


def params(flops, traffic):
    return dict(
        compiler_params=pltpu.CompilerParams(vmem_limit_bytes=40 * 1024 * 1024),
        cost_estimate=pl.CostEstimate(flops=flops, bytes_accessed=traffic, transcendentals=0),
    )


def gather_rows(block, rows):
    parts = []
    for g in range(GROUPS):
        part = block[:, g * rows : (g + 1) * rows, :]
        if rows % 16:
            part = part.astype(jnp.float32)
        parts.append(part.reshape(ROWS * rows, LANES).astype(jnp.bfloat16))
    return jnp.concatenate(parts, axis=1)


def forward_rows_kernel(layout, *refs):
    x_ref, tables, out_ref = refs[0], refs[1:-1], refs[-1]
    for (n, first_in, first_out), table in zip(layout, tables):
        rows = n // ROWS
        slots = n // 8
        block = x_ref[:, first_in : first_in + GROUPS * rows, :]
        half = dot(table[...], gather_rows(block, rows)).astype(jnp.bfloat16)
        half = half.reshape(COLS, 2, slots, GROUPS * LANES)
        for part in range(2):
            for g in range(GROUPS):
                at = first_out + (part * GROUPS + g) * slots
                out_ref[:, at : at + slots, :] = half[:, part, :, g * LANES : (g + 1) * LANES]


def forward_rows(entries, sizes):
    layout, first_in, first_out = [], 0, 0
    for n in sizes:
        layout.append((n, first_in, first_out))
        first_in += GROUPS * n // ROWS
        first_out += 2 * GROUPS * n // 8
    flops = sum(2 * n * n * GROUPS * LANES for n in sizes)
    return pl.pallas_call(
        functools.partial(forward_rows_kernel, tuple(layout)),
        out_shape=jax.ShapeDtypeStruct((COLS, first_out, LANES), jnp.bfloat16),
        name="forward_rows_" + "_".join(str(n) for n in sizes),
        **params(flops, 2 << 20),
    )(entries, *[constant(row_table(n)) for n in sizes])


def inverse_rows_kernel(n, x_ref, table, out_ref):
    rows = n // ROWS
    slots = n // 8
    parts = []
    for g in range(GROUPS):
        both = [
            x_ref[:, (part * GROUPS + g) * slots : (part * GROUPS + g + 1) * slots, :].reshape(
                COLS, 1, slots, LANES
            )
            for part in range(2)
        ]
        parts.append(jnp.concatenate(both, axis=1).reshape(n, LANES))
    result = dot(table[...], jnp.concatenate(parts, axis=1))
    pieces = [
        result[:, g * LANES : (g + 1) * LANES].reshape(ROWS, rows, LANES) for g in range(GROUPS)
    ]
    out_ref[...] = jnp.concatenate(pieces, axis=1).astype(jnp.bfloat16)


def inverse_rows(entries, n):
    return pl.pallas_call(
        functools.partial(inverse_rows_kernel, n),
        out_shape=jax.ShapeDtypeStruct((ROWS, GROUPS * n // ROWS, LANES), jnp.bfloat16),
        name="inverse_rows_" + str(n),
        **params(2 * n * n * GROUPS * LANES, 2 << 20),
    )(entries, constant(row_table(n).T))


def wide(ref, first, count):
    return jnp.concatenate([ref[q, first : first + count, :] for q in range(COLS)], axis=1)


def spectrum(ref, first, slots, special, cos, sin):
    count = GROUPS * slots
    real, imag = wide(ref, first, count), wide(ref, first + count, count)
    real_cos, real_sin = dot(real, cos), dot(real, sin)
    imag_cos, imag_sin = dot(imag, cos), dot(imag, sin)
    return (
        jnp.where(special, real_cos, real_cos + imag_sin),
        jnp.where(special, -real_sin, imag_cos - real_sin),
        jnp.where(special, imag_cos, real_cos - imag_sin),
        jnp.where(special, -imag_sin, -imag_cos - real_sin),
    )


def filters(near, kept_ref, recv_ref, first, slots):
    count = GROUPS * slots
    out = []
    for part in range(2):
        kept = wide(kept_ref, first + part * count, count).astype(jnp.float32)
        recv = wide(recv_ref, first + part * count, count).astype(jnp.float32)
        out.append((jnp.where(near, kept, recv), jnp.where(near, recv, kept)))
    return out


def put_inverse(out_ref, slots, special, up, down, cos, sin):
    count = GROUPS * slots
    (up_r, up_i), (down_r, down_i) = up, down
    bf16 = jnp.bfloat16
    sum_r = jnp.where(special, up_r, up_r + down_r).astype(bf16)
    sum_i = jnp.where(special, up_i, up_i + down_i).astype(bf16)
    dif_i = jnp.where(special, down_r, up_i - down_i).astype(bf16)
    dif_r = jnp.where(special, -down_i, up_r - down_r).astype(bf16)
    rot_real = (dot(sum_r, cos) - dot(sum_i, sin)).astype(bf16)
    rot_imag = (dot(dif_i, cos) + dot(dif_r, sin)).astype(bf16)
    for q in range(COLS):
        out_ref[q, :count, :] = rot_real[:, q * LANES : (q + 1) * LANES]
        out_ref[q, count:, :] = rot_imag[:, q * LANES : (q + 1) * LANES]


def masks(col_ref, slots):
    col = col_ref[0]
    row = lax.broadcasted_iota(jnp.int32, (GROUPS * slots, 512), 0)
    return (lax.rem(row, slots) + col * slots) == 0, col < 2


def mix_forward_kernel(n, first_filter, col_ref, x_ref, kept_ref, recv_ref, cos, sin, out_ref):
    slots = n // 8
    special, near = masks(col_ref, slots)
    up_r, up_i, down_r, down_i = spectrum(x_ref, 0, slots, special, cos[...], sin[...])
    real, imag = filters(near, kept_ref, recv_ref, first_filter, slots)
    up = (real[0] * up_r - imag[0] * up_i, real[0] * up_i + imag[0] * up_r)
    down = (real[1] * down_r - imag[1] * down_i, real[1] * down_i + imag[1] * down_r)
    put_inverse(out_ref, slots, special, up, down, cos[...], sin[...])


def mix_back_kernel(
    n, first_filter, first_field, first_grad, col_ref, x_ref, g_ref, kept_ref, recv_ref,
    cos, sin, cos_back, sin_back, out_ref, grad_ref,
):
    slots = n // 8
    count = GROUPS * slots
    special, near = masks(col_ref, slots)
    field = spectrum(x_ref, first_field, slots, special, cos[...], sin[...])
    grad = spectrum(g_ref, first_grad, slots, special, cos[...], sin[...])
    real, imag = filters(near, kept_ref, recv_ref, first_filter, slots)
    sides, terms = [], []
    for side in range(2):
        g_r, g_i = grad[2 * side], grad[2 * side + 1]
        s_r, s_i = field[2 * side], field[2 * side + 1]
        sides.append((real[side] * g_r + imag[side] * g_i, real[side] * g_i - imag[side] * g_r))
        terms.append((g_r * s_r + g_i * s_i, g_i * s_r - g_r * s_i))
    put_inverse(out_ref, slots, special, sides[0], sides[1], cos_back[...], sin_back[...])
    for part in range(2):
        up, down = terms[0][part], terms[1][part]
        kept = jnp.where(near, up, down).astype(jnp.bfloat16)
        sent = jnp.where(near, down, up).astype(jnp.bfloat16)
        for q in range(COLS):
            lanes = slice(q * LANES, (q + 1) * LANES)
            grad_ref[q, part * count : (part + 1) * count, :] = kept[:, lanes]
            grad_ref[q, (2 + part) * count : (3 + part) * count, :] = sent[:, lanes]


def smem():
    return pl.BlockSpec(memory_space=pltpu.SMEM)


def vmem(count):
    return [pl.BlockSpec(memory_space=pltpu.VMEM)] * count


def mix_forward(n, col, entries, kept, recv, first_filter):
    rows = 2 * GROUPS * n // 8
    cos, sin = col_tables(n)
    return pl.pallas_call(
        functools.partial(mix_forward_kernel, n, first_filter),
        out_shape=jax.ShapeDtypeStruct((COLS, rows, LANES), jnp.bfloat16),
        in_specs=[smem()] + vmem(5),
        name="mix_forward_" + str(n),
        **params(8 * rows * 512 * 512, 4 << 20),
    )(col, entries, kept, recv, constant(cos), constant(sin))


def mix_back(n, col, entries, first_field, upstream, first_grad, kept, recv, first_filter):
    rows = 2 * GROUPS * n // 8
    cos, sin = col_tables(n)
    return pl.pallas_call(
        functools.partial(mix_back_kernel, n, first_filter, first_field, first_grad),
        out_shape=(
            jax.ShapeDtypeStruct((COLS, rows, LANES), jnp.bfloat16),
            jax.ShapeDtypeStruct((COLS, 2 * rows, LANES), jnp.bfloat16),
        ),
        in_specs=[smem()] + vmem(8),
        name="mix_back_" + str(n),
        **params(12 * rows * 512 * 512, 6 << 20),
    )(
        col, entries, upstream, kept, recv,
        constant(cos), constant(sin), constant(cos.T), constant(sin.T),
    )


def pair_lanes():
    matrix = np.zeros((2, COLS, 64, COLS, 2, 64))
    for p in range(2):
        for q in range(COLS):
            matrix[p, q, :, q, p, :] = np.eye(64)
    return matrix.reshape(512, 512)


def take_filters_kernel(first_ref, second_ref, pick_first, pick_second, lanes, kept_ref, sent_ref):
    at = 0
    for n, pick in ((H1, pick_first), (H2, pick_second)):
        slots = n // 8
        for part in range(2):
            for g in range(GROUPS):
                if n == H1:
                    rows = first_ref[part, g].astype(jnp.bfloat16)
                else:
                    pair = [second_ref[part, 2 * g + i].astype(jnp.bfloat16) for i in range(2)]
                    rows = dot(jnp.concatenate(pair, axis=1), lanes[...]).astype(jnp.bfloat16)
                rows = dot(pick[...], rows).astype(jnp.bfloat16)
                for q in range(COLS):
                    cut = slice(q * LANES, (q + 1) * LANES)
                    kept_ref[q, at : at + slots, :] = rows[:slots, cut]
                    sent_ref[q, at : at + slots, :] = rows[slots:, cut]
                at += slots


def slot_zero(block, first, slots):
    count = 2 * GROUPS * slots
    return block[first : first + count].reshape(2 * GROUPS, slots, LANES)[:, :1]


def put_slot_zero(block, zero, take, slots):
    shaped = block.reshape(2 * GROUPS, slots, LANES)
    here = (jnp.arange(slots) == 0)[None, :, None] & take
    return jnp.where(here, zero, shaped).reshape(2 * GROUPS * slots, LANES)


def take_filters(filter_first, filter_second, pick_first, pick_second):
    rows = 2 * GROUPS * (H1 + H2) // 8
    shape = jax.ShapeDtypeStruct((COLS, rows, LANES), jnp.bfloat16)
    kept, sent = pl.pallas_call(
        take_filters_kernel,
        out_shape=(shape, shape),
        name="take_filters",
        **params(12 * 128 * 128 * 512 * 2, 4 << 20),
    )(filter_first, filter_second, pick_first, pick_second, constant(pair_lanes()))
    quarter = lax.dynamic_index_in_dim(sent, lax.axis_index("rep"), 0, keepdims=False)
    split = 2 * GROUPS * H1 // 8
    zero = jnp.concatenate(
        [slot_zero(quarter, 0, H1 // 8), slot_zero(quarter, split, H2 // 8)], axis=1
    )
    return kept, quarter, zero


def swap_filters(quarter, zero):
    return lax.ppermute(quarter, "col", SWAP), lax.ppermute(zero, "col", ((2, 0), (3, 1)))


def patch_filters(recv, zero, col):
    split = 2 * GROUPS * H1 // 8
    near = col < 2
    recv = jnp.concatenate(
        [
            put_slot_zero(recv[:split], zero[:, :1], near, H1 // 8),
            put_slot_zero(recv[split:], zero[:, 1:], near, H2 // 8),
        ],
        axis=0,
    )
    return lax.all_gather(recv, "rep", axis=0, tiled=False)


def place_grads_kernel(
    kept_first, recv_first, kept_second, recv_second, pick_first, pick_second, lanes,
    first_ref, second_ref,
):
    for n, pick, kept, recv in (
        (H1, pick_first, kept_first, recv_first),
        (H2, pick_second, kept_second, recv_second),
    ):
        slots = n // 8
        for part in range(2):
            for g in range(GROUPS):
                at = (part * GROUPS + g) * slots
                both = jnp.concatenate([kept[at : at + slots], recv[at : at + slots]], axis=0)
                rows = dot(pick[...], both)
                if n == H1:
                    first_ref[part, g] = rows
                else:
                    rows = rows.astype(jnp.bfloat16)
                    for i in range(2):
                        second_ref[part, 2 * g + i] = dot(rows, lanes[i])


def summed(terms):
    return lax.psum_scatter(terms, "rep", scatter_dimension=0, tiled=False)


def swap_grads(total, n):
    count = 2 * GROUPS * n // 8
    sent = total[count:]
    zero = slot_zero(sent, 0, n // 8)
    return lax.ppermute(sent, "col", SWAP), lax.ppermute(zero, "col", ((0, 2), (1, 3)))


def place_grads(sum_first, swap_first, sum_second, swap_second, col, pick_first, pick_second):
    count_first, count_second = 2 * GROUPS * H1 // 8, 2 * GROUPS * H2 // 8
    far = col >= 2
    recv_first = put_slot_zero(*swap_first, far, H1 // 8)
    recv_second = put_slot_zero(*swap_second, far, H2 // 8)
    lanes = np.zeros((2, 128, 64))
    lanes[0, :64] = np.eye(64)
    lanes[1, 64:] = np.eye(64)
    return pl.pallas_call(
        place_grads_kernel,
        out_shape=(
            jax.ShapeDtypeStruct((2, GROUPS, H1 // 4, LANES), jnp.float32),
            jax.ShapeDtypeStruct((2, 2 * GROUPS, H2 // 4, LANES // 2), jnp.float32),
        ),
        name="place_grads",
        **params(12 * 128 * 128 * 128 * 2, 2 << 20),
    )(
        sum_first[:count_first], recv_first, sum_second[:count_second], recv_second,
        pick_first.T, pick_second.T, constant(lanes),
    )


def layer_normalize(entry_values, gains):
    center = entry_values - jnp.mean(entry_values, axis=1, keepdims=True)
    spread = jnp.mean(center * center, axis=1, keepdims=True)
    return center * lax.rsqrt(spread + epsilon) * gains[None, :, None, None]


def norm_pullback_step(entry_values, gains, upstream):
    _, pullback = jax.vjp(lambda inner_vals: layer_normalize(inner_vals, gains), entry_values)
    return pullback(upstream.astype(jnp.float32))[0]


def fold(values):
    total = jnp.broadcast_to(jnp.sum(values, axis=0, keepdims=True), (8, LANES))
    return (total + pltpu.roll(total, LANES // 2, 1))[:1]


def standardize(values):
    center = values - fold(values) / 192.0
    scale = lax.rsqrt(fold(center * center) / 192.0 + epsilon)
    return center * scale, scale


def first_norm_kernel(x_ref, g_ref, gain_ref, pair_ref, out_ref, grad_ref):
    pixels = x_ref[...].astype(jnp.float32)
    center = pixels - jnp.sum(pixels, axis=0, keepdims=True) / 96.0
    scale = lax.rsqrt(jnp.sum(center * center, axis=0) / 96.0 + epsilon)
    for c in range(96):
        at = (c % GROUPS) * 16
        out_ref[c // GROUPS, at : at + 16, :] = (center[c] * scale * gain_ref[c]).astype(
            jnp.bfloat16
        )
    upstream = g_ref[...].astype(jnp.float32).reshape(96, 2, 8, 64)
    packed = sum(
        dot(upstream[:, i].reshape(768, 64).astype(jnp.bfloat16), pair_ref[i]) for i in range(2)
    )
    packed = packed.reshape(ROWS, GROUPS * 8, LANES).astype(jnp.bfloat16)
    out_ref[:, GROUPS * 16 :, :] = packed
    grad_ref[...] = packed


def first_norm(images, grad_out, gains):
    pair = np.zeros((2, 64, 128))
    pair[0, :, :64] = np.eye(64)
    pair[1, :, 64:] = np.eye(64)
    return pl.pallas_call(
        first_norm_kernel,
        out_shape=(
            jax.ShapeDtypeStruct((ROWS, GROUPS * 24, LANES), jnp.bfloat16),
            jax.ShapeDtypeStruct((ROWS, GROUPS * 8, LANES), jnp.bfloat16),
        ),
        in_specs=vmem(2) + [smem()] + vmem(1),
        name="first_norm",
        **params(4 * 768 * 64 * 128, 2 << 20),
    )(images.reshape(96, 16, LANES), grad_out.reshape(192, 8, 64), gains, constant(pair))


def spread_columns():
    matrix = np.zeros((64, 2, 2, 2, 64))
    for e in range(2):
        for half in range(2):
            matrix[:, e, e, half, :] = np.eye(64)
    return matrix.reshape(128, 256)


def merge_columns():
    matrix = np.zeros((2, 2, 64, 2, 64, 2))
    for e in range(2):
        for i in range(2):
            matrix[e, i, :, i, :, e] = np.eye(64)
    return matrix.reshape(256, 256)


def low_half():
    return lax.broadcasted_iota(jnp.int32, (96, LANES), 1) < LANES // 2


def reduce_kernel(x_ref, m_ref, w_ref, gain_ref, spread_ref, norm_ref, down_ref, s_ref, n_ref):
    mixed = m_ref[...].astype(jnp.float32).reshape(1536, LANES)
    section = x_ref[...].astype(jnp.float32).reshape(1536, LANES) + mixed
    spread = dot(section.astype(jnp.bfloat16), spread_ref[...])
    for e in range(2):
        s_ref[e] = spread[:, e * LANES : (e + 1) * LANES]
    low = low_half()
    for first in range(0, 8, 2):
        patches = [
            jnp.concatenate(
                [
                    s_ref[e, pl.ds(2 * i + a, 96, stride=16), :].astype(jnp.bfloat16)
                    for a in range(2)
                    for e in range(2)
                ],
                axis=0,
            )
            for i in (first, first + 1)
        ]
        both = dot(w_ref[...], jnp.concatenate(patches, axis=1))
        for i in range(2):
            block = both[:, i * LANES : (i + 1) * LANES]
            down = jnp.where(low, block[:96], block[96:]).astype(jnp.bfloat16)
            down_ref[first + i] = down
            normed, _ = standardize(down.astype(jnp.float32))
            n_ref[pl.ds(first + i, 96, stride=8), :] = normed * gain_ref[...]
    norm_ref[...] = n_ref[...].reshape(ROWS, GROUPS * 8, LANES).astype(jnp.bfloat16)


def reduce_step(images, mixed, weight, gains):
    return pl.pallas_call(
        reduce_kernel,
        out_shape=(
            jax.ShapeDtypeStruct((ROWS, GROUPS * 8, LANES), jnp.bfloat16),
            jax.ShapeDtypeStruct((8, 96, LANES), jnp.bfloat16),
        ),
        in_specs=vmem(5),
        scratch_shapes=[
            pltpu.VMEM((2, 1536, LANES), jnp.float32),
            pltpu.VMEM((768, LANES), jnp.float32),
        ],
        name="reduce_step",
        **params(4 * 2 * 192 * 384 * 256, 2 << 20),
    )(images.reshape(96, 16, LANES), mixed, weight, gains, constant(spread_columns()))


def expand_kernel(
    b_ref, down_ref, g_ref, w_ref, gain_ref, merge_ref, out_ref, back_ref, grad_ref, o_ref
):
    back_ref[...] = b_ref[...].astype(jnp.float32).reshape(768, LANES)
    grad_ref[...] = g_ref[...].astype(jnp.float32).reshape(768, LANES)
    low = low_half()
    for first in range(0, 8, 2):
        grads = []
        for i in (first, first + 1):
            normed, scale = standardize(down_ref[i].astype(jnp.float32))
            upstream = back_ref[pl.ds(i, 96, stride=8), :] * gain_ref[...]
            step = upstream - fold(upstream) / 192.0 - normed * (fold(upstream * normed) / 192.0)
            total = grad_ref[pl.ds(i, 96, stride=8), :] + scale * step
            total = total.astype(jnp.bfloat16).astype(jnp.float32)
            grads.append((total, pltpu.roll(total, LANES // 2, 1)))
        even = jnp.where(low, grads[0][0], grads[1][1])
        odd = jnp.where(low, grads[0][1], grads[1][0])
        both = jnp.concatenate([even, odd], axis=0).astype(jnp.bfloat16)
        patches = dot(w_ref[...], both).astype(jnp.bfloat16)
        rows = [
            jnp.concatenate(
                [patches[(2 * a + e) * 96 : (2 * a + e + 1) * 96] for e in range(2)], axis=1
            )
            for a in range(2)
        ]
        merged = dot(jnp.concatenate(rows, axis=0), merge_ref[...])
        for i in range(2):
            for a in range(2):
                o_ref[pl.ds(2 * (first + i) + a, 96, stride=16), :] = merged[
                    a * 96 : (a + 1) * 96, i * LANES : (i + 1) * LANES
                ]
    out_ref[...] = o_ref[...].reshape(ROWS, GROUPS * 16, LANES).astype(jnp.bfloat16)


def expand_step(back, down, upstream, weight, gains):
    return pl.pallas_call(
        expand_kernel,
        out_shape=jax.ShapeDtypeStruct((ROWS, GROUPS * 16, LANES), jnp.bfloat16),
        in_specs=vmem(6),
        scratch_shapes=[
            pltpu.VMEM((768, LANES), jnp.float32),
            pltpu.VMEM((768, LANES), jnp.float32),
            pltpu.VMEM((1536, LANES), jnp.float32),
        ],
        name="expand_step",
        **params(4 * 2 * 192 * 384 * 256, 2 << 20),
    )(back, down, upstream, weight, gains, constant(merge_columns()))


def unpack_first(blocks):
    return blocks.reshape(1, 96, 16, LANES)


def pack_second(field):
    pairs = field.reshape(96, 2, 8, 64).transpose(0, 2, 1, 3)
    return pairs.reshape(ROWS, GROUPS * 8, LANES)


def exchange(blocks, axis):
    return lax.all_to_all(blocks, axis, split_axis=0, concat_axis=0, tiled=True)


def shards(images, gain_first, filter_first, reduce_weight, gain_second, filter_second, grad_out):
    col = lax.axis_index("col")
    col_word = col.astype(jnp.int32).reshape(1)
    picks = [
        jnp.where(col < 2, constant(np.eye(n // 4)), constant(mirror_matrix(n // 8)))
        for n in (H1, H2)
    ]
    kept, quarter, zero = take_filters(filter_first, filter_second, *picks)
    second_rows = 2 * GROUPS * H1 // 8

    weight = reduce_weight.reshape(96, 2, 384).transpose(1, 0, 2).reshape(192, 384)
    gains = jnp.repeat(gain_second.reshape(96, 2), 64, axis=1)

    both, packed_out = first_norm(images, grad_out, gain_first)
    swapped = swap_filters(quarter, zero)
    half = forward_rows(exchange(both, "row"), (H1, H2))
    half, swapped = lax.optimization_barrier((half, swapped))
    recv = patch_filters(*swapped, col)
    both = exchange(half, "col")
    mixed = exchange(mix_forward(H1, col_word, both, kept, recv, 0), "col")
    mixed_one = exchange(inverse_rows(mixed, H1), "row")

    norm_two, down = reduce_step(images, mixed_one, weight, gains)
    half_two = exchange(forward_rows(exchange(norm_two, "row"), (H2,)), "col")
    dspec_two, terms_two = mix_back(
        H2, col_word, half_two, 0, both, second_rows, kept, recv, second_rows
    )
    sum_two = summed(terms_two)
    rot_two = exchange(dspec_two, "col")
    rot_two, sum_two = lax.optimization_barrier((rot_two, sum_two))
    swap_two = swap_grads(sum_two, H2)
    back_two = exchange(inverse_rows(rot_two, H2), "row")
    back_two, swap_two = lax.optimization_barrier((back_two, swap_two))

    grad_section = expand_step(back_two, down, packed_out, weight.T, gains)
    half_grad = exchange(forward_rows(exchange(grad_section, "row"), (H1,)), "col")
    dspec_one, terms_one = mix_back(H1, col_word, both, 0, half_grad, 0, kept, recv, 0)
    sum_one = summed(terms_one)
    rot_one = exchange(dspec_one, "col")
    rot_one, sum_one = lax.optimization_barrier((rot_one, sum_one))
    swap_one = swap_grads(sum_one, H1)
    grad_norm_one = unpack_first(exchange(inverse_rows(rot_one, H1), "row"))
    grad_images = (
        unpack_first(grad_section).astype(jnp.float32)
        + norm_pullback_step(images.astype(jnp.float32), gain_first, grad_norm_one)
    ).astype(jnp.bfloat16)
    grad_first, grad_second = place_grads(
        sum_one, swap_one, sum_two, swap_two, col, *picks
    )
    return (grad_images, grad_first, grad_second)


def solution(mesh):
    placed = (
        P("rep", None, "row", "col"),
        P(),
        P(None, "row", "col", None),
        P(),
        P(),
        P(None, "row", "col", None),
        P("rep", None, "row", "col"),
    )
    return jax.shard_map(
        shards,
        mesh=mesh,
        in_specs=placed,
        out_specs=(
            P("rep", None, "row", "col"),
            P(None, "row", "col", "rep"),
            P(None, "row", "col", "rep"),
        ),
        check_vma=False,
    )
```

```python
import functools
import math

import jax
import jax.numpy as jnp
import numpy as np
from jax import lax
from jax.experimental import pallas as pl
from jax.experimental.pallas import tpu as pltpu
from jax.sharding import PartitionSpec as P

H1 = 512
H2 = 256
GROUPS = 3
COLS = 4
ROWS = 32
LANES = 128

epsilon = 1e-06

ORDER = (0, 2, 3, 1)
SWAP = ((0, 3), (3, 0), (1, 2), (2, 1))


def cos_sin(n):
    index = np.arange(n)
    angles = (index[:, None] * index[None, :] % n) * (2.0 * math.pi / n)
    factor = 1.0 / math.sqrt(n)
    return np.cos(angles) * factor, np.sin(angles) * factor


def row_table(n):
    cos, sin = cos_sin(n)
    slots = n // 8
    parts = []
    for c in range(COLS):
        k = ORDER[c] * slots + np.arange(slots)
        real, imag = cos[k], -sin[k]
        if c == 0:
            imag[0] = cos[n // 2]
        parts += [real, imag]
    return np.concatenate(parts, axis=0)


def col_tables(n):
    cos, sin = cos_sin(n)
    pair = 512 // n
    width = LANES // pair
    if pair == 1:
        return cos, sin
    out = []
    for table in (cos, sin):
        blocks = table.reshape(COLS, width, COLS, width)
        full = np.zeros((COLS, pair, width, COLS, pair, width))
        for p in range(pair):
            full[:, p, :, :, p, :] = blocks
        out.append(full.reshape(512, 512))
    return tuple(out)


def constant(values):
    return jnp.asarray(np.asarray(values, np.float32).astype(jnp.bfloat16))


def dot(a, b):
    return jnp.dot(a, b, preferred_element_type=jnp.float32)


def params(flops, traffic):
    return dict(
        compiler_params=pltpu.CompilerParams(vmem_limit_bytes=40 * 1024 * 1024),
        cost_estimate=pl.CostEstimate(flops=flops, bytes_accessed=traffic, transcendentals=0),
    )


def gather_rows(block, rows):
    parts = []
    for g in range(GROUPS):
        part = block[:, g * rows : (g + 1) * rows, :]
        if rows % 16:
            part = part.astype(jnp.float32)
        parts.append(part.reshape(ROWS * rows, LANES).astype(jnp.bfloat16))
    return jnp.concatenate(parts, axis=1)


def forward_rows_kernel(layout, *refs):
    x_ref, tables, out_ref = refs[0], refs[1:-1], refs[-1]
    for (n, first_in, first_out), table in zip(layout, tables):
        rows = n // ROWS
        slots = n // 8
        block = x_ref[:, first_in : first_in + GROUPS * rows, :]
        half = dot(table[...], gather_rows(block, rows)).astype(jnp.bfloat16)
        half = half.reshape(COLS, 2, slots, GROUPS * LANES)
        for part in range(2):
            for g in range(GROUPS):
                at = first_out + (part * GROUPS + g) * slots
                out_ref[:, at : at + slots, :] = half[:, part, :, g * LANES : (g + 1) * LANES]


def forward_rows(entries, sizes):
    layout, first_in, first_out = [], 0, 0
    for n in sizes:
        layout.append((n, first_in, first_out))
        first_in += GROUPS * n // ROWS
        first_out += 2 * GROUPS * n // 8
    flops = sum(2 * n * n * GROUPS * LANES for n in sizes)
    return pl.pallas_call(
        functools.partial(forward_rows_kernel, tuple(layout)),
        out_shape=jax.ShapeDtypeStruct((COLS, first_out, LANES), jnp.bfloat16),
        name="forward_rows_" + "_".join(str(n) for n in sizes),
        **params(flops, 2 << 20),
    )(entries, *[constant(row_table(n)) for n in sizes])


def inverse_rows_kernel(n, x_ref, table, out_ref):
    rows = n // ROWS
    slots = n // 8
    parts = []
    for g in range(GROUPS):
        both = [
            x_ref[:, (part * GROUPS + g) * slots : (part * GROUPS + g + 1) * slots, :].reshape(
                COLS, 1, slots, LANES
            )
            for part in range(2)
        ]
        parts.append(jnp.concatenate(both, axis=1).reshape(n, LANES))
    result = dot(table[...], jnp.concatenate(parts, axis=1))
    pieces = [
        result[:, g * LANES : (g + 1) * LANES].reshape(ROWS, rows, LANES) for g in range(GROUPS)
    ]
    out_ref[...] = jnp.concatenate(pieces, axis=1).astype(jnp.bfloat16)


def inverse_rows(entries, n):
    return pl.pallas_call(
        functools.partial(inverse_rows_kernel, n),
        out_shape=jax.ShapeDtypeStruct((ROWS, GROUPS * n // ROWS, LANES), jnp.bfloat16),
        name="inverse_rows_" + str(n),
        **params(2 * n * n * GROUPS * LANES, 2 << 20),
    )(entries, constant(row_table(n).T))


def wide(ref, first, count):
    return jnp.concatenate([ref[q, first : first + count, :] for q in range(COLS)], axis=1)


def spectrum(ref, first, slots, special, cos, sin):
    count = GROUPS * slots
    real, imag = wide(ref, first, count), wide(ref, first + count, count)
    real_cos, real_sin = dot(real, cos), dot(real, sin)
    imag_cos, imag_sin = dot(imag, cos), dot(imag, sin)
    return (
        jnp.where(special, real_cos, real_cos + imag_sin),
        jnp.where(special, -real_sin, imag_cos - real_sin),
        jnp.where(special, imag_cos, real_cos - imag_sin),
        jnp.where(special, -imag_sin, -imag_cos - real_sin),
    )


def filters(near, kept_ref, recv_ref, first, slots):
    count = GROUPS * slots
    out = []
    for part in range(2):
        kept = wide(kept_ref, first + part * count, count).astype(jnp.float32)
        recv = wide(recv_ref, first + part * count, count).astype(jnp.float32)
        out.append((jnp.where(near, kept, recv), jnp.where(near, recv, kept)))
    return out


def put_inverse(out_ref, slots, special, up, down, cos, sin):
    count = GROUPS * slots
    (up_r, up_i), (down_r, down_i) = up, down
    bf16 = jnp.bfloat16
    sum_r = jnp.where(special, up_r, up_r + down_r).astype(bf16)
    sum_i = jnp.where(special, up_i, up_i + down_i).astype(bf16)
    dif_i = jnp.where(special, down_r, up_i - down_i).astype(bf16)
    dif_r = jnp.where(special, -down_i, up_r - down_r).astype(bf16)
    rot_real = (dot(sum_r, cos) - dot(sum_i, sin)).astype(bf16)
    rot_imag = (dot(dif_i, cos) + dot(dif_r, sin)).astype(bf16)
    for q in range(COLS):
        out_ref[q, :count, :] = rot_real[:, q * LANES : (q + 1) * LANES]
        out_ref[q, count:, :] = rot_imag[:, q * LANES : (q + 1) * LANES]


def masks(place_ref, slots):
    col = place_ref[0]
    row = lax.broadcasted_iota(jnp.int32, (GROUPS * slots, 512), 0)
    return (lax.rem(row, slots) + col * slots) == 0, col < 2


def mix_forward_kernel(n, first_filter, place_ref, x_ref, kept_ref, recv_ref, tables, out_ref):
    slots = n // 8
    special, near = masks(place_ref, slots)
    cos, sin = tables[0], tables[1]
    up_r, up_i, down_r, down_i = spectrum(x_ref, 0, slots, special, cos, sin)
    real, imag = filters(near, kept_ref, recv_ref, first_filter, slots)
    up = (real[0] * up_r - imag[0] * up_i, real[0] * up_i + imag[0] * up_r)
    down = (real[1] * down_r - imag[1] * down_i, real[1] * down_i + imag[1] * down_r)
    put_inverse(out_ref, slots, special, up, down, cos, sin)


def mix_back_kernel(
    n, first_filter, first_field, first_grad, place_ref, x_ref, g_ref, kept_ref, recv_ref,
    tables, out_ref, total_ref, grad_ref, sem,
):
    slots = n // 8
    count = GROUPS * slots
    special, near = masks(place_ref, slots)
    field = spectrum(x_ref, first_field, slots, special, tables[0], tables[1])
    grad = spectrum(g_ref, first_grad, slots, special, tables[0], tables[1])
    terms = []
    for side in range(2):
        g_r, g_i = grad[2 * side], grad[2 * side + 1]
        s_r, s_i = field[2 * side], field[2 * side + 1]
        terms.append((g_r * s_r + g_i * s_i, g_i * s_r - g_r * s_i))
    for part in range(2):
        up, down = terms[0][part], terms[1][part]
        kept = jnp.where(near, up, down).astype(jnp.bfloat16)
        sent = jnp.where(near, down, up).astype(jnp.bfloat16)
        for q in range(COLS):
            lanes = slice(q * LANES, (q + 1) * LANES)
            grad_ref[q, part * count : (part + 1) * count, :] = kept[:, lanes]
            grad_ref[q, (2 + part) * count : (3 + part) * count, :] = sent[:, lanes]
    copy = pltpu.make_async_copy(grad_ref, total_ref, sem)
    copy.start()
    real, imag = filters(near, kept_ref, recv_ref, first_filter, slots)
    sides = []
    for side in range(2):
        g_r, g_i = grad[2 * side], grad[2 * side + 1]
        sides.append((real[side] * g_r + imag[side] * g_i, real[side] * g_i - imag[side] * g_r))
    last = tables.shape[0] - 2
    put_inverse(out_ref, slots, special, sides[0], sides[1], tables[last], tables[last + 1])
    copy.wait()


def smem():
    return pl.BlockSpec(memory_space=pltpu.SMEM)


def hbm(count):
    return [pl.BlockSpec(memory_space=pltpu.HBM)] * count


def vmem(count):
    return [pl.BlockSpec(memory_space=pltpu.VMEM)] * count


def mix_forward(n, place, entries, kept, recv, first_filter):
    rows = 2 * GROUPS * n // 8
    return pl.pallas_call(
        functools.partial(mix_forward_kernel, n, first_filter),
        out_shape=jax.ShapeDtypeStruct((COLS, rows, LANES), jnp.bfloat16),
        in_specs=[smem()] + vmem(4),
        name="mix_forward_" + str(n),
        **params(8 * rows * 512 * 512, 4 << 20),
    )(place, entries, kept, recv, constant(np.stack(col_tables(n))))


def mix_back(n, place, entries, first_field, upstream, first_grad, kept, recv, first_filter):
    rows = 2 * GROUPS * n // 8
    tables = col_tables(n)
    if n == H2:
        tables = tables + tuple(table.T for table in tables)
    total = (COLS, 2 * rows, LANES)
    return pl.pallas_call(
        functools.partial(mix_back_kernel, n, first_filter, first_field, first_grad),
        out_shape=(
            jax.ShapeDtypeStruct((COLS, rows, LANES), jnp.bfloat16),
            jax.ShapeDtypeStruct(total, jnp.bfloat16),
        ),
        in_specs=[smem()] + vmem(5),
        out_specs=tuple(vmem(1) + hbm(1)),
        scratch_shapes=[pltpu.VMEM(total, jnp.bfloat16), pltpu.SemaphoreType.DMA],
        name="mix_back_" + str(n),
        **params(12 * rows * 512 * 512, 6 << 20),
    )(place, entries, upstream, kept, recv, constant(np.stack(tables)))


def grid_of(rows, columns):
    shape = (rows, columns)
    return lax.broadcasted_iota(jnp.int32, shape, 0), lax.broadcasted_iota(jnp.int32, shape, 1)


def ones_at(mask):
    return jnp.where(mask, 1.0, 0.0).astype(jnp.bfloat16)


def kept_rows(near, slots):
    slot, local = grid_of(slots, 2 * slots)
    return ones_at(local == jnp.where(near, slot, slots - slot))


def sent_rows(near, slots):
    slot, local = grid_of(slots, 2 * slots)
    return ones_at(local == jnp.where(near, slots + slot, lax.rem(2 * slots - slot, 2 * slots)))


def quarter_lanes(quarter):
    wide_at, narrow_at = grid_of(512, LANES)
    return ones_at(
        wide_at == lax.div(narrow_at, 64) * 256 + 64 * quarter + lax.rem(narrow_at, 64)
    )


def second_pair(ref, part, g):
    pair = [ref[part, 2 * g + i].astype(jnp.bfloat16) for i in range(2)]
    return jnp.concatenate(pair, axis=1)


def send_filters_kernel(
    place_ref, first_ref, second_ref, sent_ref, zero_ref, first_buf, second_buf, sems
):
    quarter = place_ref[1]
    at = pl.ds(pl.multiple_of(quarter * LANES, LANES), LANES)
    first_copy = pltpu.make_async_copy(first_ref.at[:, :, :, at], first_buf, sems.at[0])
    second_copy = pltpu.make_async_copy(second_ref, second_buf, sems.at[1])
    first_copy.start()
    second_copy.start()
    near = place_ref[0] < 2
    zeros = []
    for n in (H1, H2):
        slots = n // 8
        first = 0 if n == H1 else 2 * GROUPS * H1 // 8
        pick = sent_rows(near, slots)
        if n == H1:
            first_copy.wait()
        else:
            second_copy.wait()
            lanes = quarter_lanes(quarter)
        for part in range(2):
            for g in range(GROUPS):
                if n == H1:
                    rows = first_buf[part, g].astype(jnp.bfloat16)
                else:
                    rows = dot(second_pair(second_buf, part, g), lanes).astype(jnp.bfloat16)
                rows = dot(pick, rows)
                zeros.append(rows[:1])
                sent_ref[first : first + slots, :] = rows.astype(jnp.bfloat16)
                first += slots
    zeros.append(jnp.zeros((4, LANES), jnp.float32))
    zero_ref[...] = jnp.concatenate(zeros, axis=0).astype(jnp.bfloat16)


def keep_filters_kernel(place_ref, first_ref, second_ref, kept_ref):
    near = place_ref[0] < 2
    first = 0
    lanes = [quarter_lanes(q) for q in range(COLS)]
    for n in (H1, H2):
        slots = n // 8
        pick = kept_rows(near, slots)
        for part in range(2):
            for g in range(GROUPS):
                if n == H1:
                    rows = first_ref[part, g].astype(jnp.bfloat16)
                else:
                    rows = second_pair(second_ref, part, g)
                rows = dot(pick, rows).astype(jnp.bfloat16)
                for q in range(COLS):
                    if n == H1:
                        cut = rows[:, q * LANES : (q + 1) * LANES]
                    else:
                        cut = dot(rows, lanes[q]).astype(jnp.bfloat16)
                    kept_ref[q, first : first + slots, :] = cut
                first += slots


FILTER_ROWS = 2 * GROUPS * (H1 + H2) // 8


def send_filters(place, filter_first, filter_second):
    return pl.pallas_call(
        send_filters_kernel,
        out_shape=(
            jax.ShapeDtypeStruct((FILTER_ROWS, LANES), jnp.bfloat16),
            jax.ShapeDtypeStruct((16, LANES), jnp.bfloat16),
        ),
        in_specs=[smem()] + hbm(2),
        scratch_shapes=[
            pltpu.VMEM((2, GROUPS, H1 // 4, LANES), jnp.float32),
            pltpu.VMEM((2, 2 * GROUPS, H2 // 4, H2), jnp.float32),
            pltpu.SemaphoreType.DMA((2,)),
        ],
        name="send_filters",
        **params(12 * 64 * 512 * 128 * 2, 2 << 20),
    )(place, filter_first, filter_second)


def keep_filters(place, filter_first, filter_second):
    return pl.pallas_call(
        keep_filters_kernel,
        out_shape=jax.ShapeDtypeStruct((COLS, FILTER_ROWS, LANES), jnp.bfloat16),
        in_specs=[smem()] + vmem(2),
        name="keep_filters",
        **params(12 * 64 * 512 * 512 * 2, 4 << 20),
    )(place, filter_first, filter_second)


def put_slot_zero(block, zero, take, slots):
    shaped = block.reshape(2 * GROUPS, slots, LANES)
    here = (jnp.arange(slots) == 0)[None, :, None] & take
    return jnp.where(here, zero[:, None, :], shaped).reshape(2 * GROUPS * slots, LANES)


def put_slots_zero(block, zero, take):
    split, groups = 2 * GROUPS * H1 // 8, 2 * GROUPS
    return (
        put_slot_zero(block[:split], zero[:groups], take, H1 // 8),
        put_slot_zero(block[split:], zero[groups : 2 * groups], take, H2 // 8),
    )


def swap_filters(sent, zero):
    return lax.ppermute(sent, "col", SWAP), lax.ppermute(zero, "col", ((2, 0), (3, 1)))


def patch_filters(recv, zero, col):
    recv = jnp.concatenate(put_slots_zero(recv, zero, col < 2), axis=0)
    return lax.all_gather(recv, "rep", axis=0, tiled=False)


def place_grads_kernel(
    place_ref, kept_first, recv_first, kept_second, recv_second, first_ref, second_ref
):
    near = place_ref[0] < 2
    wide_at, narrow_at = grid_of(LANES, LANES // 2)
    lanes = [ones_at(wide_at == narrow_at + 64 * i) for i in range(2)]
    for n, kept, recv in ((H1, kept_first, recv_first), (H2, kept_second, recv_second)):
        slots = n // 8
        local, slot = grid_of(2 * slots, slots)
        mirror = lax.rem(2 * slots - slot, 2 * slots)
        pick_kept = ones_at(local == jnp.where(near, slot, slots - slot))
        pick_recv = ones_at(local == jnp.where(near, slots + slot, mirror))
        for part in range(2):
            for g in range(GROUPS):
                at = (part * GROUPS + g) * slots
                rows = dot(pick_kept, kept[at : at + slots]) + dot(
                    pick_recv, recv[at : at + slots]
                )
                if n == H1:
                    first_ref[part, g] = rows
                else:
                    rows = rows.astype(jnp.bfloat16)
                    for i in range(2):
                        second_ref[part, 2 * g + i] = dot(rows, lanes[i])


def summed(terms):
    return lax.psum_scatter(terms, "rep", scatter_dimension=0, tiled=False)


def swap_grads(sum_first, sum_second):
    count_first, count_second = 2 * GROUPS * H1 // 8, 2 * GROUPS * H2 // 8
    sent = jnp.concatenate([sum_first[count_first:], sum_second[count_second:]], axis=0)
    zero = jnp.concatenate(
        [
            sum_first[count_first:].reshape(2 * GROUPS, H1 // 8, LANES)[:, 0],
            sum_second[count_second:].reshape(2 * GROUPS, H2 // 8, LANES)[:, 0],
            jnp.zeros((4, LANES), jnp.bfloat16),
        ],
        axis=0,
    )
    return lax.ppermute(sent, "col", SWAP), lax.ppermute(zero, "col", ((0, 2), (1, 3)))


def place_grads(place, sum_first, sum_second, swapped, col):
    count_first, count_second = 2 * GROUPS * H1 // 8, 2 * GROUPS * H2 // 8
    recv_first, recv_second = put_slots_zero(*swapped, col >= 2)
    return pl.pallas_call(
        place_grads_kernel,
        out_shape=(
            jax.ShapeDtypeStruct((2, GROUPS, H1 // 4, LANES), jnp.float32),
            jax.ShapeDtypeStruct((2, 2 * GROUPS, H2 // 4, LANES // 2), jnp.float32),
        ),
        in_specs=[smem()] + vmem(4),
        name="place_grads",
        **params(12 * 128 * 128 * 128 * 2, 2 << 20),
    )(place, sum_first[:count_first], recv_first, sum_second[:count_second], recv_second)


def layer_normalize(entry_values, gains):
    center = entry_values - jnp.mean(entry_values, axis=1, keepdims=True)
    spread = jnp.mean(center * center, axis=1, keepdims=True)
    return center * lax.rsqrt(spread + epsilon) * gains[None, :, None, None]


def norm_pullback_step(entry_values, gains, upstream):
    _, pullback = jax.vjp(lambda inner_vals: layer_normalize(inner_vals, gains), entry_values)
    return pullback(upstream.astype(jnp.float32))[0]


def fold(values):
    total = jnp.broadcast_to(jnp.sum(values, axis=0, keepdims=True), (8, LANES))
    return (total + pltpu.roll(total, LANES // 2, 1))[:1]


def standardize(values):
    center = values - fold(values) / 192.0
    scale = lax.rsqrt(fold(center * center) / 192.0 + epsilon)
    return center * scale, scale


def pack_pairs(block):
    fields = block.astype(jnp.float32).reshape(96, 2, 8, 64)
    at, lane = grid_of(64, LANES)
    return sum(
        dot(fields[:, i].reshape(768, 64).astype(jnp.bfloat16), ones_at(lane == at + 64 * i))
        for i in range(2)
    )


def first_norm_kernel(x_ref, g_ref, gain_ref, out_ref, x_buf, g_buf, gain_buf, sems):
    copies = [
        pltpu.make_async_copy(source, target, sems.at[i])
        for i, (source, target) in enumerate(
            ((x_ref, x_buf), (gain_ref, gain_buf), (g_ref, g_buf))
        )
    ]
    for copy in copies:
        copy.start()
    copies[0].wait()
    copies[1].wait()
    pixels = x_buf[...].astype(jnp.float32)
    center = pixels - jnp.sum(pixels, axis=0, keepdims=True) / 96.0
    scale = lax.rsqrt(jnp.sum(center * center, axis=0) / 96.0 + epsilon)
    for c in range(96):
        at = (c % GROUPS) * 16
        out_ref[c // GROUPS, at : at + 16, :] = (center[c] * scale * gain_buf[c]).astype(
            jnp.bfloat16
        )
    copies[2].wait()
    packed = pack_pairs(g_buf[...]).reshape(ROWS, GROUPS * 8, LANES)
    out_ref[:, GROUPS * 16 :, :] = packed.astype(jnp.bfloat16)


def first_norm(images, grad_out, gains):
    return pl.pallas_call(
        first_norm_kernel,
        out_shape=jax.ShapeDtypeStruct((ROWS, GROUPS * 24, LANES), jnp.bfloat16),
        in_specs=hbm(3),
        scratch_shapes=[
            pltpu.VMEM((96, 16, LANES), jnp.bfloat16),
            pltpu.VMEM((192, 8, 64), jnp.bfloat16),
            pltpu.SMEM((96,), jnp.float32),
            pltpu.SemaphoreType.DMA((3,)),
        ],
        name="first_norm",
        **params(4 * 768 * 64 * 128, 2 << 20),
    )(images, grad_out, gains)


def low_half():
    return lax.broadcasted_iota(jnp.int32, (96, LANES), 1) < LANES // 2


def reduce_kernel(
    x_hbm, m_ref, w_hbm, gain_ref, norm_ref, down_hbm, x_ref, w_ref, down_ref, s_ref, n_ref, sems
):
    copies = [
        pltpu.make_async_copy(x_hbm, x_ref, sems.at[0]),
        pltpu.make_async_copy(w_hbm, w_ref, sems.at[1]),
    ]
    for copy in copies:
        copy.start()
    at, lane = grid_of(LANES, 2 * LANES)
    spread_at = ones_at(at == 2 * lax.rem(lane, 64) + lax.div(lane, LANES))
    copies[0].wait()
    mixed = m_ref[...].astype(jnp.float32).reshape(1536, LANES)
    section = x_ref[...].astype(jnp.float32).reshape(1536, LANES) + mixed
    spread = dot(section.astype(jnp.bfloat16), spread_at)
    for e in range(2):
        s_ref[e] = spread[:, e * LANES : (e + 1) * LANES]
    low = low_half()
    copies[1].wait()
    for first in range(0, 8, 2):
        patches = [
            jnp.concatenate(
                [
                    s_ref[e, pl.ds(2 * i + a, 96, stride=16), :].astype(jnp.bfloat16)
                    for a in range(2)
                    for e in range(2)
                ],
                axis=0,
            )
            for i in (first, first + 1)
        ]
        both = dot(w_ref[...], jnp.concatenate(patches, axis=1))
        for i in range(2):
            block = both[:, i * LANES : (i + 1) * LANES]
            down = jnp.where(low, block[:96], block[96:]).astype(jnp.bfloat16)
            down_ref[first + i] = down
            normed, _ = standardize(down.astype(jnp.float32))
            n_ref[pl.ds(first + i, 96, stride=8), :] = normed * gain_ref[...]
    copy = pltpu.make_async_copy(down_ref, down_hbm, sems.at[2])
    copy.start()
    norm_ref[...] = n_ref[...].reshape(ROWS, GROUPS * 8, LANES).astype(jnp.bfloat16)
    copy.wait()


def reduce_step(images, mixed, weight, gains):
    return pl.pallas_call(
        reduce_kernel,
        out_shape=(
            jax.ShapeDtypeStruct((ROWS, GROUPS * 8, LANES), jnp.bfloat16),
            jax.ShapeDtypeStruct((8, 96, LANES), jnp.bfloat16),
        ),
        in_specs=hbm(1) + vmem(1) + hbm(1) + vmem(1),
        out_specs=tuple(vmem(1) + hbm(1)),
        scratch_shapes=[
            pltpu.VMEM((96, 16, LANES), jnp.bfloat16),
            pltpu.VMEM((192, 384), jnp.bfloat16),
            pltpu.VMEM((8, 96, LANES), jnp.bfloat16),
            pltpu.VMEM((2, 1536, LANES), jnp.float32),
            pltpu.VMEM((768, LANES), jnp.float32),
            pltpu.SemaphoreType.DMA((3,)),
        ],
        name="reduce_step",
        **params(4 * 2 * 192 * 384 * 256, 2 << 20),
    )(images, mixed, weight, gains)


def expand_kernel(
    b_ref, down_hbm, g_hbm, w_hbm, gain_ref, out_ref,
    down_ref, g_ref, w_ref, back_ref, grad_ref, o_ref, sems,
):
    copies = [
        pltpu.make_async_copy(source, target, sems.at[i])
        for i, (source, target) in enumerate(
            ((g_hbm, g_ref), (down_hbm, down_ref), (w_hbm, w_ref))
        )
    ]
    for copy in copies:
        copy.start()
    at, lane = grid_of(2 * LANES, 2 * LANES)
    here = LANES * lax.rem(lax.div(at, 64), 2) + 2 * lax.rem(at, 64) + lax.div(at, LANES)
    merge_at = ones_at(lane == here)
    back_ref[...] = b_ref[...].astype(jnp.float32).reshape(768, LANES)
    for copy in copies:
        copy.wait()
    grad_ref[...] = pack_pairs(g_ref[...])
    low = low_half()
    for first in range(0, 8, 2):
        grads = []
        for i in (first, first + 1):
            normed, scale = standardize(down_ref[i].astype(jnp.float32))
            upstream = back_ref[pl.ds(i, 96, stride=8), :] * gain_ref[...]
            step = upstream - fold(upstream) / 192.0 - normed * (fold(upstream * normed) / 192.0)
            total = grad_ref[pl.ds(i, 96, stride=8), :] + scale * step
            total = total.astype(jnp.bfloat16).astype(jnp.float32)
            grads.append((total, pltpu.roll(total, LANES // 2, 1)))
        even = jnp.where(low, grads[0][0], grads[1][1])
        odd = jnp.where(low, grads[0][1], grads[1][0])
        both = jnp.concatenate([even, odd], axis=0).astype(jnp.bfloat16)
        patches = dot(w_ref[...], both).astype(jnp.bfloat16)
        rows = [
            jnp.concatenate(
                [patches[(2 * a + e) * 96 : (2 * a + e + 1) * 96] for e in range(2)], axis=1
            )
            for a in range(2)
        ]
        merged = dot(jnp.concatenate(rows, axis=0), merge_at)
        for i in range(2):
            for a in range(2):
                o_ref[pl.ds(2 * (first + i) + a, 96, stride=16), :] = merged[
                    a * 96 : (a + 1) * 96, i * LANES : (i + 1) * LANES
                ]
    out_ref[...] = o_ref[...].reshape(ROWS, GROUPS * 16, LANES).astype(jnp.bfloat16)


def expand_step(back, down, grad_out, weight, gains):
    return pl.pallas_call(
        expand_kernel,
        out_shape=jax.ShapeDtypeStruct((ROWS, GROUPS * 16, LANES), jnp.bfloat16),
        in_specs=vmem(1) + hbm(3) + vmem(1),
        scratch_shapes=[
            pltpu.VMEM((8, 96, LANES), jnp.bfloat16),
            pltpu.VMEM((192, 8, 64), jnp.bfloat16),
            pltpu.VMEM((384, 192), jnp.bfloat16),
            pltpu.VMEM((768, LANES), jnp.float32),
            pltpu.VMEM((768, LANES), jnp.float32),
            pltpu.VMEM((1536, LANES), jnp.float32),
            pltpu.SemaphoreType.DMA((3,)),
        ],
        name="expand_step",
        **params(4 * 2 * 192 * 384 * 256, 2 << 20),
    )(back, down, grad_out, weight, gains)


def unpack_first(blocks):
    return blocks.reshape(1, 96, 16, LANES)


def pack_second(field):
    pairs = field.reshape(96, 2, 8, 64).transpose(0, 2, 1, 3)
    return pairs.reshape(ROWS, GROUPS * 8, LANES)


def exchange(blocks, axis):
    return lax.all_to_all(blocks, axis, split_axis=0, concat_axis=0, tiled=True)


def shards(images, gain_first, filter_first, reduce_weight, gain_second, filter_second, grad_out):
    col = lax.axis_index("col")
    place = jnp.stack([col, lax.axis_index("rep")]).astype(jnp.int32)
    second_rows = 2 * GROUPS * H1 // 8
    pixels = images.reshape(96, 16, LANES)
    upstream = grad_out.reshape(192, 8, 64)
    weight = reduce_weight.reshape(96, 2, 384).transpose(1, 0, 2).reshape(192, 384)
    gains = jnp.repeat(gain_second.reshape(96, 2), 64, axis=1)

    sent, zero = send_filters(place, filter_first, filter_second)
    swapped = swap_filters(sent, zero)
    pixels, sent = lax.optimization_barrier((pixels, sent))
    both = exchange(first_norm(pixels, upstream, gain_first), "row")
    kept = keep_filters(place, filter_first, filter_second)
    half = forward_rows(both, (H1, H2))
    half, swapped = lax.optimization_barrier((half, swapped))
    recv = patch_filters(*swapped, col)
    both = exchange(half, "col")
    mixed = exchange(mix_forward(H1, place, both, kept, recv, 0), "col")
    mixed_one = exchange(inverse_rows(mixed, H1), "row")

    norm_two, down = reduce_step(pixels, mixed_one, weight, gains)
    half_two = exchange(forward_rows(exchange(norm_two, "row"), (H2,)), "col")
    dspec_two, terms_two = mix_back(
        H2, place, half_two, 0, both, second_rows, kept, recv, second_rows
    )
    sum_two = summed(terms_two)
    rot_two = exchange(dspec_two, "col")
    rot_two, sum_two = lax.optimization_barrier((rot_two, sum_two))
    back_two = exchange(inverse_rows(rot_two, H2), "row")

    grad_section = expand_step(back_two, down, upstream, weight.T, gains)
    half_grad = exchange(forward_rows(exchange(grad_section, "row"), (H1,)), "col")
    dspec_one, terms_one = mix_back(H1, place, both, 0, half_grad, 0, kept, recv, 0)
    sum_one = summed(terms_one)
    rot_one = exchange(dspec_one, "col")
    rot_one, sum_one = lax.optimization_barrier((rot_one, sum_one))
    swapped = swap_grads(sum_one, sum_two)
    grad_norm_one = unpack_first(exchange(inverse_rows(rot_one, H1), "row"))
    grad_images = (
        unpack_first(grad_section).astype(jnp.float32)
        + norm_pullback_step(images.astype(jnp.float32), gain_first, grad_norm_one)
    ).astype(jnp.bfloat16)
    grad_first, grad_second = place_grads(place, sum_one, sum_two, swapped, col)
    return (grad_images, grad_first, grad_second)


def solution(mesh):
    placed = (
        P("rep", None, "row", "col"),
        P(),
        P(None, "row", "col", None),
        P(),
        P(),
        P(None, "row", "col", None),
        P("rep", None, "row", "col"),
    )
    return jax.shard_map(
        shards,
        mesh=mesh,
        in_specs=placed,
        out_specs=(
            P("rep", None, "row", "col"),
            P(None, "row", "col", "rep"),
            P(None, "row", "col", "rep"),
        ),
        check_vma=False,
    )
```

```python
import functools
import math

import jax
import jax.numpy as jnp
import numpy as np
from jax import lax
from jax.experimental import pallas as pl
from jax.experimental.pallas import tpu as pltpu
from jax.sharding import PartitionSpec as P

H1 = 512
H2 = 256
GROUPS = 3
COLS = 4
ROWS = 32
LANES = 128
SECOND_SLOT = 2 * GROUPS * H1 // 8
FILTER_ROWS = 2 * GROUPS * (H1 + H2) // 8

epsilon = 1e-06

ORDER = (0, 2, 3, 1)
SWAP = ((0, 3), (3, 0), (1, 2), (2, 1))


def cos_sin(n):
    index = np.arange(n)
    angles = (index[:, None] * index[None, :] % n) * (2.0 * math.pi / n)
    factor = 1.0 / math.sqrt(n)
    return np.cos(angles) * factor, np.sin(angles) * factor


def row_table(n):
    cos, sin = cos_sin(n)
    slots = n // 8
    parts = []
    for c in range(COLS):
        k = ORDER[c] * slots + np.arange(slots)
        real, imag = cos[k], -sin[k]
        if c == 0:
            imag[0] = cos[n // 2]
        parts += [real, imag]
    return np.concatenate(parts, axis=0)


def col_tables(n):
    cos, sin = cos_sin(n)
    pair = 512 // n
    width = LANES // pair
    if pair == 1:
        return cos, sin
    out = []
    for table in (cos, sin):
        blocks = table.reshape(COLS, width, COLS, width)
        full = np.zeros((COLS, pair, width, COLS, pair, width))
        for p in range(pair):
            full[:, p, :, :, p, :] = blocks
        out.append(full.reshape(512, 512))
    return tuple(out)


def constant(values):
    return jnp.asarray(np.asarray(values, np.float32).astype(jnp.bfloat16))


def dot(a, b):
    return jnp.dot(a, b, preferred_element_type=jnp.float32)


def params(flops, traffic, vmem_mib=40):
    return dict(
        compiler_params=pltpu.CompilerParams(vmem_limit_bytes=vmem_mib * 1024 * 1024),
        cost_estimate=pl.CostEstimate(flops=flops, bytes_accessed=traffic, transcendentals=0),
    )


def gather_rows(block, rows):
    parts = []
    for g in range(GROUPS):
        part = block[:, g * rows : (g + 1) * rows, :]
        if rows % 16:
            part = part.astype(jnp.float32)
        parts.append(part.reshape(ROWS * rows, LANES).astype(jnp.bfloat16))
    return jnp.concatenate(parts, axis=1)


def forward_rows_kernel(layout, *refs):
    x_ref, tables, out_ref = refs[0], refs[1:-1], refs[-1]
    for (n, first_in, first_out), table in zip(layout, tables):
        rows = n // ROWS
        slots = n // 8
        block = x_ref[:, first_in : first_in + GROUPS * rows, :]
        half = dot(table[...], gather_rows(block, rows)).astype(jnp.bfloat16)
        half = half.reshape(COLS, 2, slots, GROUPS * LANES)
        for part in range(2):
            for g in range(GROUPS):
                at = first_out + (part * GROUPS + g) * slots
                out_ref[:, at : at + slots, :] = half[:, part, :, g * LANES : (g + 1) * LANES]


def forward_rows(entries, sizes):
    layout, _, slots = layout_of(sizes)
    flops = sum(2 * n * n * GROUPS * LANES for n in sizes)
    return pl.pallas_call(
        functools.partial(forward_rows_kernel, layout),
        out_shape=jax.ShapeDtypeStruct((COLS, slots, LANES), jnp.bfloat16),
        name="forward_rows_" + "_".join(str(n) for n in sizes),
        **params(flops, 2 << 20),
    )(entries, *[constant(row_table(n)) for n in sizes])


def inverse_rows_kernel(layout, *refs):
    x_ref, tables, out_ref = refs[0], refs[1:-1], refs[-1]
    for (n, first_out, first_in), table in zip(layout, tables):
        rows = n // ROWS
        slots = n // 8
        parts = []
        for g in range(GROUPS):
            both = []
            for part in range(2):
                at = first_in + (part * GROUPS + g) * slots
                both.append(x_ref[:, at : at + slots, :].reshape(COLS, 1, slots, LANES))
            parts.append(jnp.concatenate(both, axis=1).reshape(n, LANES))
        result = dot(table[...], jnp.concatenate(parts, axis=1))
        pieces = [
            result[:, g * LANES : (g + 1) * LANES].reshape(ROWS, rows, LANES)
            for g in range(GROUPS)
        ]
        out_ref[:, first_out : first_out + GROUPS * rows, :] = jnp.concatenate(
            pieces, axis=1
        ).astype(jnp.bfloat16)


def layout_of(sizes):
    layout, first_token, first_slot = [], 0, 0
    for n in sizes:
        layout.append((n, first_token, first_slot))
        first_token += GROUPS * n // ROWS
        first_slot += 2 * GROUPS * n // 8
    return tuple(layout), first_token, first_slot


def inverse_rows(entries, sizes):
    layout, tokens, _ = layout_of(sizes)
    flops = sum(2 * n * n * GROUPS * LANES for n in sizes)
    return pl.pallas_call(
        functools.partial(inverse_rows_kernel, layout),
        out_shape=jax.ShapeDtypeStruct((ROWS, tokens, LANES), jnp.bfloat16),
        name="inverse_rows_" + "_".join(str(n) for n in sizes),
        **params(flops, 2 << 20),
    )(entries, *[constant(row_table(n).T) for n in sizes])


def wide(ref, first, count):
    return jnp.concatenate([ref[q, first : first + count, :] for q in range(COLS)], axis=1)


def spectrum(ref, first, slots, special, cos, sin):
    count = GROUPS * slots
    real, imag = wide(ref, first, count), wide(ref, first + count, count)
    real_cos, real_sin = dot(real, cos), dot(real, sin)
    imag_cos, imag_sin = dot(imag, cos), dot(imag, sin)
    return (
        jnp.where(special, real_cos, real_cos + imag_sin),
        jnp.where(special, -real_sin, imag_cos - real_sin),
        jnp.where(special, imag_cos, real_cos - imag_sin),
        jnp.where(special, -imag_sin, -imag_cos - real_sin),
    )


def filters(near, kept_ref, recv_ref, first, slots):
    count = GROUPS * slots
    out = []
    for part in range(2):
        kept = wide(kept_ref, first + part * count, count).astype(jnp.float32)
        recv = wide(recv_ref, first + part * count, count).astype(jnp.float32)
        out.append((jnp.where(near, kept, recv), jnp.where(near, recv, kept)))
    return out


def put_inverse(out_ref, first, slots, special, up, down, cos, sin):
    count = GROUPS * slots
    (up_r, up_i), (down_r, down_i) = up, down
    bf16 = jnp.bfloat16
    sum_r = jnp.where(special, up_r, up_r + down_r).astype(bf16)
    sum_i = jnp.where(special, up_i, up_i + down_i).astype(bf16)
    dif_i = jnp.where(special, down_r, up_i - down_i).astype(bf16)
    dif_r = jnp.where(special, -down_i, up_r - down_r).astype(bf16)
    rot_real = (dot(sum_r, cos) - dot(sum_i, sin)).astype(bf16)
    rot_imag = (dot(dif_i, cos) + dot(dif_r, sin)).astype(bf16)
    for q in range(COLS):
        lanes = slice(q * LANES, (q + 1) * LANES)
        out_ref[q, first : first + count, :] = rot_real[:, lanes]
        out_ref[q, first + count : first + 2 * count, :] = rot_imag[:, lanes]


def masks(place_ref, slots):
    col = place_ref[0]
    row = lax.broadcasted_iota(jnp.int32, (GROUPS * slots, 512), 0)
    return (lax.rem(row, slots) + col * slots) == 0, col < 2


def apply_back(real, imag, grad):
    return [
        (
            real[side] * grad[2 * side] + imag[side] * grad[2 * side + 1],
            real[side] * grad[2 * side + 1] - imag[side] * grad[2 * side],
        )
        for side in range(2)
    ]


def mix_first_kernel(place_ref, x_ref, kept_ref, recv_ref, first_tables, second_tables, out_ref):
    slots = H1 // 8
    special, near = masks(place_ref, slots)
    cos, sin = first_tables[0], first_tables[1]
    up_r, up_i, down_r, down_i = spectrum(x_ref, 0, slots, special, cos, sin)
    real, imag = filters(near, kept_ref, recv_ref, 0, slots)
    up = (real[0] * up_r - imag[0] * up_i, real[0] * up_i + imag[0] * up_r)
    down = (real[1] * down_r - imag[1] * down_i, real[1] * down_i + imag[1] * down_r)
    put_inverse(out_ref, 0, slots, special, up, down, cos, sin)

    first, slots = SECOND_SLOT, H2 // 8
    special, near = masks(place_ref, slots)
    cos, sin = second_tables[0], second_tables[1]
    grad = spectrum(x_ref, first, slots, special, cos, sin)
    real, imag = filters(near, kept_ref, recv_ref, first, slots)
    up, down = apply_back(real, imag, grad)
    put_inverse(out_ref, first, slots, special, up, down, cos, sin)


def put_terms(out_ref, first, slots, near, field, grad):
    count = GROUPS * slots
    terms = []
    for side in range(2):
        g_r, g_i = grad[2 * side], grad[2 * side + 1]
        s_r, s_i = field[2 * side], field[2 * side + 1]
        terms.append((g_r * s_r + g_i * s_i, g_i * s_r - g_r * s_i))
    for part in range(2):
        up, down = terms[0][part], terms[1][part]
        kept = jnp.where(near, up, down).astype(jnp.bfloat16)
        sent = jnp.where(near, down, up).astype(jnp.bfloat16)
        at = first + part * count
        for q in range(COLS):
            lanes = slice(q * LANES, (q + 1) * LANES)
            out_ref[q, at : at + count, :] = kept[:, lanes]
            out_ref[q, FILTER_ROWS + at : FILTER_ROWS + at + count, :] = sent[:, lanes]


def mix_last_kernel(
    place_ref, x_ref, y_ref, kept_ref, recv_ref, first_tables, second_tables,
    out_ref, total_ref, terms_ref, sem,
):
    slots = H2 // 8
    special, near = masks(place_ref, slots)
    tables = second_tables[0], second_tables[1]
    grad = spectrum(x_ref, SECOND_SLOT, slots, special, *tables)
    field = spectrum(y_ref, SECOND_SLOT, slots, special, *tables)
    put_terms(terms_ref, SECOND_SLOT, slots, near, field, grad)
    slots = H1 // 8
    special, near = masks(place_ref, slots)
    tables = first_tables[0], first_tables[1]
    field = spectrum(x_ref, 0, slots, special, *tables)
    grad = spectrum(y_ref, 0, slots, special, *tables)
    put_terms(terms_ref, 0, slots, near, field, grad)
    copy = pltpu.make_async_copy(terms_ref, total_ref, sem)
    copy.start()
    real, imag = filters(near, kept_ref, recv_ref, 0, slots)
    up, down = apply_back(real, imag, grad)
    put_inverse(out_ref, 0, slots, special, up, down, *tables)
    copy.wait()


def smem():
    return pl.BlockSpec(memory_space=pltpu.SMEM)


def hbm(count):
    return [pl.BlockSpec(memory_space=pltpu.HBM)] * count


def vmem(count):
    return [pl.BlockSpec(memory_space=pltpu.VMEM)] * count


def both_tables():
    return [constant(np.stack(col_tables(n))) for n in (H1, H2)]


def mix_first(place, entries, kept, recv):
    return pl.pallas_call(
        mix_first_kernel,
        out_shape=jax.ShapeDtypeStruct((COLS, FILTER_ROWS, LANES), jnp.bfloat16),
        in_specs=[smem()] + vmem(5),
        name="mix_first",
        **params(8 * FILTER_ROWS * 512 * 512, 6 << 20),
    )(place, entries, kept, recv, *both_tables())


def mix_last(place, entries, later, kept, recv):
    total = (COLS, 2 * FILTER_ROWS, LANES)
    return pl.pallas_call(
        mix_last_kernel,
        out_shape=(
            jax.ShapeDtypeStruct((COLS, SECOND_SLOT, LANES), jnp.bfloat16),
            jax.ShapeDtypeStruct(total, jnp.bfloat16),
        ),
        in_specs=[smem()] + vmem(6),
        out_specs=tuple(vmem(1) + hbm(1)),
        scratch_shapes=[pltpu.VMEM(total, jnp.bfloat16), pltpu.SemaphoreType.DMA],
        name="mix_last",
        **params(12 * FILTER_ROWS * 512 * 512, 8 << 20),
    )(place, entries, later, kept, recv, *both_tables())


def grid_of(rows, columns):
    shape = (rows, columns)
    return lax.broadcasted_iota(jnp.int32, shape, 0), lax.broadcasted_iota(jnp.int32, shape, 1)


def ones_at(mask):
    return jnp.where(mask, 1.0, 0.0).astype(jnp.bfloat16)


def kept_rows(near, slots):
    slot, local = grid_of(slots, 2 * slots)
    return ones_at(local == jnp.where(near, slot, slots - slot))


def sent_rows(near, slots):
    slot, local = grid_of(slots, 2 * slots)
    return ones_at(local == jnp.where(near, slots + slot, lax.rem(2 * slots - slot, 2 * slots)))


def quarter_lanes(quarter):
    wide_at, narrow_at = grid_of(512, LANES)
    return ones_at(
        wide_at == lax.div(narrow_at, 64) * 256 + 64 * quarter + lax.rem(narrow_at, 64)
    )


def second_pair(ref, part, g):
    pair = [ref[part, 2 * g + i].astype(jnp.bfloat16) for i in range(2)]
    return jnp.concatenate(pair, axis=1)


def send_filters_kernel(
    place_ref, first_ref, second_ref, sent_ref, zero_ref, first_buf, second_buf, sems
):
    quarter = place_ref[1]
    at = pl.ds(pl.multiple_of(quarter * LANES, LANES), LANES)
    first_copy = pltpu.make_async_copy(first_ref.at[:, :, :, at], first_buf, sems.at[0])
    second_copy = pltpu.make_async_copy(second_ref, second_buf, sems.at[1])
    first_copy.start()
    second_copy.start()
    near = place_ref[0] < 2
    zeros = []
    for n in (H1, H2):
        slots = n // 8
        first = 0 if n == H1 else 2 * GROUPS * H1 // 8
        pick = sent_rows(near, slots)
        if n == H1:
            first_copy.wait()
        else:
            second_copy.wait()
            lanes = quarter_lanes(quarter)
        for part in range(2):
            for g in range(GROUPS):
                if n == H1:
                    rows = first_buf[part, g].astype(jnp.bfloat16)
                else:
                    rows = dot(second_pair(second_buf, part, g), lanes).astype(jnp.bfloat16)
                rows = dot(pick, rows)
                zeros.append(rows[:1])
                sent_ref[first : first + slots, :] = rows.astype(jnp.bfloat16)
                first += slots
    zeros.append(jnp.zeros((4, LANES), jnp.float32))
    zero_ref[...] = jnp.concatenate(zeros, axis=0).astype(jnp.bfloat16)


def keep_filters_kernel(place_ref, first_ref, second_ref, kept_ref):
    near = place_ref[0] < 2
    first = 0
    lanes = [quarter_lanes(q) for q in range(COLS)]
    for n in (H1, H2):
        slots = n // 8
        pick = kept_rows(near, slots)
        for part in range(2):
            for g in range(GROUPS):
                if n == H1:
                    rows = first_ref[part, g].astype(jnp.bfloat16)
                else:
                    rows = second_pair(second_ref, part, g)
                rows = dot(pick, rows).astype(jnp.bfloat16)
                for q in range(COLS):
                    if n == H1:
                        cut = rows[:, q * LANES : (q + 1) * LANES]
                    else:
                        cut = dot(rows, lanes[q]).astype(jnp.bfloat16)
                    kept_ref[q, first : first + slots, :] = cut
                first += slots


def send_filters(place, filter_first, filter_second):
    return pl.pallas_call(
        send_filters_kernel,
        out_shape=(
            jax.ShapeDtypeStruct((FILTER_ROWS, LANES), jnp.bfloat16),
            jax.ShapeDtypeStruct((16, LANES), jnp.bfloat16),
        ),
        in_specs=[smem()] + hbm(2),
        scratch_shapes=[
            pltpu.VMEM((2, GROUPS, H1 // 4, LANES), jnp.float32),
            pltpu.VMEM((2, 2 * GROUPS, H2 // 4, H2), jnp.float32),
            pltpu.SemaphoreType.DMA((2,)),
        ],
        name="send_filters",
        **params(12 * 64 * 512 * 128 * 2, 2 << 20, 60),
    )(place, filter_first, filter_second)


def keep_filters(place, filter_first, filter_second):
    return pl.pallas_call(
        keep_filters_kernel,
        out_shape=jax.ShapeDtypeStruct((COLS, FILTER_ROWS, LANES), jnp.bfloat16),
        in_specs=[smem()] + vmem(2),
        name="keep_filters",
        **params(12 * 64 * 512 * 512 * 2, 4 << 20),
    )(place, filter_first, filter_second)


def put_slot_zero(block, zero, take, slots):
    shaped = block.reshape(2 * GROUPS, slots, LANES)
    here = (jnp.arange(slots) == 0)[None, :, None] & take
    return jnp.where(here, zero[:, None, :], shaped).reshape(2 * GROUPS * slots, LANES)


def put_slots_zero(block, zero, take):
    split, groups = 2 * GROUPS * H1 // 8, 2 * GROUPS
    return (
        put_slot_zero(block[:split], zero[:groups], take, H1 // 8),
        put_slot_zero(block[split:], zero[groups : 2 * groups], take, H2 // 8),
    )


def swap_filters(sent, zero):
    return lax.ppermute(sent, "col", SWAP), lax.ppermute(zero, "col", ((2, 0), (3, 1)))


def patch_filters(recv, zero, col):
    recv = jnp.concatenate(put_slots_zero(recv, zero, col < 2), axis=0)
    return lax.all_gather(recv, "rep", axis=0, tiled=False)


def place_grads_kernel(
    place_ref, kept_first, recv_first, kept_second, recv_second, first_ref, second_ref
):
    near = place_ref[0] < 2
    wide_at, narrow_at = grid_of(LANES, LANES // 2)
    lanes = [ones_at(wide_at == narrow_at + 64 * i) for i in range(2)]
    for n, kept, recv in ((H1, kept_first, recv_first), (H2, kept_second, recv_second)):
        slots = n // 8
        local, slot = grid_of(2 * slots, slots)
        mirror = lax.rem(2 * slots - slot, 2 * slots)
        pick_kept = ones_at(local == jnp.where(near, slot, slots - slot))
        pick_recv = ones_at(local == jnp.where(near, slots + slot, mirror))
        for part in range(2):
            for g in range(GROUPS):
                at = (part * GROUPS + g) * slots
                rows = dot(pick_kept, kept[at : at + slots]) + dot(
                    pick_recv, recv[at : at + slots]
                )
                if n == H1:
                    first_ref[part, g] = rows
                else:
                    rows = rows.astype(jnp.bfloat16)
                    for i in range(2):
                        second_ref[part, 2 * g + i] = dot(rows, lanes[i])


def summed(terms):
    return lax.psum_scatter(terms, "rep", scatter_dimension=0, tiled=False)


def swap_grads(sent):
    groups = 2 * GROUPS
    zero = jnp.concatenate(
        [
            sent[:SECOND_SLOT].reshape(groups, H1 // 8, LANES)[:, 0],
            sent[SECOND_SLOT:].reshape(groups, H2 // 8, LANES)[:, 0],
            jnp.zeros((4, LANES), jnp.bfloat16),
        ],
        axis=0,
    )
    return lax.ppermute(sent, "col", SWAP), lax.ppermute(zero, "col", ((0, 2), (1, 3)))


def place_grads(place, kept, swapped, col):
    recv_first, recv_second = put_slots_zero(*swapped, col >= 2)
    return pl.pallas_call(
        place_grads_kernel,
        out_shape=(
            jax.ShapeDtypeStruct((2, GROUPS, H1 // 4, LANES), jnp.float32),
            jax.ShapeDtypeStruct((2, 2 * GROUPS, H2 // 4, LANES // 2), jnp.float32),
        ),
        in_specs=[smem()] + vmem(4),
        name="place_grads",
        **params(12 * 128 * 128 * 128 * 2, 2 << 20),
    )(place, kept[:SECOND_SLOT], recv_first, kept[SECOND_SLOT:], recv_second)


def layer_normalize(entry_values, gains):
    center = entry_values - jnp.mean(entry_values, axis=1, keepdims=True)
    spread = jnp.mean(center * center, axis=1, keepdims=True)
    return center * lax.rsqrt(spread + epsilon) * gains[None, :, None, None]


def norm_pullback_step(entry_values, gains, upstream):
    _, pullback = jax.vjp(lambda inner_vals: layer_normalize(inner_vals, gains), entry_values)
    return pullback(upstream.astype(jnp.float32))[0]


def fold(values):
    total = jnp.broadcast_to(jnp.sum(values, axis=0, keepdims=True), (8, LANES))
    return (total + pltpu.roll(total, LANES // 2, 1))[:1]


def standardize(values):
    center = values - fold(values) / 192.0
    scale = lax.rsqrt(fold(center * center) / 192.0 + epsilon)
    return center * scale, scale


def pack_pairs(block):
    fields = block.astype(jnp.float32).reshape(96, 2, 8, 64)
    at, lane = grid_of(64, LANES)
    return sum(
        dot(fields[:, i].reshape(768, 64).astype(jnp.bfloat16), ones_at(lane == at + 64 * i))
        for i in range(2)
    )


def first_norm_kernel(x_ref, g_ref, gain_ref, out_ref, x_buf, g_buf, gain_buf, sems):
    copies = [
        pltpu.make_async_copy(source, target, sems.at[i])
        for i, (source, target) in enumerate(
            ((x_ref, x_buf), (gain_ref, gain_buf), (g_ref, g_buf))
        )
    ]
    for copy in copies:
        copy.start()
    copies[0].wait()
    copies[1].wait()
    pixels = x_buf[...].astype(jnp.float32)
    center = pixels - jnp.sum(pixels, axis=0, keepdims=True) / 96.0
    scale = lax.rsqrt(jnp.sum(center * center, axis=0) / 96.0 + epsilon)
    for c in range(96):
        at = (c % GROUPS) * 16
        out_ref[c // GROUPS, at : at + 16, :] = (center[c] * scale * gain_buf[c]).astype(
            jnp.bfloat16
        )
    copies[2].wait()
    packed = pack_pairs(g_buf[...]).reshape(ROWS, GROUPS * 8, LANES)
    out_ref[:, GROUPS * 16 :, :] = packed.astype(jnp.bfloat16)


def first_norm(images, grad_out, gains):
    return pl.pallas_call(
        first_norm_kernel,
        out_shape=jax.ShapeDtypeStruct((ROWS, GROUPS * 24, LANES), jnp.bfloat16),
        in_specs=hbm(3),
        scratch_shapes=[
            pltpu.VMEM((96, 16, LANES), jnp.bfloat16),
            pltpu.VMEM((192, 8, 64), jnp.bfloat16),
            pltpu.SMEM((96,), jnp.float32),
            pltpu.SemaphoreType.DMA((3,)),
        ],
        name="first_norm",
        **params(4 * 768 * 64 * 128, 2 << 20, 60),
    )(images, grad_out, gains)


def low_half():
    return lax.broadcasted_iota(jnp.int32, (96, LANES), 1) < LANES // 2


def token_kernel(
    x_hbm, m_ref, g_hbm, w_hbm, wt_hbm, gain_ref, out_ref,
    x_ref, g_ref, w_ref, wt_ref, s_ref, n_ref, back_ref, grad_ref, o_ref, sems,
):
    copies = [
        pltpu.make_async_copy(source, target, sems.at[i])
        for i, (source, target) in enumerate(
            ((x_hbm, x_ref), (w_hbm, w_ref), (g_hbm, g_ref), (wt_hbm, wt_ref))
        )
    ]
    for copy in copies:
        copy.start()
    at, lane = grid_of(LANES, 2 * LANES)
    spread_at = ones_at(at == 2 * lax.rem(lane, 64) + lax.div(lane, LANES))
    at, lane = grid_of(2 * LANES, 2 * LANES)
    here = LANES * lax.rem(lax.div(at, 64), 2) + 2 * lax.rem(at, 64) + lax.div(at, LANES)
    merge_at = ones_at(lane == here)
    mixed = m_ref[:, : GROUPS * 16, :].astype(jnp.float32).reshape(1536, LANES)
    back_ref[...] = m_ref[:, GROUPS * 16 :, :].astype(jnp.float32).reshape(768, LANES)
    copies[0].wait()
    section = x_ref[...].astype(jnp.float32).reshape(1536, LANES) + mixed
    spread = dot(section.astype(jnp.bfloat16), spread_at)
    for e in range(2):
        s_ref[e] = spread[:, e * LANES : (e + 1) * LANES]
    low = low_half()
    for copy in copies[1:]:
        copy.wait()
    grad_ref[...] = pack_pairs(g_ref[...])
    for first in range(0, 8, 2):
        patches = [
            jnp.concatenate(
                [
                    s_ref[e, pl.ds(2 * i + a, 96, stride=16), :].astype(jnp.bfloat16)
                    for a in range(2)
                    for e in range(2)
                ],
                axis=0,
            )
            for i in (first, first + 1)
        ]
        both = dot(w_ref[...], jnp.concatenate(patches, axis=1))
        grads = []
        for i in range(2):
            block = both[:, i * LANES : (i + 1) * LANES]
            down = jnp.where(low, block[:96], block[96:]).astype(jnp.bfloat16)
            normed, scale = standardize(down.astype(jnp.float32))
            rows = pl.ds(first + i, 96, stride=8)
            n_ref[rows, :] = normed * gain_ref[...]
            upstream = back_ref[rows, :] * gain_ref[...]
            step = upstream - fold(upstream) / 192.0 - normed * (fold(upstream * normed) / 192.0)
            total = grad_ref[rows, :] + scale * step
            total = total.astype(jnp.bfloat16).astype(jnp.float32)
            grads.append((total, pltpu.roll(total, LANES // 2, 1)))
        even = jnp.where(low, grads[0][0], grads[1][1])
        odd = jnp.where(low, grads[0][1], grads[1][0])
        both = jnp.concatenate([even, odd], axis=0).astype(jnp.bfloat16)
        patches = dot(wt_ref[...], both).astype(jnp.bfloat16)
        rows = [
            jnp.concatenate(
                [patches[(2 * a + e) * 96 : (2 * a + e + 1) * 96] for e in range(2)], axis=1
            )
            for a in range(2)
        ]
        merged = dot(jnp.concatenate(rows, axis=0), merge_at)
        for i in range(2):
            for a in range(2):
                o_ref[pl.ds(2 * (first + i) + a, 96, stride=16), :] = merged[
                    a * 96 : (a + 1) * 96, i * LANES : (i + 1) * LANES
                ]
    out_ref[:, : GROUPS * 16, :] = (
        o_ref[...].reshape(ROWS, GROUPS * 16, LANES).astype(jnp.bfloat16)
    )
    out_ref[:, GROUPS * 16 :, :] = (
        n_ref[...].reshape(ROWS, GROUPS * 8, LANES).astype(jnp.bfloat16)
    )


def token_step(images, back, grad_out, weight, gains):
    return pl.pallas_call(
        token_kernel,
        out_shape=jax.ShapeDtypeStruct((ROWS, GROUPS * 24, LANES), jnp.bfloat16),
        in_specs=hbm(1) + vmem(1) + hbm(3) + vmem(1),
        scratch_shapes=[
            pltpu.VMEM((96, 16, LANES), jnp.bfloat16),
            pltpu.VMEM((192, 8, 64), jnp.bfloat16),
            pltpu.VMEM((192, 384), jnp.bfloat16),
            pltpu.VMEM((384, 192), jnp.bfloat16),
            pltpu.VMEM((2, 1536, LANES), jnp.float32),
            pltpu.VMEM((768, LANES), jnp.float32),
            pltpu.VMEM((768, LANES), jnp.float32),
            pltpu.VMEM((768, LANES), jnp.float32),
            pltpu.VMEM((1536, LANES), jnp.float32),
            pltpu.SemaphoreType.DMA((4,)),
        ],
        name="token_step",
        **params(8 * 2 * 192 * 384 * 256, 4 << 20),
    )(images, back, grad_out, weight, weight.T, gains)


def unpack_first(blocks):
    return blocks.reshape(1, 96, 16, LANES)


def pack_second(field):
    pairs = field.reshape(96, 2, 8, 64).transpose(0, 2, 1, 3)
    return pairs.reshape(ROWS, GROUPS * 8, LANES)


def exchange(blocks, axis):
    return lax.all_to_all(blocks, axis, split_axis=0, concat_axis=0, tiled=True)


def shards(images, gain_first, filter_first, reduce_weight, gain_second, filter_second, grad_out):
    col = lax.axis_index("col")
    place = jnp.stack([col, lax.axis_index("rep")]).astype(jnp.int32)
    pixels = images.reshape(96, 16, LANES)
    upstream = grad_out.reshape(192, 8, 64)
    weight = reduce_weight.reshape(96, 2, 384).transpose(1, 0, 2).reshape(192, 384)
    gains = jnp.repeat(gain_second.reshape(96, 2), 64, axis=1)

    sent, zero = send_filters(place, filter_first, filter_second)
    swapped = swap_filters(sent, zero)
    kept = keep_filters(place, filter_first, filter_second)
    both = exchange(first_norm(pixels, upstream, gain_first), "row")
    half = forward_rows(both, (H1, H2))
    half, swapped = lax.optimization_barrier((half, swapped))
    recv = patch_filters(*swapped, col)
    both = exchange(half, "col")
    mixed = exchange(mix_first(place, both, kept, recv), "col")
    mixed = exchange(inverse_rows(mixed, (H1, H2)), "row")
    tokens = token_step(pixels, mixed, upstream, weight, gains)
    later = exchange(forward_rows(exchange(tokens, "row"), (H1, H2)), "col")
    dspec_one, terms = mix_last(place, both, later, kept, recv)
    terms = summed(terms)
    rot_one = exchange(dspec_one, "col")
    rot_one, terms = lax.optimization_barrier((rot_one, terms))
    swapped = swap_grads(terms[FILTER_ROWS:])
    grad_norm_one = unpack_first(exchange(inverse_rows(rot_one, (H1,)), "row"))
    grad_images = (
        unpack_first(tokens[:, : GROUPS * 16]).astype(jnp.float32)
        + norm_pullback_step(images.astype(jnp.float32), gain_first, grad_norm_one)
    ).astype(jnp.bfloat16)
    grad_first, grad_second = place_grads(place, terms[:FILTER_ROWS], swapped, col)
    return (grad_images, grad_first, grad_second)


def solution(mesh):
    placed = (
        P("rep", None, "row", "col"),
        P(),
        P(None, "row", "col", None),
        P(),
        P(),
        P(None, "row", "col", None),
        P("rep", None, "row", "col"),
    )
    return jax.shard_map(
        shards,
        mesh=mesh,
        in_specs=placed,
        out_specs=(
            P("rep", None, "row", "col"),
            P(None, "row", "col", "rep"),
            P(None, "row", "col", "rep"),
        ),
        check_vma=False,
    )
```

```python
import functools
import math

import jax
import jax.numpy as jnp
import numpy as np
from jax import lax
from jax.experimental import pallas as pl
from jax.experimental.pallas import tpu as pltpu
from jax.sharding import PartitionSpec as P

H1 = 512
H2 = 256
GROUPS = 3
COLS = 4
ROWS = 32
LANES = 128
SECOND_SLOT = 2 * GROUPS * H1 // 8
FILTER_ROWS = 2 * GROUPS * (H1 + H2) // 8

epsilon = 1e-06

ORDER = (0, 2, 3, 1)
SWAP = ((0, 3), (3, 0), (1, 2), (2, 1))


def cos_sin(n):
    index = np.arange(n)
    angles = (index[:, None] * index[None, :] % n) * (2.0 * math.pi / n)
    factor = 1.0 / math.sqrt(n)
    return np.cos(angles) * factor, np.sin(angles) * factor


def row_table(n):
    cos, sin = cos_sin(n)
    slots = n // 8
    parts = []
    for c in range(COLS):
        k = ORDER[c] * slots + np.arange(slots)
        real, imag = cos[k], -sin[k]
        if c == 0:
            imag[0] = cos[n // 2]
        parts += [real, imag]
    return np.concatenate(parts, axis=0)


def col_tables(n):
    cos, sin = cos_sin(n)
    pair = 512 // n
    width = LANES // pair
    if pair == 1:
        return cos, sin
    out = []
    for table in (cos, sin):
        blocks = table.reshape(COLS, width, COLS, width)
        full = np.zeros((COLS, pair, width, COLS, pair, width))
        for p in range(pair):
            full[:, p, :, :, p, :] = blocks
        out.append(full.reshape(512, 512))
    return tuple(out)


def constant(values):
    return jnp.asarray(np.asarray(values, np.float32).astype(jnp.bfloat16))


def dot(a, b):
    return jnp.dot(a, b, preferred_element_type=jnp.float32)


def params(flops, traffic, vmem_mib=40):
    return dict(
        compiler_params=pltpu.CompilerParams(vmem_limit_bytes=vmem_mib * 1024 * 1024),
        cost_estimate=pl.CostEstimate(flops=flops, bytes_accessed=traffic, transcendentals=0),
    )


def gather_rows(block, rows):
    parts = []
    for g in range(GROUPS):
        part = block[:, g * rows : (g + 1) * rows, :]
        if rows % 16:
            part = part.astype(jnp.float32)
        parts.append(part.reshape(ROWS * rows, LANES).astype(jnp.bfloat16))
    return jnp.concatenate(parts, axis=1)


def forward_rows_kernel(layout, *refs):
    x_ref, tables, out_ref = refs[0], refs[1:-1], refs[-1]
    for (n, first_in, first_out), table in zip(layout, tables):
        rows = n // ROWS
        slots = n // 8
        block = x_ref[:, first_in : first_in + GROUPS * rows, :]
        half = dot(table[...], gather_rows(block, rows)).astype(jnp.bfloat16)
        half = half.reshape(COLS, 2, slots, GROUPS * LANES)
        for part in range(2):
            for g in range(GROUPS):
                at = first_out + (part * GROUPS + g) * slots
                out_ref[:, at : at + slots, :] = half[:, part, :, g * LANES : (g + 1) * LANES]


def forward_rows(entries, sizes):
    layout, _, slots = layout_of(sizes)
    flops = sum(2 * n * n * GROUPS * LANES for n in sizes)
    return pl.pallas_call(
        functools.partial(forward_rows_kernel, layout),
        out_shape=jax.ShapeDtypeStruct((COLS, slots, LANES), jnp.bfloat16),
        name="forward_rows_" + "_".join(str(n) for n in sizes),
        **params(flops, 2 << 20),
    )(entries, *[constant(row_table(n)) for n in sizes])


def inverse_rows_kernel(layout, *refs):
    x_ref, tables, out_ref = refs[0], refs[1:-1], refs[-1]
    for (n, first_out, first_in), table in zip(layout, tables):
        rows = n // ROWS
        slots = n // 8
        parts = []
        for g in range(GROUPS):
            both = []
            for part in range(2):
                at = first_in + (part * GROUPS + g) * slots
                both.append(x_ref[:, at : at + slots, :].reshape(COLS, 1, slots, LANES))
            parts.append(jnp.concatenate(both, axis=1).reshape(n, LANES))
        result = dot(table[...], jnp.concatenate(parts, axis=1))
        pieces = [
            result[:, g * LANES : (g + 1) * LANES].reshape(ROWS, rows, LANES)
            for g in range(GROUPS)
        ]
        out_ref[:, first_out : first_out + GROUPS * rows, :] = jnp.concatenate(
            pieces, axis=1
        ).astype(jnp.bfloat16)


def layout_of(sizes):
    layout, first_token, first_slot = [], 0, 0
    for n in sizes:
        layout.append((n, first_token, first_slot))
        first_token += GROUPS * n // ROWS
        first_slot += 2 * GROUPS * n // 8
    return tuple(layout), first_token, first_slot


def inverse_rows(entries, sizes):
    layout, tokens, _ = layout_of(sizes)
    flops = sum(2 * n * n * GROUPS * LANES for n in sizes)
    return pl.pallas_call(
        functools.partial(inverse_rows_kernel, layout),
        out_shape=jax.ShapeDtypeStruct((ROWS, tokens, LANES), jnp.bfloat16),
        name="inverse_rows_" + "_".join(str(n) for n in sizes),
        **params(flops, 2 << 20),
    )(entries, *[constant(row_table(n).T) for n in sizes])


def wide(ref, first, count):
    return jnp.concatenate([ref[q, first : first + count, :] for q in range(COLS)], axis=1)


def spectrum(ref, first, slots, special, cos, sin):
    count = GROUPS * slots
    real, imag = wide(ref, first, count), wide(ref, first + count, count)
    real_cos, real_sin = dot(real, cos), dot(real, sin)
    imag_cos, imag_sin = dot(imag, cos), dot(imag, sin)
    return (
        jnp.where(special, real_cos, real_cos + imag_sin),
        jnp.where(special, -real_sin, imag_cos - real_sin),
        jnp.where(special, imag_cos, real_cos - imag_sin),
        jnp.where(special, -imag_sin, -imag_cos - real_sin),
    )


def filters(near, kept_ref, recv_ref, first, slots):
    count = GROUPS * slots
    out = []
    for part in range(2):
        kept = wide(kept_ref, first + part * count, count).astype(jnp.float32)
        recv = wide(recv_ref, first + part * count, count).astype(jnp.float32)
        out.append((jnp.where(near, kept, recv), jnp.where(near, recv, kept)))
    return out


def put_inverse(out_ref, first, slots, special, up, down, cos, sin):
    count = GROUPS * slots
    (up_r, up_i), (down_r, down_i) = up, down
    bf16 = jnp.bfloat16
    sum_r = jnp.where(special, up_r, up_r + down_r).astype(bf16)
    sum_i = jnp.where(special, up_i, up_i + down_i).astype(bf16)
    dif_i = jnp.where(special, down_r, up_i - down_i).astype(bf16)
    dif_r = jnp.where(special, -down_i, up_r - down_r).astype(bf16)
    rot_real = (dot(sum_r, cos) - dot(sum_i, sin)).astype(bf16)
    rot_imag = (dot(dif_i, cos) + dot(dif_r, sin)).astype(bf16)
    for q in range(COLS):
        lanes = slice(q * LANES, (q + 1) * LANES)
        out_ref[q, first : first + count, :] = rot_real[:, lanes]
        out_ref[q, first + count : first + 2 * count, :] = rot_imag[:, lanes]


def masks(place_ref, slots):
    col = place_ref[0]
    row = lax.broadcasted_iota(jnp.int32, (GROUPS * slots, 512), 0)
    return (lax.rem(row, slots) + col * slots) == 0, col < 2


def apply_back(real, imag, grad):
    return [
        (
            real[side] * grad[2 * side] + imag[side] * grad[2 * side + 1],
            real[side] * grad[2 * side + 1] - imag[side] * grad[2 * side],
        )
        for side in range(2)
    ]


def mix_first_kernel(place_ref, x_ref, kept_ref, recv_ref, first_tables, second_tables, out_ref):
    slots = H1 // 8
    special, near = masks(place_ref, slots)
    cos, sin = first_tables[0], first_tables[1]
    up_r, up_i, down_r, down_i = spectrum(x_ref, 0, slots, special, cos, sin)
    real, imag = filters(near, kept_ref, recv_ref, 0, slots)
    up = (real[0] * up_r - imag[0] * up_i, real[0] * up_i + imag[0] * up_r)
    down = (real[1] * down_r - imag[1] * down_i, real[1] * down_i + imag[1] * down_r)
    put_inverse(out_ref, 0, slots, special, up, down, cos, sin)

    first, slots = SECOND_SLOT, H2 // 8
    special, near = masks(place_ref, slots)
    cos, sin = second_tables[0], second_tables[1]
    grad = spectrum(x_ref, first, slots, special, cos, sin)
    real, imag = filters(near, kept_ref, recv_ref, first, slots)
    up, down = apply_back(real, imag, grad)
    put_inverse(out_ref, first, slots, special, up, down, cos, sin)


def put_terms(out_ref, first, slots, near, field, grad):
    count = GROUPS * slots
    terms = []
    for side in range(2):
        g_r, g_i = grad[2 * side], grad[2 * side + 1]
        s_r, s_i = field[2 * side], field[2 * side + 1]
        terms.append((g_r * s_r + g_i * s_i, g_i * s_r - g_r * s_i))
    for part in range(2):
        up, down = terms[0][part], terms[1][part]
        kept = jnp.where(near, up, down).astype(jnp.bfloat16)
        sent = jnp.where(near, down, up).astype(jnp.bfloat16)
        at = first + part * count
        for q in range(COLS):
            lanes = slice(q * LANES, (q + 1) * LANES)
            out_ref[q, at : at + count, :] = kept[:, lanes]
            out_ref[q, FILTER_ROWS + at : FILTER_ROWS + at + count, :] = sent[:, lanes]


def mix_last_kernel(
    place_ref, x_ref, y_ref, kept_ref, recv_ref, first_tables, second_tables,
    out_ref, total_ref, terms_ref, sem,
):
    slots = H2 // 8
    special, near = masks(place_ref, slots)
    tables = second_tables[0], second_tables[1]
    grad = spectrum(x_ref, SECOND_SLOT, slots, special, *tables)
    field = spectrum(y_ref, SECOND_SLOT, slots, special, *tables)
    put_terms(terms_ref, SECOND_SLOT, slots, near, field, grad)
    slots = H1 // 8
    special, near = masks(place_ref, slots)
    tables = first_tables[0], first_tables[1]
    field = spectrum(x_ref, 0, slots, special, *tables)
    grad = spectrum(y_ref, 0, slots, special, *tables)
    put_terms(terms_ref, 0, slots, near, field, grad)
    copy = pltpu.make_async_copy(terms_ref, total_ref, sem)
    copy.start()
    real, imag = filters(near, kept_ref, recv_ref, 0, slots)
    up, down = apply_back(real, imag, grad)
    put_inverse(out_ref, 0, slots, special, up, down, *tables)
    copy.wait()


def smem():
    return pl.BlockSpec(memory_space=pltpu.SMEM)


def hbm(count):
    return [pl.BlockSpec(memory_space=pltpu.HBM)] * count


def vmem(count):
    return [pl.BlockSpec()] * count


def both_tables():
    return [constant(np.stack(col_tables(n))) for n in (H1, H2)]


def mix_first(place, entries, kept, recv):
    return pl.pallas_call(
        mix_first_kernel,
        out_shape=jax.ShapeDtypeStruct((COLS, FILTER_ROWS, LANES), jnp.bfloat16),
        in_specs=[smem()] + vmem(5),
        name="mix_first",
        **params(8 * FILTER_ROWS * 512 * 512, 6 << 20),
    )(place, entries, kept, recv, *both_tables())


def mix_last(place, entries, later, kept, recv):
    total = (COLS, 2 * FILTER_ROWS, LANES)
    return pl.pallas_call(
        mix_last_kernel,
        out_shape=(
            jax.ShapeDtypeStruct((COLS, SECOND_SLOT, LANES), jnp.bfloat16),
            jax.ShapeDtypeStruct(total, jnp.bfloat16),
        ),
        in_specs=[smem()] + vmem(6),
        out_specs=tuple(vmem(1) + hbm(1)),
        scratch_shapes=[pltpu.VMEM(total, jnp.bfloat16), pltpu.SemaphoreType.DMA],
        name="mix_last",
        **params(12 * FILTER_ROWS * 512 * 512, 8 << 20),
    )(place, entries, later, kept, recv, *both_tables())


def grid_of(rows, columns):
    shape = (rows, columns)
    return lax.broadcasted_iota(jnp.int32, shape, 0), lax.broadcasted_iota(jnp.int32, shape, 1)


def ones_at(mask):
    return jnp.where(mask, 1.0, 0.0).astype(jnp.bfloat16)


def kept_rows(near, slots):
    slot, local = grid_of(slots, 2 * slots)
    return ones_at(local == jnp.where(near, slot, slots - slot))


def sent_rows(near, slots):
    slot, local = grid_of(slots, 2 * slots)
    return ones_at(local == jnp.where(near, slots + slot, lax.rem(2 * slots - slot, 2 * slots)))


def quarter_lanes(quarter):
    wide_at, narrow_at = grid_of(512, LANES)
    return ones_at(
        wide_at == lax.div(narrow_at, 64) * 256 + 64 * quarter + lax.rem(narrow_at, 64)
    )


def second_pair(ref, part, g):
    pair = [ref[part, 2 * g + i].astype(jnp.bfloat16) for i in range(2)]
    return jnp.concatenate(pair, axis=1)


def send_filters_kernel(
    place_ref, first_ref, second_ref, sent_ref, zero_ref, first_buf, second_buf, sems
):
    quarter = place_ref[1]
    at = pl.ds(pl.multiple_of(quarter * LANES, LANES), LANES)
    first_copy = pltpu.make_async_copy(first_ref.at[:, :, :, at], first_buf, sems.at[0])
    second_copy = pltpu.make_async_copy(second_ref, second_buf, sems.at[1])
    first_copy.start()
    second_copy.start()
    near = place_ref[0] < 2
    zeros = []
    for n in (H1, H2):
        slots = n // 8
        first = 0 if n == H1 else 2 * GROUPS * H1 // 8
        pick = sent_rows(near, slots)
        if n == H1:
            first_copy.wait()
        else:
            second_copy.wait()
            lanes = quarter_lanes(quarter)
        for part in range(2):
            for g in range(GROUPS):
                if n == H1:
                    rows = first_buf[part, g].astype(jnp.bfloat16)
                else:
                    rows = dot(second_pair(second_buf, part, g), lanes).astype(jnp.bfloat16)
                rows = dot(pick, rows)
                zeros.append(rows[:1])
                sent_ref[first : first + slots, :] = rows.astype(jnp.bfloat16)
                first += slots
    zeros.append(jnp.zeros((4, LANES), jnp.float32))
    zero_ref[...] = jnp.concatenate(zeros, axis=0).astype(jnp.bfloat16)


def keep_filters_kernel(place_ref, first_ref, second_ref, kept_ref):
    near = place_ref[0] < 2
    first = 0
    lanes = [quarter_lanes(q) for q in range(COLS)]
    for n in (H1, H2):
        slots = n // 8
        pick = kept_rows(near, slots)
        for part in range(2):
            for g in range(GROUPS):
                if n == H1:
                    rows = first_ref[part, g].astype(jnp.bfloat16)
                else:
                    rows = second_pair(second_ref, part, g)
                rows = dot(pick, rows).astype(jnp.bfloat16)
                for q in range(COLS):
                    if n == H1:
                        cut = rows[:, q * LANES : (q + 1) * LANES]
                    else:
                        cut = dot(rows, lanes[q]).astype(jnp.bfloat16)
                    kept_ref[q, first : first + slots, :] = cut
                first += slots


def send_filters(place, filter_first, filter_second):
    return pl.pallas_call(
        send_filters_kernel,
        out_shape=(
            jax.ShapeDtypeStruct((FILTER_ROWS, LANES), jnp.bfloat16),
            jax.ShapeDtypeStruct((16, LANES), jnp.bfloat16),
        ),
        in_specs=[smem()] + hbm(2),
        scratch_shapes=[
            pltpu.VMEM((2, GROUPS, H1 // 4, LANES), jnp.float32),
            pltpu.VMEM((2, 2 * GROUPS, H2 // 4, H2), jnp.float32),
            pltpu.SemaphoreType.DMA((2,)),
        ],
        name="send_filters",
        **params(12 * 64 * 512 * 128 * 2, 2 << 20, 60),
    )(place, filter_first, filter_second)


def keep_filters(place, filter_first, filter_second):
    return pl.pallas_call(
        keep_filters_kernel,
        out_shape=jax.ShapeDtypeStruct((COLS, FILTER_ROWS, LANES), jnp.bfloat16),
        in_specs=[smem()] + vmem(2),
        name="keep_filters",
        **params(12 * 64 * 512 * 512 * 2, 4 << 20),
    )(place, filter_first, filter_second)


def put_slot_zero(block, zero, take, slots):
    shaped = block.reshape(2 * GROUPS, slots, LANES)
    here = (jnp.arange(slots) == 0)[None, :, None] & take
    return jnp.where(here, zero[:, None, :], shaped).reshape(2 * GROUPS * slots, LANES)


def put_slots_zero(block, zero, take):
    split, groups = 2 * GROUPS * H1 // 8, 2 * GROUPS
    return (
        put_slot_zero(block[:split], zero[:groups], take, H1 // 8),
        put_slot_zero(block[split:], zero[groups : 2 * groups], take, H2 // 8),
    )


def swap_filters(sent, zero):
    return lax.ppermute(sent, "col", SWAP), lax.ppermute(zero, "col", ((2, 0), (3, 1)))


def patch_filters(recv, zero, col):
    recv = jnp.concatenate(put_slots_zero(recv, zero, col < 2), axis=0)
    return lax.all_gather(recv, "rep", axis=0, tiled=False)


def place_grads_kernel(
    place_ref, kept_first, recv_first, kept_second, recv_second, first_ref, second_ref
):
    near = place_ref[0] < 2
    wide_at, narrow_at = grid_of(LANES, LANES // 2)
    lanes = [ones_at(wide_at == narrow_at + 64 * i) for i in range(2)]
    for n, kept, recv in ((H1, kept_first, recv_first), (H2, kept_second, recv_second)):
        slots = n // 8
        local, slot = grid_of(2 * slots, slots)
        mirror = lax.rem(2 * slots - slot, 2 * slots)
        pick_kept = ones_at(local == jnp.where(near, slot, slots - slot))
        pick_recv = ones_at(local == jnp.where(near, slots + slot, mirror))
        for part in range(2):
            for g in range(GROUPS):
                at = (part * GROUPS + g) * slots
                rows = dot(pick_kept, kept[at : at + slots]) + dot(
                    pick_recv, recv[at : at + slots]
                )
                if n == H1:
                    first_ref[part, g] = rows
                else:
                    rows = rows.astype(jnp.bfloat16)
                    for i in range(2):
                        second_ref[part, 2 * g + i] = dot(rows, lanes[i])


def summed(terms):
    return lax.psum_scatter(terms, "rep", scatter_dimension=0, tiled=False)


def swap_grads(sent):
    groups = 2 * GROUPS
    zero = jnp.concatenate(
        [
            sent[:SECOND_SLOT].reshape(groups, H1 // 8, LANES)[:, 0],
            sent[SECOND_SLOT:].reshape(groups, H2 // 8, LANES)[:, 0],
            jnp.zeros((4, LANES), jnp.bfloat16),
        ],
        axis=0,
    )
    return lax.ppermute(sent, "col", SWAP), lax.ppermute(zero, "col", ((0, 2), (1, 3)))


def place_grads(place, kept, swapped, col):
    recv_first, recv_second = put_slots_zero(*swapped, col >= 2)
    return pl.pallas_call(
        place_grads_kernel,
        out_shape=(
            jax.ShapeDtypeStruct((2, GROUPS, H1 // 4, LANES), jnp.float32),
            jax.ShapeDtypeStruct((2, 2 * GROUPS, H2 // 4, LANES // 2), jnp.float32),
        ),
        in_specs=[smem()] + vmem(4),
        name="place_grads",
        **params(12 * 128 * 128 * 128 * 2, 2 << 20),
    )(place, kept[:SECOND_SLOT], recv_first, kept[SECOND_SLOT:], recv_second)


def layer_normalize(entry_values, gains):
    center = entry_values - jnp.mean(entry_values, axis=1, keepdims=True)
    spread = jnp.mean(center * center, axis=1, keepdims=True)
    return center * lax.rsqrt(spread + epsilon) * gains[None, :, None, None]


def norm_pullback_step(entry_values, gains, upstream):
    _, pullback = jax.vjp(lambda inner_vals: layer_normalize(inner_vals, gains), entry_values)
    return pullback(upstream.astype(jnp.float32))[0]


def fold(values):
    total = jnp.broadcast_to(jnp.sum(values, axis=0, keepdims=True), (8, LANES))
    return (total + pltpu.roll(total, LANES // 2, 1))[:1]


def standardize(values):
    center = values - fold(values) / 192.0
    scale = lax.rsqrt(fold(center * center) / 192.0 + epsilon)
    return center * scale, scale


def pack_pairs(block):
    at, lane = grid_of(LANES, 192)
    mine = lax.rem(lane, 2) == lax.div(at, 64)
    fields = []
    for i in range(8):
        field = block[i].astype(jnp.float32)
        fields.append(jnp.where(mine, jnp.concatenate([field, field], axis=0), 0.0))
    at, lane = grid_of(96, 192)
    return lax.dot_general(
        ones_at(lax.div(lane, 2) == at),
        jnp.concatenate(fields, axis=0).astype(jnp.bfloat16),
        (((1,), (1,)), ((), ())),
        preferred_element_type=jnp.float32,
    )


def first_norm_kernel(
    x_ref, g_ref, gain_ref, out_ref, x_buf, g_buf, gain_buf, pack_buf, sems
):
    copies = [
        pltpu.make_async_copy(source, target, sems.at[i])
        for i, (source, target) in enumerate(
            ((x_ref, x_buf), (gain_ref, gain_buf), (g_ref, g_buf))
        )
    ]
    for copy in copies:
        copy.start()
    copies[0].wait()
    copies[1].wait()
    pixels = x_buf[...].astype(jnp.float32)
    center = pixels - jnp.sum(pixels, axis=0, keepdims=True) / 96.0
    scale = lax.rsqrt(jnp.sum(center * center, axis=0) / 96.0 + epsilon)
    for c in range(96):
        at = (c % GROUPS) * 16
        out_ref[c // GROUPS, at : at + 16, :] = (center[c] * scale * gain_buf[c]).astype(
            jnp.bfloat16
        )
    copies[2].wait()
    packed = pack_pairs(g_buf[...])
    for i in range(8):
        pack_buf[pl.ds(i, 96, stride=8), :] = packed[:, i * LANES : (i + 1) * LANES]
    packed = pack_buf[...].reshape(ROWS, GROUPS * 8, LANES)
    out_ref[:, GROUPS * 16 :, :] = packed.astype(jnp.bfloat16)


def first_norm(images, grad_out, gains):
    return pl.pallas_call(
        first_norm_kernel,
        out_shape=jax.ShapeDtypeStruct((ROWS, GROUPS * 24, LANES), jnp.bfloat16),
        in_specs=hbm(3),
        scratch_shapes=[
            pltpu.VMEM((96, 16, LANES), jnp.bfloat16),
            pltpu.VMEM((8, 64, 192), jnp.bfloat16),
            pltpu.SMEM((96,), jnp.float32),
            pltpu.VMEM((768, LANES), jnp.float32),
            pltpu.SemaphoreType.DMA((3,)),
        ],
        name="first_norm",
        **params(4 * 768 * 64 * 128, 2 << 20, 60),
    )(images, grad_out, gains)


def low_half():
    return lax.broadcasted_iota(jnp.int32, (96, LANES), 1) < LANES // 2


def token_kernel(
    x_hbm, m_ref, g_hbm, w_hbm, wt_hbm, gain_ref, out_ref,
    x_ref, g_ref, w_ref, wt_ref, s_ref, n_ref, back_ref, o_ref, sems,
):
    copies = [
        pltpu.make_async_copy(source, target, sems.at[i])
        for i, (source, target) in enumerate(
            ((x_hbm, x_ref), (w_hbm, w_ref), (g_hbm, g_ref), (wt_hbm, wt_ref))
        )
    ]
    for copy in copies:
        copy.start()
    at, lane = grid_of(LANES, 2 * LANES)
    spread_at = ones_at(at == 2 * lax.rem(lane, 64) + lax.div(lane, LANES))
    at, lane = grid_of(2 * LANES, 2 * LANES)
    here = LANES * lax.rem(lax.div(at, 64), 2) + 2 * lax.rem(at, 64) + lax.div(at, LANES)
    merge_at = ones_at(lane == here)
    mixed = m_ref[:, : GROUPS * 16, :].astype(jnp.float32).reshape(1536, LANES)
    back_ref[...] = m_ref[:, GROUPS * 16 :, :].astype(jnp.float32).reshape(768, LANES)
    copies[0].wait()
    section = x_ref[...].astype(jnp.float32).reshape(1536, LANES) + mixed
    spread = dot(section.astype(jnp.bfloat16), spread_at)
    for e in range(2):
        s_ref[e] = spread[:, e * LANES : (e + 1) * LANES]
    low = low_half()
    for copy in copies[1:]:
        copy.wait()
    packed = pack_pairs(g_ref[...])
    for first in range(0, 8, 2):
        patches = [
            jnp.concatenate(
                [
                    s_ref[e, pl.ds(2 * i + a, 96, stride=16), :].astype(jnp.bfloat16)
                    for a in range(2)
                    for e in range(2)
                ],
                axis=0,
            )
            for i in (first, first + 1)
        ]
        both = dot(w_ref[...], jnp.concatenate(patches, axis=1))
        grads = []
        for i in range(2):
            block = both[:, i * LANES : (i + 1) * LANES]
            down = jnp.where(low, block[:96], block[96:]).astype(jnp.bfloat16)
            normed, scale = standardize(down.astype(jnp.float32))
            rows = pl.ds(first + i, 96, stride=8)
            n_ref[rows, :] = normed * gain_ref[...]
            upstream = back_ref[rows, :] * gain_ref[...]
            step = upstream - fold(upstream) / 192.0 - normed * (fold(upstream * normed) / 192.0)
            at = (first + i) * LANES
            total = packed[:, at : at + LANES] + scale * step
            total = total.astype(jnp.bfloat16).astype(jnp.float32)
            grads.append((total, pltpu.roll(total, LANES // 2, 1)))
        even = jnp.where(low, grads[0][0], grads[1][1])
        odd = jnp.where(low, grads[0][1], grads[1][0])
        both = jnp.concatenate([even, odd], axis=0).astype(jnp.bfloat16)
        patches = dot(wt_ref[...], both).astype(jnp.bfloat16)
        rows = [
            jnp.concatenate(
                [patches[(2 * a + e) * 96 : (2 * a + e + 1) * 96] for e in range(2)], axis=1
            )
            for a in range(2)
        ]
        merged = dot(jnp.concatenate(rows, axis=0), merge_at)
        for i in range(2):
            for a in range(2):
                o_ref[pl.ds(2 * (first + i) + a, 96, stride=16), :] = merged[
                    a * 96 : (a + 1) * 96, i * LANES : (i + 1) * LANES
                ]
    out_ref[:, : GROUPS * 16, :] = (
        o_ref[...].reshape(ROWS, GROUPS * 16, LANES).astype(jnp.bfloat16)
    )
    out_ref[:, GROUPS * 16 :, :] = (
        n_ref[...].reshape(ROWS, GROUPS * 8, LANES).astype(jnp.bfloat16)
    )


def token_step(images, back, grad_out, weight, gains):
    return pl.pallas_call(
        token_kernel,
        out_shape=jax.ShapeDtypeStruct((ROWS, GROUPS * 24, LANES), jnp.bfloat16),
        in_specs=hbm(1) + vmem(1) + hbm(3) + vmem(1),
        scratch_shapes=[
            pltpu.VMEM((96, 16, LANES), jnp.bfloat16),
            pltpu.VMEM((8, 64, 192), jnp.bfloat16),
            pltpu.VMEM((192, 384), jnp.bfloat16),
            pltpu.VMEM((384, 192), jnp.bfloat16),
            pltpu.VMEM((2, 1536, LANES), jnp.float32),
            pltpu.VMEM((768, LANES), jnp.float32),
            pltpu.VMEM((768, LANES), jnp.float32),
            pltpu.VMEM((1536, LANES), jnp.float32),
            pltpu.SemaphoreType.DMA((4,)),
        ],
        name="token_step",
        **params(8 * 2 * 192 * 384 * 256, 4 << 20),
    )(images, back, grad_out, weight, weight.T, gains)


def unpack_first(blocks):
    return blocks.reshape(1, 96, 16, LANES)


def pack_second(field):
    pairs = field.reshape(96, 2, 8, 64).transpose(0, 2, 1, 3)
    return pairs.reshape(ROWS, GROUPS * 8, LANES)


def exchange(blocks, axis):
    return lax.all_to_all(blocks, axis, split_axis=0, concat_axis=0, tiled=True)


def shards(images, gain_first, filter_first, reduce_weight, gain_second, filter_second, grad_out):
    col = lax.axis_index("col")
    place = jnp.stack([col, lax.axis_index("rep")]).astype(jnp.int32)
    pixels = images.reshape(96, 16, LANES)
    upstream = grad_out.transpose(0, 2, 3, 1).reshape(8, 64, 192)
    weight = reduce_weight.reshape(96, 2, 384).transpose(1, 0, 2).reshape(192, 384)
    gains = jnp.repeat(gain_second.reshape(96, 2), 64, axis=1)

    sent, zero = send_filters(place, filter_first, filter_second)
    swapped = swap_filters(sent, zero)
    kept = keep_filters(place, filter_first, filter_second)
    both = exchange(first_norm(pixels, upstream, gain_first), "row")
    half = forward_rows(both, (H1, H2))
    half, swapped = lax.optimization_barrier((half, swapped))
    recv = patch_filters(*swapped, col)
    both = exchange(half, "col")
    mixed = exchange(mix_first(place, both, kept, recv), "col")
    mixed = exchange(inverse_rows(mixed, (H1, H2)), "row")
    tokens = token_step(pixels, mixed, upstream, weight, gains)
    later = exchange(forward_rows(exchange(tokens, "row"), (H1, H2)), "col")
    dspec_one, terms = mix_last(place, both, later, kept, recv)
    terms = summed(terms)
    rot_one = exchange(dspec_one, "col")
    rot_one, terms = lax.optimization_barrier((rot_one, terms))
    swapped = swap_grads(terms[FILTER_ROWS:])
    grad_norm_one = unpack_first(exchange(inverse_rows(rot_one, (H1,)), "row"))
    grad_images = (
        unpack_first(tokens[:, : GROUPS * 16]).astype(jnp.float32)
        + norm_pullback_step(images.astype(jnp.float32), gain_first, grad_norm_one)
    ).astype(jnp.bfloat16)
    grad_first, grad_second = place_grads(place, terms[:FILTER_ROWS], swapped, col)
    return (grad_images, grad_first, grad_second)


def solution(mesh):
    placed = (
        P("rep", None, "row", "col"),
        P(),
        P(None, "row", "col", None),
        P(),
        P(),
        P(None, "row", "col", None),
        P("rep", None, "row", "col"),
    )
    return jax.shard_map(
        shards,
        mesh=mesh,
        in_specs=placed,
        out_specs=(
            P("rep", None, "row", "col"),
            P(None, "row", "col", "rep"),
            P(None, "row", "col", "rep"),
        ),
        check_vma=False,
    )
```

```python
import functools
import math

import jax
import jax.numpy as jnp
import numpy as np
from jax import lax
from jax.experimental import pallas as pl
from jax.experimental.pallas import tpu as pltpu
from jax.sharding import PartitionSpec as P

H1 = 512
H2 = 256
GROUPS = 3
COLS = 4
ROWS = 32
LANES = 128
SECOND_SLOT = 2 * GROUPS * H1 // 8
FILTER_ROWS = 2 * GROUPS * (H1 + H2) // 8
EDGE_ROWS = 16

epsilon = 1e-06

ORDER = (0, 2, 3, 1)
SWAP = ((0, 3), (3, 0), (1, 2), (2, 1))


def cos_sin(n):
    index = np.arange(n)
    angles = (index[:, None] * index[None, :] % n) * (2.0 * math.pi / n)
    factor = 1.0 / math.sqrt(n)
    return np.cos(angles) * factor, np.sin(angles) * factor


def row_table(n):
    cos, sin = cos_sin(n)
    slots = n // 8
    parts = []
    for c in range(COLS):
        k = ORDER[c] * slots + np.arange(slots)
        real, imag = cos[k], -sin[k]
        if c == 0:
            imag[0] = cos[n // 2]
        parts += [real, imag]
    return np.concatenate(parts, axis=0)


def edge_table(n):
    cos, sin = cos_sin(n)
    table = np.zeros((EDGE_ROWS, n))
    table[4] = cos[n // 2]
    table[6], table[7] = cos[n // 4], -sin[n // 4]
    return table


def col_tables(n):
    cos, sin = cos_sin(n)
    pair = 512 // n
    width = LANES // pair
    if pair == 1:
        return cos, sin
    out = []
    for table in (cos, sin):
        blocks = table.reshape(COLS, width, COLS, width)
        full = np.zeros((COLS, pair, width, COLS, pair, width))
        for p in range(pair):
            full[:, p, :, :, p, :] = blocks
        out.append(full.reshape(512, 512))
    return tuple(out)


def constant(values):
    return jnp.asarray(np.asarray(values, np.float32).astype(jnp.bfloat16))


def dot(a, b):
    return jnp.dot(a, b, preferred_element_type=jnp.float32)


def params(flops, traffic, vmem_mib=40):
    return dict(
        compiler_params=pltpu.CompilerParams(vmem_limit_bytes=vmem_mib * 1024 * 1024),
        cost_estimate=pl.CostEstimate(flops=flops, bytes_accessed=traffic, transcendentals=0),
    )


def gather_rows(block, rows):
    parts = []
    for g in range(GROUPS):
        part = block[:, g * rows : (g + 1) * rows, :]
        if rows % 16:
            part = part.astype(jnp.float32)
        parts.append(part.reshape(ROWS * rows, LANES).astype(jnp.bfloat16))
    return jnp.concatenate(parts, axis=1)


def forward_rows_kernel(layout, *refs):
    x_ref, tables, out_ref = refs[0], refs[1:-1], refs[-1]
    edges = []
    for i, (n, first_in, first_out) in enumerate(layout):
        rows = n // ROWS
        slots = n // 8
        block = x_ref[:, first_in : first_in + GROUPS * rows, :]
        gathered = gather_rows(block, rows)
        half = dot(tables[2 * i][...], gathered).astype(jnp.bfloat16)
        edges.append(dot(tables[2 * i + 1][...], gathered))
        half = half.reshape(COLS, 2, slots, GROUPS * LANES)
        for part in range(2):
            for g in range(GROUPS):
                at = first_out + (part * GROUPS + g) * slots
                out_ref[:, at : at + slots, :] = half[:, part, :, g * LANES : (g + 1) * LANES]
    for c in range(COLS):
        pieces = [
            edge[2 * c + part : 2 * c + part + 1, g * LANES : (g + 1) * LANES]
            for edge in edges
            for part in range(2)
            for g in range(GROUPS)
        ]
        pieces.append(jnp.zeros((EDGE_ROWS - len(pieces), LANES), jnp.float32))
        out_ref[c, FILTER_ROWS:, :] = jnp.concatenate(pieces, axis=0).astype(jnp.bfloat16)


def forward_rows(entries, sizes):
    layout, _, slots = layout_of(sizes)
    flops = sum(2 * n * n * GROUPS * LANES for n in sizes)
    return pl.pallas_call(
        functools.partial(forward_rows_kernel, layout),
        out_shape=jax.ShapeDtypeStruct((COLS, slots + EDGE_ROWS, LANES), jnp.bfloat16),
        name="forward_rows_" + "_".join(str(n) for n in sizes),
        **params(flops, 2 << 20),
    )(entries, *[constant(table(n)) for n in sizes for table in (row_table, edge_table)])


def inverse_rows_kernel(layout, *refs):
    x_ref, tables, out_ref = refs[0], refs[1:-1], refs[-1]
    for (n, first_out, first_in), table in zip(layout, tables):
        rows = n // ROWS
        slots = n // 8
        parts = []
        for g in range(GROUPS):
            both = []
            for part in range(2):
                at = first_in + (part * GROUPS + g) * slots
                both.append(x_ref[:, at : at + slots, :].reshape(COLS, 1, slots, LANES))
            parts.append(jnp.concatenate(both, axis=1).reshape(n, LANES))
        result = dot(table[...], jnp.concatenate(parts, axis=1))
        pieces = [
            result[:, g * LANES : (g + 1) * LANES].reshape(ROWS, rows, LANES)
            for g in range(GROUPS)
        ]
        out_ref[:, first_out : first_out + GROUPS * rows, :] = jnp.concatenate(
            pieces, axis=1
        ).astype(jnp.bfloat16)


def layout_of(sizes):
    layout, first_token, first_slot = [], 0, 0
    for n in sizes:
        layout.append((n, first_token, first_slot))
        first_token += GROUPS * n // ROWS
        first_slot += 2 * GROUPS * n // 8
    return tuple(layout), first_token, first_slot


def inverse_rows(entries, sizes):
    layout, tokens, _ = layout_of(sizes)
    flops = sum(2 * n * n * GROUPS * LANES for n in sizes)
    return pl.pallas_call(
        functools.partial(inverse_rows_kernel, layout),
        out_shape=jax.ShapeDtypeStruct((ROWS, tokens, LANES), jnp.bfloat16),
        name="inverse_rows_" + "_".join(str(n) for n in sizes),
        **params(flops, 2 << 20),
    )(entries, *[constant(row_table(n).T) for n in sizes])


def wide(ref, first, count):
    return jnp.concatenate([ref[q, first : first + count, :] for q in range(COLS)], axis=1)


def spectrum(ref, first, slots, special, cos, sin):
    count = GROUPS * slots
    real, imag = wide(ref, first, count), wide(ref, first + count, count)
    real_cos, real_sin = dot(real, cos), dot(real, sin)
    imag_cos, imag_sin = dot(imag, cos), dot(imag, sin)
    return (
        jnp.where(special, real_cos, real_cos + imag_sin),
        jnp.where(special, -real_sin, imag_cos - real_sin),
        jnp.where(special, imag_cos, real_cos - imag_sin),
        jnp.where(special, -imag_sin, -imag_cos - real_sin),
    )


def filters(near, kept_ref, recv_ref, first, slots):
    count = GROUPS * slots
    out = []
    for part in range(2):
        kept = wide(kept_ref, first + part * count, count).astype(jnp.float32)
        recv = wide(recv_ref, first + part * count, count).astype(jnp.float32)
        out.append((jnp.where(near, kept, recv), jnp.where(near, recv, kept)))
    return out


def put_inverse(out_ref, first, slots, special, up, down, cos, sin):
    count = GROUPS * slots
    (up_r, up_i), (down_r, down_i) = up, down
    bf16 = jnp.bfloat16
    sum_r = jnp.where(special, up_r, up_r + down_r).astype(bf16)
    sum_i = jnp.where(special, up_i, up_i + down_i).astype(bf16)
    dif_i = jnp.where(special, down_r, up_i - down_i).astype(bf16)
    dif_r = jnp.where(special, -down_i, up_r - down_r).astype(bf16)
    rot_real = (dot(sum_r, cos) - dot(sum_i, sin)).astype(bf16)
    rot_imag = (dot(dif_i, cos) + dot(dif_r, sin)).astype(bf16)
    for q in range(COLS):
        lanes = slice(q * LANES, (q + 1) * LANES)
        out_ref[q, first : first + count, :] = rot_real[:, lanes]
        out_ref[q, first + count : first + 2 * count, :] = rot_imag[:, lanes]


def masks(place_ref, slots):
    col = place_ref[0]
    row = lax.broadcasted_iota(jnp.int32, (GROUPS * slots, 512), 0)
    return (lax.rem(row, slots) + col * slots) == 0, col < 2


def apply_back(real, imag, grad):
    return [
        (
            real[side] * grad[2 * side] + imag[side] * grad[2 * side + 1],
            real[side] * grad[2 * side + 1] - imag[side] * grad[2 * side],
        )
        for side in range(2)
    ]


def mix_first_kernel(place_ref, x_ref, kept_ref, recv_ref, first_tables, second_tables, out_ref):
    slots = H1 // 8
    special, near = masks(place_ref, slots)
    cos, sin = first_tables[0], first_tables[1]
    up_r, up_i, down_r, down_i = spectrum(x_ref, 0, slots, special, cos, sin)
    real, imag = filters(near, kept_ref, recv_ref, 0, slots)
    up = (real[0] * up_r - imag[0] * up_i, real[0] * up_i + imag[0] * up_r)
    down = (real[1] * down_r - imag[1] * down_i, real[1] * down_i + imag[1] * down_r)
    put_inverse(out_ref, 0, slots, special, up, down, cos, sin)

    first, slots = SECOND_SLOT, H2 // 8
    special, near = masks(place_ref, slots)
    cos, sin = second_tables[0], second_tables[1]
    grad = spectrum(x_ref, first, slots, special, cos, sin)
    real, imag = filters(near, kept_ref, recv_ref, first, slots)
    up, down = apply_back(real, imag, grad)
    put_inverse(out_ref, first, slots, special, up, down, cos, sin)


def put_terms(out_ref, first, slots, near, field, grad):
    count = GROUPS * slots
    terms = []
    for side in range(2):
        g_r, g_i = grad[2 * side], grad[2 * side + 1]
        s_r, s_i = field[2 * side], field[2 * side + 1]
        terms.append((g_r * s_r + g_i * s_i, g_i * s_r - g_r * s_i))
    for part in range(2):
        up, down = terms[0][part], terms[1][part]
        kept = jnp.where(near, up, down).astype(jnp.bfloat16)
        sent = jnp.where(near, down, up).astype(jnp.bfloat16)
        at = first + part * count
        for q in range(COLS):
            lanes = slice(q * LANES, (q + 1) * LANES)
            out_ref[q, at : at + count, :] = kept[:, lanes]
            out_ref[q, FILTER_ROWS + at : FILTER_ROWS + at + count, :] = sent[:, lanes]


def edge_spectrum(ref, first, tables):
    edges = wide(ref, FILTER_ROWS, EDGE_ROWS)
    with_cos, with_sin = dot(edges, tables[0]), dot(edges, tables[1])
    real, imag = slice(first, first + GROUPS), slice(first + GROUPS, first + 2 * GROUPS)
    return with_cos[real] - with_sin[imag], -with_cos[imag] - with_sin[real]


def edge_terms(field, grad):
    (s_r, s_i), (g_r, g_i) = field, grad
    return [g_r * s_r + g_i * s_i, g_i * s_r - g_r * s_i]


def mix_last_kernel(
    place_ref, x_ref, y_ref, kept_ref, recv_ref, first_tables, second_tables,
    out_ref, total_ref, terms_ref, sem,
):
    slots = H2 // 8
    special, near = masks(place_ref, slots)
    tables = second_tables[0], second_tables[1]
    grad = spectrum(x_ref, SECOND_SLOT, slots, special, *tables)
    field = spectrum(y_ref, SECOND_SLOT, slots, special, *tables)
    put_terms(terms_ref, SECOND_SLOT, slots, near, field, grad)
    at = 2 * GROUPS
    second_edges = edge_terms(
        edge_spectrum(y_ref, at, tables), edge_spectrum(x_ref, at, tables)
    )
    slots = H1 // 8
    special, near = masks(place_ref, slots)
    tables = first_tables[0], first_tables[1]
    field = spectrum(x_ref, 0, slots, special, *tables)
    grad = spectrum(y_ref, 0, slots, special, *tables)
    put_terms(terms_ref, 0, slots, near, field, grad)
    edges = edge_terms(edge_spectrum(x_ref, 0, tables), edge_spectrum(y_ref, 0, tables))
    filled = jnp.zeros((EDGE_ROWS - 4 * GROUPS, 512), jnp.float32)
    edges = jnp.concatenate(edges + second_edges + [filled], axis=0).astype(jnp.bfloat16)
    for q in range(COLS):
        terms_ref[q, 2 * FILTER_ROWS :, :] = edges[:, q * LANES : (q + 1) * LANES]
    copy = pltpu.make_async_copy(terms_ref, total_ref, sem)
    copy.start()
    real, imag = filters(near, kept_ref, recv_ref, 0, slots)
    up, down = apply_back(real, imag, grad)
    put_inverse(out_ref, 0, slots, special, up, down, *tables)
    copy.wait()


def smem():
    return pl.BlockSpec(memory_space=pltpu.SMEM)


def hbm(count):
    return [pl.BlockSpec(memory_space=pltpu.HBM)] * count


def vmem(count):
    return [pl.BlockSpec()] * count


def both_tables():
    return [constant(np.stack(col_tables(n))) for n in (H1, H2)]


def mix_first(place, entries, kept, recv):
    return pl.pallas_call(
        mix_first_kernel,
        out_shape=jax.ShapeDtypeStruct((COLS, FILTER_ROWS, LANES), jnp.bfloat16),
        in_specs=[smem()] + vmem(5),
        name="mix_first",
        **params(8 * FILTER_ROWS * 512 * 512, 6 << 20),
    )(place, entries, kept, recv, *both_tables())


def mix_last(place, entries, later, kept, recv):
    total = (COLS, 2 * FILTER_ROWS + EDGE_ROWS, LANES)
    return pl.pallas_call(
        mix_last_kernel,
        out_shape=(
            jax.ShapeDtypeStruct((COLS, SECOND_SLOT, LANES), jnp.bfloat16),
            jax.ShapeDtypeStruct(total, jnp.bfloat16),
        ),
        in_specs=[smem()] + vmem(6),
        out_specs=tuple(vmem(1) + hbm(1)),
        scratch_shapes=[pltpu.VMEM(total, jnp.bfloat16), pltpu.SemaphoreType.DMA],
        name="mix_last",
        **params(12 * FILTER_ROWS * 512 * 512, 8 << 20),
    )(place, entries, later, kept, recv, *both_tables())


def grid_of(rows, columns):
    shape = (rows, columns)
    return lax.broadcasted_iota(jnp.int32, shape, 0), lax.broadcasted_iota(jnp.int32, shape, 1)


def ones_at(mask):
    return jnp.where(mask, 1.0, 0.0).astype(jnp.bfloat16)


def kept_rows(near, slots):
    slot, local = grid_of(slots, 2 * slots)
    return ones_at(local == jnp.where(near, slot, slots - slot))


def sent_rows(near, slots):
    slot, local = grid_of(slots, 2 * slots)
    return ones_at(local == jnp.where(near, slots + slot, lax.rem(2 * slots - slot, 2 * slots)))


def quarter_lanes(quarter):
    wide_at, narrow_at = grid_of(512, LANES)
    return ones_at(
        wide_at == lax.div(narrow_at, 64) * 256 + 64 * quarter + lax.rem(narrow_at, 64)
    )


def second_pair(ref, part, g):
    pair = [ref[part, 2 * g + i].astype(jnp.bfloat16) for i in range(2)]
    return jnp.concatenate(pair, axis=1)


def send_filters_kernel(
    place_ref, first_ref, second_ref, sent_ref, zero_ref, first_buf, second_buf, sems
):
    quarter = place_ref[1]
    at = pl.ds(pl.multiple_of(quarter * LANES, LANES), LANES)
    first_copy = pltpu.make_async_copy(first_ref.at[:, :, :, at], first_buf, sems.at[0])
    second_copy = pltpu.make_async_copy(second_ref, second_buf, sems.at[1])
    first_copy.start()
    second_copy.start()
    near = place_ref[0] < 2
    zeros = []
    for n in (H1, H2):
        slots = n // 8
        first = 0 if n == H1 else 2 * GROUPS * H1 // 8
        pick = sent_rows(near, slots)
        if n == H1:
            first_copy.wait()
        else:
            second_copy.wait()
            lanes = quarter_lanes(quarter)
        for part in range(2):
            for g in range(GROUPS):
                if n == H1:
                    rows = first_buf[part, g].astype(jnp.bfloat16)
                else:
                    rows = dot(second_pair(second_buf, part, g), lanes).astype(jnp.bfloat16)
                rows = dot(pick, rows)
                zeros.append(rows[:1])
                sent_ref[first : first + slots, :] = rows.astype(jnp.bfloat16)
                first += slots
    zeros.append(jnp.zeros((4, LANES), jnp.float32))
    zero_ref[...] = jnp.concatenate(zeros, axis=0).astype(jnp.bfloat16)


def keep_filters_kernel(place_ref, first_ref, second_ref, kept_ref):
    near = place_ref[0] < 2
    first = 0
    lanes = [quarter_lanes(q) for q in range(COLS)]
    for n in (H1, H2):
        slots = n // 8
        pick = kept_rows(near, slots)
        for part in range(2):
            for g in range(GROUPS):
                if n == H1:
                    rows = first_ref[part, g].astype(jnp.bfloat16)
                else:
                    rows = second_pair(second_ref, part, g)
                rows = dot(pick, rows).astype(jnp.bfloat16)
                for q in range(COLS):
                    if n == H1:
                        cut = rows[:, q * LANES : (q + 1) * LANES]
                    else:
                        cut = dot(rows, lanes[q]).astype(jnp.bfloat16)
                    kept_ref[q, first : first + slots, :] = cut
                first += slots


def send_filters(place, filter_first, filter_second):
    return pl.pallas_call(
        send_filters_kernel,
        out_shape=(
            jax.ShapeDtypeStruct((FILTER_ROWS, LANES), jnp.bfloat16),
            jax.ShapeDtypeStruct((16, LANES), jnp.bfloat16),
        ),
        in_specs=[smem()] + hbm(2),
        scratch_shapes=[
            pltpu.VMEM((2, GROUPS, H1 // 4, LANES), jnp.float32),
            pltpu.VMEM((2, 2 * GROUPS, H2 // 4, H2), jnp.float32),
            pltpu.SemaphoreType.DMA((2,)),
        ],
        name="send_filters",
        **params(12 * 64 * 512 * 128 * 2, 2 << 20, 60),
    )(place, filter_first, filter_second)


def keep_filters(place, filter_first, filter_second):
    return pl.pallas_call(
        keep_filters_kernel,
        out_shape=jax.ShapeDtypeStruct((COLS, FILTER_ROWS, LANES), jnp.bfloat16),
        in_specs=[smem()] + vmem(2),
        name="keep_filters",
        **params(12 * 64 * 512 * 512 * 2, 4 << 20),
    )(place, filter_first, filter_second)


def put_slot_zero(block, zero, take, slots):
    shaped = block.reshape(2 * GROUPS, slots, LANES)
    here = (jnp.arange(slots) == 0)[None, :, None] & take
    return jnp.where(here, zero[:, None, :], shaped).reshape(2 * GROUPS * slots, LANES)


def put_slots_zero(block, zero, take):
    split, groups = 2 * GROUPS * H1 // 8, 2 * GROUPS
    return (
        put_slot_zero(block[:split], zero[:groups], take, H1 // 8),
        put_slot_zero(block[split:], zero[groups : 2 * groups], take, H2 // 8),
    )


def swap_filters(sent, zero):
    return lax.ppermute(sent, "col", SWAP), lax.ppermute(zero, "col", ((2, 0), (3, 1)))


def patch_filters(recv, zero, col):
    recv = jnp.concatenate(put_slots_zero(recv, zero, col < 2), axis=0)
    return lax.all_gather(recv, "rep", axis=0, tiled=False)


def place_grads_kernel(
    place_ref, kept_first, recv_first, kept_second, recv_second, first_ref, second_ref
):
    near = place_ref[0] < 2
    wide_at, narrow_at = grid_of(LANES, LANES // 2)
    lanes = [ones_at(wide_at == narrow_at + 64 * i) for i in range(2)]
    for n, kept, recv in ((H1, kept_first, recv_first), (H2, kept_second, recv_second)):
        slots = n // 8
        local, slot = grid_of(2 * slots, slots)
        mirror = lax.rem(2 * slots - slot, 2 * slots)
        pick_kept = ones_at(local == jnp.where(near, slot, slots - slot))
        pick_recv = ones_at(local == jnp.where(near, slots + slot, mirror))
        for part in range(2):
            for g in range(GROUPS):
                at = (part * GROUPS + g) * slots
                rows = dot(pick_kept, kept[at : at + slots]) + dot(
                    pick_recv, recv[at : at + slots]
                )
                if n == H1:
                    first_ref[part, g] = rows
                else:
                    rows = rows.astype(jnp.bfloat16)
                    for i in range(2):
                        second_ref[part, 2 * g + i] = dot(rows, lanes[i])


def summed(terms):
    return lax.psum_scatter(terms, "rep", scatter_dimension=0, tiled=False)


def place_grads(place, kept, recv, edges, col):
    recv_first, recv_second = put_slots_zero(recv, edges, col >= 2)
    return pl.pallas_call(
        place_grads_kernel,
        out_shape=(
            jax.ShapeDtypeStruct((2, GROUPS, H1 // 4, LANES), jnp.float32),
            jax.ShapeDtypeStruct((2, 2 * GROUPS, H2 // 4, LANES // 2), jnp.float32),
        ),
        in_specs=[smem()] + vmem(4),
        name="place_grads",
        **params(12 * 128 * 128 * 128 * 2, 2 << 20),
    )(place, kept[:SECOND_SLOT], recv_first, kept[SECOND_SLOT:], recv_second)


def layer_normalize(entry_values, gains):
    center = entry_values - jnp.mean(entry_values, axis=1, keepdims=True)
    spread = jnp.mean(center * center, axis=1, keepdims=True)
    return center * lax.rsqrt(spread + epsilon) * gains[None, :, None, None]


def norm_pullback_step(entry_values, gains, upstream):
    _, pullback = jax.vjp(lambda inner_vals: layer_normalize(inner_vals, gains), entry_values)
    return pullback(upstream.astype(jnp.float32))[0]


def fold(values):
    total = jnp.broadcast_to(jnp.sum(values, axis=0, keepdims=True), (8, LANES))
    return (total + pltpu.roll(total, LANES // 2, 1))[:1]


def standardize(values):
    center = values - fold(values) / 192.0
    scale = lax.rsqrt(fold(center * center) / 192.0 + epsilon)
    return center * scale, scale


def pack_pairs(block):
    at, lane = grid_of(LANES, 192)
    mine = lax.rem(lane, 2) == lax.div(at, 64)
    fields = []
    for i in range(8):
        field = block[i].astype(jnp.float32)
        fields.append(jnp.where(mine, jnp.concatenate([field, field], axis=0), 0.0))
    at, lane = grid_of(96, 192)
    return lax.dot_general(
        ones_at(lax.div(lane, 2) == at),
        jnp.concatenate(fields, axis=0).astype(jnp.bfloat16),
        (((1,), (1,)), ((), ())),
        preferred_element_type=jnp.float32,
    )


def first_norm_kernel(
    x_ref, g_ref, gain_ref, out_ref, x_buf, g_buf, gain_buf, pack_buf, sems
):
    copies = [
        pltpu.make_async_copy(source, target, sems.at[i])
        for i, (source, target) in enumerate(
            ((x_ref, x_buf), (gain_ref, gain_buf), (g_ref, g_buf))
        )
    ]
    for copy in copies:
        copy.start()
    copies[0].wait()
    copies[1].wait()
    pixels = x_buf[...].astype(jnp.float32)
    center = pixels - jnp.sum(pixels, axis=0, keepdims=True) / 96.0
    scale = lax.rsqrt(jnp.sum(center * center, axis=0) / 96.0 + epsilon)
    for c in range(96):
        at = (c % GROUPS) * 16
        out_ref[c // GROUPS, at : at + 16, :] = (center[c] * scale * gain_buf[c]).astype(
            jnp.bfloat16
        )
    copies[2].wait()
    packed = pack_pairs(g_buf[...])
    for i in range(8):
        pack_buf[pl.ds(i, 96, stride=8), :] = packed[:, i * LANES : (i + 1) * LANES]
    packed = pack_buf[...].reshape(ROWS, GROUPS * 8, LANES)
    out_ref[:, GROUPS * 16 :, :] = packed.astype(jnp.bfloat16)


def first_norm(images, grad_out, gains):
    return pl.pallas_call(
        first_norm_kernel,
        out_shape=jax.ShapeDtypeStruct((ROWS, GROUPS * 24, LANES), jnp.bfloat16),
        in_specs=hbm(3),
        scratch_shapes=[
            pltpu.VMEM((96, 16, LANES), jnp.bfloat16),
            pltpu.VMEM((8, 64, 192), jnp.bfloat16),
            pltpu.SMEM((96,), jnp.float32),
            pltpu.VMEM((768, LANES), jnp.float32),
            pltpu.SemaphoreType.DMA((3,)),
        ],
        name="first_norm",
        **params(4 * 768 * 64 * 128, 2 << 20, 60),
    )(images, grad_out, gains)


def low_half():
    return lax.broadcasted_iota(jnp.int32, (96, LANES), 1) < LANES // 2


def token_kernel(
    x_hbm, m_ref, g_hbm, w_hbm, wt_hbm, gain_ref, out_ref,
    x_ref, g_ref, w_ref, wt_ref, s_ref, n_ref, back_ref, o_ref, sems,
):
    copies = [
        pltpu.make_async_copy(source, target, sems.at[i])
        for i, (source, target) in enumerate(
            ((x_hbm, x_ref), (w_hbm, w_ref), (g_hbm, g_ref), (wt_hbm, wt_ref))
        )
    ]
    for copy in copies:
        copy.start()
    at, lane = grid_of(LANES, 2 * LANES)
    spread_at = ones_at(at == 2 * lax.rem(lane, 64) + lax.div(lane, LANES))
    at, lane = grid_of(2 * LANES, 2 * LANES)
    here = LANES * lax.rem(lax.div(at, 64), 2) + 2 * lax.rem(at, 64) + lax.div(at, LANES)
    merge_at = ones_at(lane == here)
    mixed = m_ref[:, : GROUPS * 16, :].astype(jnp.float32).reshape(1536, LANES)
    back_ref[...] = m_ref[:, GROUPS * 16 :, :].astype(jnp.float32).reshape(768, LANES)
    copies[0].wait()
    section = x_ref[...].astype(jnp.float32).reshape(1536, LANES) + mixed
    spread = dot(section.astype(jnp.bfloat16), spread_at)
    for e in range(2):
        s_ref[e] = spread[:, e * LANES : (e + 1) * LANES]
    low = low_half()
    for copy in copies[1:]:
        copy.wait()
    packed = pack_pairs(g_ref[...])
    for first in range(0, 8, 2):
        patches = [
            jnp.concatenate(
                [
                    s_ref[e, pl.ds(2 * i + a, 96, stride=16), :].astype(jnp.bfloat16)
                    for a in range(2)
                    for e in range(2)
                ],
                axis=0,
            )
            for i in (first, first + 1)
        ]
        both = dot(w_ref[...], jnp.concatenate(patches, axis=1))
        grads = []
        for i in range(2):
            block = both[:, i * LANES : (i + 1) * LANES]
            down = jnp.where(low, block[:96], block[96:]).astype(jnp.bfloat16)
            normed, scale = standardize(down.astype(jnp.float32))
            rows = pl.ds(first + i, 96, stride=8)
            n_ref[rows, :] = normed * gain_ref[...]
            upstream = back_ref[rows, :] * gain_ref[...]
            step = upstream - fold(upstream) / 192.0 - normed * (fold(upstream * normed) / 192.0)
            at = (first + i) * LANES
            total = packed[:, at : at + LANES] + scale * step
            total = total.astype(jnp.bfloat16).astype(jnp.float32)
            grads.append((total, pltpu.roll(total, LANES // 2, 1)))
        even = jnp.where(low, grads[0][0], grads[1][1])
        odd = jnp.where(low, grads[0][1], grads[1][0])
        both = jnp.concatenate([even, odd], axis=0).astype(jnp.bfloat16)
        patches = dot(wt_ref[...], both).astype(jnp.bfloat16)
        rows = [
            jnp.concatenate(
                [patches[(2 * a + e) * 96 : (2 * a + e + 1) * 96] for e in range(2)], axis=1
            )
            for a in range(2)
        ]
        merged = dot(jnp.concatenate(rows, axis=0), merge_at)
        for i in range(2):
            for a in range(2):
                o_ref[pl.ds(2 * (first + i) + a, 96, stride=16), :] = merged[
                    a * 96 : (a + 1) * 96, i * LANES : (i + 1) * LANES
                ]
    out_ref[:, : GROUPS * 16, :] = (
        o_ref[...].reshape(ROWS, GROUPS * 16, LANES).astype(jnp.bfloat16)
    )
    out_ref[:, GROUPS * 16 :, :] = (
        n_ref[...].reshape(ROWS, GROUPS * 8, LANES).astype(jnp.bfloat16)
    )


def token_step(images, back, grad_out, weight, gains):
    return pl.pallas_call(
        token_kernel,
        out_shape=jax.ShapeDtypeStruct((ROWS, GROUPS * 24, LANES), jnp.bfloat16),
        in_specs=hbm(1) + vmem(1) + hbm(3) + vmem(1),
        scratch_shapes=[
            pltpu.VMEM((96, 16, LANES), jnp.bfloat16),
            pltpu.VMEM((8, 64, 192), jnp.bfloat16),
            pltpu.VMEM((192, 384), jnp.bfloat16),
            pltpu.VMEM((384, 192), jnp.bfloat16),
            pltpu.VMEM((2, 1536, LANES), jnp.float32),
            pltpu.VMEM((768, LANES), jnp.float32),
            pltpu.VMEM((768, LANES), jnp.float32),
            pltpu.VMEM((1536, LANES), jnp.float32),
            pltpu.SemaphoreType.DMA((4,)),
        ],
        name="token_step",
        **params(8 * 2 * 192 * 384 * 256, 4 << 20),
    )(images, back, grad_out, weight, weight.T, gains)


def unpack_first(blocks):
    return blocks.reshape(1, 96, 16, LANES)


def pack_second(field):
    pairs = field.reshape(96, 2, 8, 64).transpose(0, 2, 1, 3)
    return pairs.reshape(ROWS, GROUPS * 8, LANES)


def exchange(blocks, axis):
    return lax.all_to_all(blocks, axis, split_axis=0, concat_axis=0, tiled=True)


def shards(images, gain_first, filter_first, reduce_weight, gain_second, filter_second, grad_out):
    col = lax.axis_index("col")
    place = jnp.stack([col, lax.axis_index("rep")]).astype(jnp.int32)
    pixels = images.reshape(96, 16, LANES)
    upstream = grad_out.transpose(0, 2, 3, 1).reshape(8, 64, 192)
    weight = reduce_weight.reshape(96, 2, 384).transpose(1, 0, 2).reshape(192, 384)
    gains = jnp.repeat(gain_second.reshape(96, 2), 64, axis=1)

    sent, zero = send_filters(place, filter_first, filter_second)
    swapped = swap_filters(sent, zero)
    kept = keep_filters(place, filter_first, filter_second)
    both = exchange(first_norm(pixels, upstream, gain_first), "row")
    half = forward_rows(both, (H1, H2))
    half, swapped = lax.optimization_barrier((half, swapped))
    recv = patch_filters(*swapped, col)
    both = exchange(half, "col")
    mixed = exchange(mix_first(place, both, kept, recv), "col")
    mixed = exchange(inverse_rows(mixed, (H1, H2)), "row")
    tokens = token_step(pixels, mixed, upstream, weight, gains)
    later = exchange(forward_rows(exchange(tokens, "row"), (H1, H2)), "col")
    dspec_one, terms = mix_last(place, both, later, kept, recv)
    terms = summed(terms)
    rot_one = exchange(dspec_one, "col")
    rot_one, terms = lax.optimization_barrier((rot_one, terms))
    swapped = lax.ppermute(terms[FILTER_ROWS : 2 * FILTER_ROWS], "col", SWAP)
    grad_norm_one = unpack_first(exchange(inverse_rows(rot_one, (H1,)), "row"))
    grad_images = (
        unpack_first(tokens[:, : GROUPS * 16]).astype(jnp.float32)
        + norm_pullback_step(images.astype(jnp.float32), gain_first, grad_norm_one)
    ).astype(jnp.bfloat16)
    grad_images, swapped = lax.optimization_barrier((grad_images, swapped))
    grad_first, grad_second = place_grads(
        place, terms[:FILTER_ROWS], swapped, terms[2 * FILTER_ROWS :], col
    )
    return (grad_images, grad_first, grad_second)


def solution(mesh):
    placed = (
        P("rep", None, "row", "col"),
        P(),
        P(None, "row", "col", None),
        P(),
        P(),
        P(None, "row", "col", None),
        P("rep", None, "row", "col"),
    )
    return jax.shard_map(
        shards,
        mesh=mesh,
        in_specs=placed,
        out_specs=(
            P("rep", None, "row", "col"),
            P(None, "row", "col", "rep"),
            P(None, "row", "col", "rep"),
        ),
        check_vma=False,
    )
```

```python
import functools
import math

import jax
import jax.numpy as jnp
import numpy as np
from jax import lax
from jax.experimental import pallas as pl
from jax.experimental.pallas import tpu as pltpu
from jax.sharding import PartitionSpec as P

H1 = 512
H2 = 256
GROUPS = 3
COLS = 4
ROWS = 32
LANES = 128
SECOND_SLOT = 2 * GROUPS * H1 // 8
FILTER_ROWS = 2 * GROUPS * (H1 + H2) // 8
EDGE_ROWS = 16

epsilon = 1e-06

ORDER = (0, 2, 3, 1)
SWAP = ((0, 3), (3, 0), (1, 2), (2, 1))


def cos_sin(n):
    index = np.arange(n)
    angles = (index[:, None] * index[None, :] % n) * (2.0 * math.pi / n)
    factor = 1.0 / math.sqrt(n)
    return np.cos(angles) * factor, np.sin(angles) * factor


def row_table(n):
    cos, sin = cos_sin(n)
    slots = n // 8
    parts = []
    for c in range(COLS):
        k = ORDER[c] * slots + np.arange(slots)
        real, imag = cos[k], -sin[k]
        if c == 0:
            imag[0] = cos[n // 2]
        parts += [real, imag]
    return np.concatenate(parts, axis=0)


def edge_table(n):
    cos, sin = cos_sin(n)
    table = np.zeros((EDGE_ROWS, n))
    table[4] = cos[n // 2]
    table[6], table[7] = cos[n // 4], -sin[n // 4]
    return table


def col_tables(n):
    cos, sin = cos_sin(n)
    pair = 512 // n
    width = LANES // pair
    if pair == 1:
        return cos, sin
    out = []
    for table in (cos, sin):
        blocks = table.reshape(COLS, width, COLS, width)
        full = np.zeros((COLS, pair, width, COLS, pair, width))
        for p in range(pair):
            full[:, p, :, :, p, :] = blocks
        out.append(full.reshape(512, 512))
    return tuple(out)


def constant(values):
    return jnp.asarray(np.asarray(values, np.float32).astype(jnp.bfloat16))


def dot(a, b):
    return jnp.dot(a, b, preferred_element_type=jnp.float32)


def params(flops, traffic, vmem_mib=40):
    return dict(
        compiler_params=pltpu.CompilerParams(vmem_limit_bytes=vmem_mib * 1024 * 1024),
        cost_estimate=pl.CostEstimate(flops=flops, bytes_accessed=traffic, transcendentals=0),
    )


def gather_rows(block, rows):
    parts = []
    for g in range(GROUPS):
        part = block[:, g * rows : (g + 1) * rows, :]
        if rows % 16:
            part = part.astype(jnp.float32)
        parts.append(part.reshape(ROWS * rows, LANES).astype(jnp.bfloat16))
    return jnp.concatenate(parts, axis=1)


def forward_rows_kernel(layout, *refs):
    x_ref, tables, out_ref = refs[0], refs[1:-1], refs[-1]
    edges = []
    for i, (n, first_in, first_out) in enumerate(layout):
        rows = n // ROWS
        slots = n // 8
        block = x_ref[:, first_in : first_in + GROUPS * rows, :]
        gathered = gather_rows(block, rows)
        result = dot(tables[i][...], gathered)
        half = result[:n].astype(jnp.bfloat16)
        edges.append(result[n:])
        half = half.reshape(COLS, 2, slots, GROUPS * LANES)
        for part in range(2):
            for g in range(GROUPS):
                at = first_out + (part * GROUPS + g) * slots
                out_ref[:, at : at + slots, :] = half[:, part, :, g * LANES : (g + 1) * LANES]
    for c in range(COLS):
        pieces = [
            edge[2 * c + part : 2 * c + part + 1, g * LANES : (g + 1) * LANES]
            for edge in edges
            for part in range(2)
            for g in range(GROUPS)
        ]
        pieces.append(jnp.zeros((EDGE_ROWS - len(pieces), LANES), jnp.float32))
        out_ref[c, FILTER_ROWS:, :] = jnp.concatenate(pieces, axis=0).astype(jnp.bfloat16)


def forward_rows(entries, sizes):
    layout, _, slots = layout_of(sizes)
    flops = sum(2 * n * n * GROUPS * LANES for n in sizes)
    return pl.pallas_call(
        functools.partial(forward_rows_kernel, layout),
        out_shape=jax.ShapeDtypeStruct((COLS, slots + EDGE_ROWS, LANES), jnp.bfloat16),
        name="forward_rows_" + "_".join(str(n) for n in sizes),
        **params(flops, 2 << 20),
    )(entries, *[constant(np.concatenate([row_table(n), edge_table(n)])) for n in sizes])


def inverse_rows_kernel(layout, *refs):
    x_ref, tables, out_ref = refs[0], refs[1:-1], refs[-1]
    for (n, first_out, first_in), table in zip(layout, tables):
        rows = n // ROWS
        slots = n // 8
        parts = []
        for g in range(GROUPS):
            both = []
            for part in range(2):
                at = first_in + (part * GROUPS + g) * slots
                both.append(x_ref[:, at : at + slots, :].reshape(COLS, 1, slots, LANES))
            parts.append(jnp.concatenate(both, axis=1).reshape(n, LANES))
        result = dot(table[...], jnp.concatenate(parts, axis=1))
        pieces = [
            result[:, g * LANES : (g + 1) * LANES].reshape(ROWS, rows, LANES)
            for g in range(GROUPS)
        ]
        out_ref[:, first_out : first_out + GROUPS * rows, :] = jnp.concatenate(
            pieces, axis=1
        ).astype(jnp.bfloat16)


def layout_of(sizes):
    layout, first_token, first_slot = [], 0, 0
    for n in sizes:
        layout.append((n, first_token, first_slot))
        first_token += GROUPS * n // ROWS
        first_slot += 2 * GROUPS * n // 8
    return tuple(layout), first_token, first_slot


def inverse_rows(entries, sizes):
    layout, tokens, _ = layout_of(sizes)
    flops = sum(2 * n * n * GROUPS * LANES for n in sizes)
    return pl.pallas_call(
        functools.partial(inverse_rows_kernel, layout),
        out_shape=jax.ShapeDtypeStruct((ROWS, tokens, LANES), jnp.bfloat16),
        name="inverse_rows_" + "_".join(str(n) for n in sizes),
        **params(flops, 2 << 20),
    )(entries, *[constant(row_table(n).T) for n in sizes])


def wide(ref, first, count):
    return jnp.concatenate([ref[q, first : first + count, :] for q in range(COLS)], axis=1)


def spectrum(ref, first, slots, special, cos, sin):
    count = GROUPS * slots
    real, imag = wide(ref, first, count), wide(ref, first + count, count)
    real_cos, real_sin = dot(real, cos), dot(real, sin)
    imag_cos, imag_sin = dot(imag, cos), dot(imag, sin)
    return (
        jnp.where(special, real_cos, real_cos + imag_sin),
        jnp.where(special, -real_sin, imag_cos - real_sin),
        jnp.where(special, imag_cos, real_cos - imag_sin),
        jnp.where(special, -imag_sin, -imag_cos - real_sin),
    )


def filters(near, kept_ref, recv_ref, first, slots):
    count = GROUPS * slots
    out = []
    for part in range(2):
        kept = wide(kept_ref, first + part * count, count).astype(jnp.float32)
        recv = wide(recv_ref, first + part * count, count).astype(jnp.float32)
        out.append((jnp.where(near, kept, recv), jnp.where(near, recv, kept)))
    return out


def put_inverse(out_ref, first, slots, special, up, down, cos, sin):
    count = GROUPS * slots
    (up_r, up_i), (down_r, down_i) = up, down
    bf16 = jnp.bfloat16
    sum_r = jnp.where(special, up_r, up_r + down_r).astype(bf16)
    sum_i = jnp.where(special, up_i, up_i + down_i).astype(bf16)
    dif_i = jnp.where(special, down_r, up_i - down_i).astype(bf16)
    dif_r = jnp.where(special, -down_i, up_r - down_r).astype(bf16)
    rot_real = (dot(sum_r, cos) - dot(sum_i, sin)).astype(bf16)
    rot_imag = (dot(dif_i, cos) + dot(dif_r, sin)).astype(bf16)
    for q in range(COLS):
        lanes = slice(q * LANES, (q + 1) * LANES)
        out_ref[q, first : first + count, :] = rot_real[:, lanes]
        out_ref[q, first + count : first + 2 * count, :] = rot_imag[:, lanes]


def masks(place_ref, slots):
    col = place_ref[0]
    row = lax.broadcasted_iota(jnp.int32, (GROUPS * slots, 512), 0)
    return (lax.rem(row, slots) + col * slots) == 0, col < 2


def apply_back(real, imag, grad):
    return [
        (
            real[side] * grad[2 * side] + imag[side] * grad[2 * side + 1],
            real[side] * grad[2 * side + 1] - imag[side] * grad[2 * side],
        )
        for side in range(2)
    ]


def mix_first_kernel(place_ref, x_ref, kept_ref, recv_ref, tables, out_ref):
    slots = H1 // 8
    special, near = masks(place_ref, slots)
    cos, sin = tables[0], tables[1]
    up_r, up_i, down_r, down_i = spectrum(x_ref, 0, slots, special, cos, sin)
    real, imag = filters(near, kept_ref, recv_ref, 0, slots)
    up = (real[0] * up_r - imag[0] * up_i, real[0] * up_i + imag[0] * up_r)
    down = (real[1] * down_r - imag[1] * down_i, real[1] * down_i + imag[1] * down_r)
    put_inverse(out_ref, 0, slots, special, up, down, cos, sin)

    first, slots = SECOND_SLOT, H2 // 8
    special, near = masks(place_ref, slots)
    cos, sin = tables[2], tables[3]
    grad = spectrum(x_ref, first, slots, special, cos, sin)
    real, imag = filters(near, kept_ref, recv_ref, first, slots)
    up, down = apply_back(real, imag, grad)
    put_inverse(out_ref, first, slots, special, up, down, cos, sin)


def put_terms(out_ref, first, slots, near, field, grad):
    count = GROUPS * slots
    terms = []
    for side in range(2):
        g_r, g_i = grad[2 * side], grad[2 * side + 1]
        s_r, s_i = field[2 * side], field[2 * side + 1]
        terms.append((g_r * s_r + g_i * s_i, g_i * s_r - g_r * s_i))
    for part in range(2):
        up, down = terms[0][part], terms[1][part]
        kept = jnp.where(near, up, down).astype(jnp.bfloat16)
        sent = jnp.where(near, down, up).astype(jnp.bfloat16)
        at = first + part * count
        for q in range(COLS):
            lanes = slice(q * LANES, (q + 1) * LANES)
            out_ref[q, at : at + count, :] = kept[:, lanes]
            out_ref[q, FILTER_ROWS + at : FILTER_ROWS + at + count, :] = sent[:, lanes]


def edge_spectrum(ref, first, tables):
    edges = wide(ref, FILTER_ROWS, EDGE_ROWS)
    with_cos, with_sin = dot(edges, tables[0]), dot(edges, tables[1])
    real, imag = slice(first, first + GROUPS), slice(first + GROUPS, first + 2 * GROUPS)
    return with_cos[real] - with_sin[imag], -with_cos[imag] - with_sin[real]


def edge_terms(field, grad):
    (s_r, s_i), (g_r, g_i) = field, grad
    return [g_r * s_r + g_i * s_i, g_i * s_r - g_r * s_i]


def mix_last_kernel(
    place_ref, x_ref, y_ref, kept_ref, recv_ref, tables_ref,
    out_ref, total_ref, terms_ref, sem,
):
    slots = H2 // 8
    special, near = masks(place_ref, slots)
    tables = tables_ref[2], tables_ref[3]
    grad = spectrum(x_ref, SECOND_SLOT, slots, special, *tables)
    field = spectrum(y_ref, SECOND_SLOT, slots, special, *tables)
    put_terms(terms_ref, SECOND_SLOT, slots, near, field, grad)
    at = 2 * GROUPS
    second_edges = edge_terms(
        edge_spectrum(y_ref, at, tables), edge_spectrum(x_ref, at, tables)
    )
    slots = H1 // 8
    special, near = masks(place_ref, slots)
    tables = tables_ref[0], tables_ref[1]
    field = spectrum(x_ref, 0, slots, special, *tables)
    grad = spectrum(y_ref, 0, slots, special, *tables)
    put_terms(terms_ref, 0, slots, near, field, grad)
    edges = edge_terms(edge_spectrum(x_ref, 0, tables), edge_spectrum(y_ref, 0, tables))
    filled = jnp.zeros((EDGE_ROWS - 4 * GROUPS, 512), jnp.float32)
    edges = jnp.concatenate(edges + second_edges + [filled], axis=0).astype(jnp.bfloat16)
    for q in range(COLS):
        terms_ref[q, 2 * FILTER_ROWS :, :] = edges[:, q * LANES : (q + 1) * LANES]
    copy = pltpu.make_async_copy(terms_ref, total_ref, sem)
    copy.start()
    real, imag = filters(near, kept_ref, recv_ref, 0, slots)
    up, down = apply_back(real, imag, grad)
    put_inverse(out_ref, 0, slots, special, up, down, *tables)
    copy.wait()


def smem():
    return pl.BlockSpec(memory_space=pltpu.SMEM)


def hbm(count):
    return [pl.BlockSpec(memory_space=pltpu.HBM)] * count


def vmem(count):
    return [pl.BlockSpec()] * count


def both_tables():
    return constant(np.stack(col_tables(H1) + col_tables(H2)))


def mix_first(place, entries, kept, recv):
    return pl.pallas_call(
        mix_first_kernel,
        out_shape=jax.ShapeDtypeStruct((COLS, FILTER_ROWS, LANES), jnp.bfloat16),
        in_specs=[smem()] + vmem(4),
        name="mix_first",
        **params(8 * FILTER_ROWS * 512 * 512, 6 << 20),
    )(place, entries, kept, recv, both_tables())


def mix_last(place, entries, later, kept, recv):
    total = (COLS, 2 * FILTER_ROWS + EDGE_ROWS, LANES)
    return pl.pallas_call(
        mix_last_kernel,
        out_shape=(
            jax.ShapeDtypeStruct((COLS, SECOND_SLOT, LANES), jnp.bfloat16),
            jax.ShapeDtypeStruct(total, jnp.bfloat16),
        ),
        in_specs=[smem()] + vmem(5),
        out_specs=tuple(vmem(1) + hbm(1)),
        scratch_shapes=[pltpu.VMEM(total, jnp.bfloat16), pltpu.SemaphoreType.DMA],
        name="mix_last",
        **params(12 * FILTER_ROWS * 512 * 512, 8 << 20),
    )(place, entries, later, kept, recv, both_tables())


def grid_of(rows, columns):
    shape = (rows, columns)
    return lax.broadcasted_iota(jnp.int32, shape, 0), lax.broadcasted_iota(jnp.int32, shape, 1)


def ones_at(mask):
    return jnp.where(mask, 1.0, 0.0).astype(jnp.bfloat16)


def kept_rows(near, slots):
    slot, local = grid_of(slots, 2 * slots)
    return ones_at(local == jnp.where(near, slot, slots - slot))


def sent_rows(near, slots):
    slot, local = grid_of(slots, 2 * slots)
    return ones_at(local == jnp.where(near, slots + slot, lax.rem(2 * slots - slot, 2 * slots)))


def quarter_lanes(quarter):
    wide_at, narrow_at = grid_of(512, LANES)
    return ones_at(
        wide_at == lax.div(narrow_at, 64) * 256 + 64 * quarter + lax.rem(narrow_at, 64)
    )


def second_pair(ref, part, g):
    pair = [ref[part, 2 * g + i].astype(jnp.bfloat16) for i in range(2)]
    return jnp.concatenate(pair, axis=1)


def send_filters_kernel(
    place_ref, quarter_ref, first_ref, second_ref, sent_ref, zero_ref, first_buf, second_buf, sems
):
    quarter = quarter_ref[0]
    at = pl.ds(pl.multiple_of(quarter * LANES, LANES), LANES)
    first_copy = pltpu.make_async_copy(first_ref.at[:, :, :, at], first_buf, sems.at[0])
    second_copy = pltpu.make_async_copy(second_ref, second_buf, sems.at[1])
    first_copy.start()
    second_copy.start()
    near = place_ref[0] < 2
    lanes = quarter_lanes(quarter)
    groups = [(part, g) for part in range(2) for g in range(GROUPS)]
    zeros = []
    first = 0
    for n in (H1, H2):
        slots = n // 8
        if n == H1:
            first_copy.wait()
            rows = [first_buf[part, g].astype(jnp.bfloat16) for part, g in groups]
        else:
            second_copy.wait()
            rows = [second_pair(second_buf, part, g) for part, g in groups]
            rows = dot(jnp.concatenate(rows, axis=0), lanes).astype(jnp.bfloat16)
            rows = [rows[2 * slots * i : 2 * slots * (i + 1)] for i in range(len(groups))]
        rows = dot(sent_rows(near, slots), jnp.concatenate(rows, axis=1))
        for i in range(len(groups)):
            picked = rows[:, i * LANES : (i + 1) * LANES]
            zeros.append(picked[:1])
            sent_ref[first : first + slots, :] = picked.astype(jnp.bfloat16)
            first += slots
    zeros.append(jnp.zeros((4, LANES), jnp.float32))
    zero_ref[...] = jnp.concatenate(zeros, axis=0).astype(jnp.bfloat16)


def keep_filters_kernel(place_ref, first_ref, second_ref, kept_ref):
    near = place_ref[0] < 2
    first = 0
    lanes = [quarter_lanes(q) for q in range(COLS)]
    for n in (H1, H2):
        slots = n // 8
        pick = kept_rows(near, slots)
        for part in range(2):
            for g in range(GROUPS):
                if n == H1:
                    rows = first_ref[part, g].astype(jnp.bfloat16)
                else:
                    rows = second_pair(second_ref, part, g)
                rows = dot(pick, rows).astype(jnp.bfloat16)
                for q in range(COLS):
                    if n == H1:
                        cut = rows[:, q * LANES : (q + 1) * LANES]
                    else:
                        cut = dot(rows, lanes[q]).astype(jnp.bfloat16)
                    kept_ref[q, first : first + slots, :] = cut
                first += slots


def send_filters(place, quarter, filter_first, filter_second):
    return pl.pallas_call(
        send_filters_kernel,
        out_shape=(
            jax.ShapeDtypeStruct((FILTER_ROWS, LANES), jnp.bfloat16),
            jax.ShapeDtypeStruct((16, LANES), jnp.bfloat16),
        ),
        in_specs=[smem()] * 2 + hbm(2),
        scratch_shapes=[
            pltpu.VMEM((2, GROUPS, H1 // 4, LANES), jnp.float32),
            pltpu.VMEM((2, 2 * GROUPS, H2 // 4, H2), jnp.float32),
            pltpu.SemaphoreType.DMA((2,)),
        ],
        name="send_filters",
        **params(12 * 64 * 512 * 128 * 2, 2 << 20, 60),
    )(place, quarter, filter_first, filter_second)


def keep_filters(place, filter_first, filter_second):
    return pl.pallas_call(
        keep_filters_kernel,
        out_shape=jax.ShapeDtypeStruct((COLS, FILTER_ROWS, LANES), jnp.bfloat16),
        in_specs=[smem()] + vmem(2),
        name="keep_filters",
        **params(12 * 64 * 512 * 512 * 2, 4 << 20),
    )(place, filter_first, filter_second)


def put_slot_zero(block, zero, take, slots):
    shaped = block.reshape(2 * GROUPS, slots, LANES)
    here = (jnp.arange(slots) == 0)[None, :, None] & take
    return jnp.where(here, zero[:, None, :], shaped).reshape(2 * GROUPS * slots, LANES)


def put_slots_zero(block, zero, take):
    split, groups = 2 * GROUPS * H1 // 8, 2 * GROUPS
    return (
        put_slot_zero(block[:split], zero[:groups], take, H1 // 8),
        put_slot_zero(block[split:], zero[groups : 2 * groups], take, H2 // 8),
    )


def swap_filters(sent, zero):
    return lax.ppermute(sent, "col", SWAP), lax.ppermute(zero, "col", ((2, 0), (3, 1)))


def patch_filters(recv, zero, col):
    recv = jnp.concatenate(put_slots_zero(recv, zero, col < 2), axis=0)
    return lax.all_gather(recv, "rep", axis=0, tiled=False)


def place_grads_kernel(
    place_ref, kept_first, recv_first, kept_second, recv_second, first_ref, second_ref
):
    near = place_ref[0] < 2
    wide_at, narrow_at = grid_of(LANES, LANES // 2)
    lanes = [ones_at(wide_at == narrow_at + 64 * i) for i in range(2)]
    groups = [(part, g) for part in range(2) for g in range(GROUPS)]
    for n, kept, recv in ((H1, kept_first, recv_first), (H2, kept_second, recv_second)):
        slots = n // 8
        local, slot = grid_of(2 * slots, slots)
        mirror = lax.rem(2 * slots - slot, 2 * slots)
        pick_kept = ones_at(local == jnp.where(near, slot, slots - slot))
        pick_recv = ones_at(local == jnp.where(near, slots + slot, mirror))
        kept, recv = [
            jnp.concatenate([ref[i * slots : (i + 1) * slots] for i in range(len(groups))], axis=1)
            for ref in (kept, recv)
        ]
        rows = dot(pick_kept, kept) + dot(pick_recv, recv)
        rows = [rows[:, i * LANES : (i + 1) * LANES] for i in range(len(groups))]
        if n == H1:
            for (part, g), block in zip(groups, rows):
                first_ref[part, g] = block
        else:
            rows = jnp.concatenate(rows, axis=0).astype(jnp.bfloat16)
            for i in range(2):
                half = dot(rows, lanes[i])
                for at, (part, g) in enumerate(groups):
                    second_ref[part, 2 * g + i] = half[at * 2 * slots : (at + 1) * 2 * slots]


def summed(terms):
    return lax.psum_scatter(terms, "rep", scatter_dimension=0, tiled=False)


def place_grads(place, kept, recv, edges, col):
    recv_first, recv_second = put_slots_zero(recv, edges, col >= 2)
    return pl.pallas_call(
        place_grads_kernel,
        out_shape=(
            jax.ShapeDtypeStruct((2, GROUPS, H1 // 4, LANES), jnp.float32),
            jax.ShapeDtypeStruct((2, 2 * GROUPS, H2 // 4, LANES // 2), jnp.float32),
        ),
        in_specs=[smem()] + vmem(4),
        name="place_grads",
        **params(12 * 128 * 128 * 128 * 2, 2 << 20),
    )(place, kept[:SECOND_SLOT], recv_first, kept[SECOND_SLOT:], recv_second)


def layer_normalize(entry_values, gains):
    center = entry_values - jnp.mean(entry_values, axis=1, keepdims=True)
    spread = jnp.mean(center * center, axis=1, keepdims=True)
    return center * lax.rsqrt(spread + epsilon) * gains[None, :, None, None]


def norm_pullback_step(entry_values, gains, upstream):
    _, pullback = jax.vjp(lambda inner_vals: layer_normalize(inner_vals, gains), entry_values)
    return pullback(upstream.astype(jnp.float32))[0]


def fold(values):
    total = jnp.broadcast_to(jnp.sum(values, axis=0, keepdims=True), (8, LANES))
    return (total + pltpu.roll(total, LANES // 2, 1))[:1]


def standardize(values):
    center = values - fold(values) / 192.0
    scale = lax.rsqrt(fold(center * center) / 192.0 + epsilon)
    return center * scale, scale


def pack_pairs(block):
    at, lane = grid_of(LANES, 192)
    mine = lax.rem(lane, 2) == lax.div(at, 64)
    fields = []
    for i in range(8):
        field = block[i].astype(jnp.float32)
        fields.append(jnp.where(mine, jnp.concatenate([field, field], axis=0), 0.0))
    at, lane = grid_of(96, 192)
    return lax.dot_general(
        ones_at(lax.div(lane, 2) == at),
        jnp.concatenate(fields, axis=0).astype(jnp.bfloat16),
        (((1,), (1,)), ((), ())),
        preferred_element_type=jnp.float32,
    )


def first_norm_kernel(
    x_ref, g_ref, gain_ref, out_ref, x_buf, g_buf, gain_buf, pack_buf, sems
):
    copies = [
        pltpu.make_async_copy(source, target, sems.at[i])
        for i, (source, target) in enumerate(
            ((x_ref, x_buf), (gain_ref, gain_buf), (g_ref, g_buf))
        )
    ]
    for copy in copies:
        copy.start()
    copies[0].wait()
    copies[1].wait()
    pixels = x_buf[...].astype(jnp.float32)
    center = pixels - jnp.sum(pixels, axis=0, keepdims=True) / 96.0
    scale = lax.rsqrt(jnp.sum(center * center, axis=0) / 96.0 + epsilon)
    for c in range(96):
        at = (c % GROUPS) * 16
        out_ref[c // GROUPS, at : at + 16, :] = (center[c] * scale * gain_buf[c]).astype(
            jnp.bfloat16
        )
    copies[2].wait()
    packed = pack_pairs(g_buf[...])
    for i in range(8):
        pack_buf[pl.ds(i, 96, stride=8), :] = packed[:, i * LANES : (i + 1) * LANES]
    packed = pack_buf[...].reshape(ROWS, GROUPS * 8, LANES)
    out_ref[:, GROUPS * 16 :, :] = packed.astype(jnp.bfloat16)


def first_norm(images, grad_out, gains):
    return pl.pallas_call(
        first_norm_kernel,
        out_shape=jax.ShapeDtypeStruct((ROWS, GROUPS * 24, LANES), jnp.bfloat16),
        in_specs=hbm(3),
        scratch_shapes=[
            pltpu.VMEM((96, 16, LANES), jnp.bfloat16),
            pltpu.VMEM((8, 64, 192), jnp.bfloat16),
            pltpu.SMEM((96,), jnp.float32),
            pltpu.VMEM((768, LANES), jnp.float32),
            pltpu.SemaphoreType.DMA((3,)),
        ],
        name="first_norm",
        **params(4 * 768 * 64 * 128, 2 << 20, 60),
    )(images, grad_out, gains)


def low_half():
    return lax.broadcasted_iota(jnp.int32, (96, LANES), 1) < LANES // 2


def token_kernel(
    x_hbm, m_ref, g_hbm, w_hbm, wt_hbm, gain_ref, out_ref,
    x_ref, g_ref, w_ref, wt_ref, s_ref, n_ref, back_ref, o_ref, sems,
):
    copies = [
        pltpu.make_async_copy(source, target, sems.at[i])
        for i, (source, target) in enumerate(
            ((x_hbm, x_ref), (w_hbm, w_ref), (g_hbm, g_ref), (wt_hbm, wt_ref))
        )
    ]
    for copy in copies:
        copy.start()
    at, lane = grid_of(LANES, 2 * LANES)
    spread_at = ones_at(at == 2 * lax.rem(lane, 64) + lax.div(lane, LANES))
    at, lane = grid_of(2 * LANES, 2 * LANES)
    here = LANES * lax.rem(lax.div(at, 64), 2) + 2 * lax.rem(at, 64) + lax.div(at, LANES)
    merge_at = ones_at(lane == here)
    mixed = m_ref[:, : GROUPS * 16, :].astype(jnp.float32).reshape(1536, LANES)
    back_ref[...] = m_ref[:, GROUPS * 16 :, :].astype(jnp.float32).reshape(768, LANES)
    copies[0].wait()
    section = x_ref[...].astype(jnp.float32).reshape(1536, LANES) + mixed
    spread = dot(section.astype(jnp.bfloat16), spread_at)
    for e in range(2):
        s_ref[e] = spread[:, e * LANES : (e + 1) * LANES]
    low = low_half()
    for copy in copies[1:]:
        copy.wait()
    packed = pack_pairs(g_ref[...])
    for first in range(0, 8, 2):
        patches = [
            jnp.concatenate(
                [
                    s_ref[e, pl.ds(2 * i + a, 96, stride=16), :].astype(jnp.bfloat16)
                    for a in range(2)
                    for e in range(2)
                ],
                axis=0,
            )
            for i in (first, first + 1)
        ]
        both = dot(w_ref[...], jnp.concatenate(patches, axis=1))
        grads = []
        for i in range(2):
            block = both[:, i * LANES : (i + 1) * LANES]
            down = jnp.where(low, block[:96], block[96:]).astype(jnp.bfloat16)
            normed, scale = standardize(down.astype(jnp.float32))
            rows = pl.ds(first + i, 96, stride=8)
            n_ref[rows, :] = normed * gain_ref[...]
            upstream = back_ref[rows, :] * gain_ref[...]
            step = upstream - fold(upstream) / 192.0 - normed * (fold(upstream * normed) / 192.0)
            at = (first + i) * LANES
            total = packed[:, at : at + LANES] + scale * step
            total = total.astype(jnp.bfloat16).astype(jnp.float32)
            grads.append((total, pltpu.roll(total, LANES // 2, 1)))
        even = jnp.where(low, grads[0][0], grads[1][1])
        odd = jnp.where(low, grads[0][1], grads[1][0])
        both = jnp.concatenate([even, odd], axis=0).astype(jnp.bfloat16)
        patches = dot(wt_ref[...], both).astype(jnp.bfloat16)
        rows = [
            jnp.concatenate(
                [patches[(2 * a + e) * 96 : (2 * a + e + 1) * 96] for e in range(2)], axis=1
            )
            for a in range(2)
        ]
        merged = dot(jnp.concatenate(rows, axis=0), merge_at)
        for i in range(2):
            for a in range(2):
                o_ref[pl.ds(2 * (first + i) + a, 96, stride=16), :] = merged[
                    a * 96 : (a + 1) * 96, i * LANES : (i + 1) * LANES
                ]
    out_ref[:, : GROUPS * 16, :] = (
        o_ref[...].reshape(ROWS, GROUPS * 16, LANES).astype(jnp.bfloat16)
    )
    out_ref[:, GROUPS * 16 :, :] = (
        n_ref[...].reshape(ROWS, GROUPS * 8, LANES).astype(jnp.bfloat16)
    )


def token_step(images, back, grad_out, weight, gains):
    return pl.pallas_call(
        token_kernel,
        out_shape=jax.ShapeDtypeStruct((ROWS, GROUPS * 24, LANES), jnp.bfloat16),
        in_specs=hbm(1) + vmem(1) + hbm(3) + vmem(1),
        scratch_shapes=[
            pltpu.VMEM((96, 16, LANES), jnp.bfloat16),
            pltpu.VMEM((8, 64, 192), jnp.bfloat16),
            pltpu.VMEM((192, 384), jnp.bfloat16),
            pltpu.VMEM((384, 192), jnp.bfloat16),
            pltpu.VMEM((2, 1536, LANES), jnp.float32),
            pltpu.VMEM((768, LANES), jnp.float32),
            pltpu.VMEM((768, LANES), jnp.float32),
            pltpu.VMEM((1536, LANES), jnp.float32),
            pltpu.SemaphoreType.DMA((4,)),
        ],
        name="token_step",
        **params(8 * 2 * 192 * 384 * 256, 4 << 20),
    )(images, back, grad_out, weight, weight.T, gains)


def unpack_first(blocks):
    return blocks.reshape(1, 96, 16, LANES)


def pack_second(field):
    pairs = field.reshape(96, 2, 8, 64).transpose(0, 2, 1, 3)
    return pairs.reshape(ROWS, GROUPS * 8, LANES)


def exchange(blocks, axis):
    return lax.all_to_all(blocks, axis, split_axis=0, concat_axis=0, tiled=True)


def shards(images, gain_first, filter_first, reduce_weight, gain_second, filter_second, grad_out):
    col = lax.axis_index("col")
    place = col.astype(jnp.int32).reshape(1)
    pixels = images.reshape(96, 16, LANES)
    upstream = grad_out.transpose(0, 2, 3, 1).reshape(8, 64, 192)
    weight = reduce_weight.reshape(96, 2, 384).transpose(1, 0, 2).reshape(192, 384)
    gains = jnp.repeat(gain_second.reshape(96, 2), 64, axis=1)

    quarter = lax.axis_index("rep").astype(jnp.int32).reshape(1)
    sent, zero = send_filters(place, quarter, filter_first, filter_second)
    swapped = swap_filters(sent, zero)
    kept = keep_filters(place, filter_first, filter_second)
    both = exchange(first_norm(pixels, upstream, gain_first), "row")
    half = forward_rows(both, (H1, H2))
    half, swapped = lax.optimization_barrier((half, swapped))
    recv = patch_filters(*swapped, col)
    both = exchange(half, "col")
    mixed = exchange(mix_first(place, both, kept, recv), "col")
    mixed = exchange(inverse_rows(mixed, (H1, H2)), "row")
    tokens = token_step(pixels, mixed, upstream, weight, gains)
    later = exchange(forward_rows(exchange(tokens, "row"), (H1, H2)), "col")
    dspec_one, terms = mix_last(place, both, later, kept, recv)
    terms = summed(terms)
    rot_one = exchange(dspec_one, "col")
    rot_one, terms = lax.optimization_barrier((rot_one, terms))
    swapped = lax.ppermute(terms[FILTER_ROWS : 2 * FILTER_ROWS], "col", SWAP)
    grad_norm_one = unpack_first(exchange(inverse_rows(rot_one, (H1,)), "row"))
    grad_images = (
        unpack_first(tokens[:, : GROUPS * 16]).astype(jnp.float32)
        + norm_pullback_step(images.astype(jnp.float32), gain_first, grad_norm_one)
    ).astype(jnp.bfloat16)
    grad_images, swapped = lax.optimization_barrier((grad_images, swapped))
    grad_first, grad_second = place_grads(
        place, terms[:FILTER_ROWS], swapped, terms[2 * FILTER_ROWS :], col
    )
    return (grad_images, grad_first, grad_second)


def solution(mesh):
    placed = (
        P("rep", None, "row", "col"),
        P(),
        P(None, "row", "col", None),
        P(),
        P(),
        P(None, "row", "col", None),
        P("rep", None, "row", "col"),
    )
    return jax.shard_map(
        shards,
        mesh=mesh,
        in_specs=placed,
        out_specs=(
            P("rep", None, "row", "col"),
            P(None, "row", "col", "rep"),
            P(None, "row", "col", "rep"),
        ),
        check_vma=False,
    )
```

```python
import functools
import math

import jax
import jax.numpy as jnp
import numpy as np
from jax import lax
from jax.experimental import pallas as pl
from jax.experimental.pallas import tpu as pltpu
from jax.sharding import PartitionSpec as P

H1 = 512
H2 = 256
GROUPS = 3
COLS = 4
ROWS = 32
LANES = 128
SECOND_SLOT = 2 * GROUPS * H1 // 8
FILTER_ROWS = 2 * GROUPS * (H1 + H2) // 8
EDGE_ROWS = 16

epsilon = 1e-06

ORDER = (0, 2, 3, 1)
SWAP = ((0, 3), (3, 0), (1, 2), (2, 1))


def cos_sin(n):
    index = np.arange(n)
    angles = (index[:, None] * index[None, :] % n) * (2.0 * math.pi / n)
    factor = 1.0 / math.sqrt(n)
    return np.cos(angles) * factor, np.sin(angles) * factor


def row_table(n):
    cos, sin = cos_sin(n)
    slots = n // 8
    parts = []
    for c in range(COLS):
        k = ORDER[c] * slots + np.arange(slots)
        real, imag = cos[k], -sin[k]
        if c == 0:
            imag[0] = cos[n // 2]
        parts += [real, imag]
    return np.concatenate(parts, axis=0)


def edge_table(n):
    cos, sin = cos_sin(n)
    table = np.zeros((EDGE_ROWS, n))
    table[4] = cos[n // 2]
    table[6], table[7] = cos[n // 4], -sin[n // 4]
    return table


def col_tables(n):
    cos, sin = cos_sin(n)
    pair = 512 // n
    width = LANES // pair
    if pair == 1:
        return cos, sin
    out = []
    for table in (cos, sin):
        blocks = table.reshape(COLS, width, COLS, width)
        full = np.zeros((COLS, pair, width, COLS, pair, width))
        for p in range(pair):
            full[:, p, :, :, p, :] = blocks
        out.append(full.reshape(512, 512))
    return tuple(out)


def constant(values):
    return jnp.asarray(np.asarray(values, np.float32).astype(jnp.bfloat16))


def dot(a, b):
    return jnp.dot(a, b, preferred_element_type=jnp.float32)


def params(flops, traffic, vmem_mib=40):
    return dict(
        compiler_params=pltpu.CompilerParams(vmem_limit_bytes=vmem_mib * 1024 * 1024),
        cost_estimate=pl.CostEstimate(flops=flops, bytes_accessed=traffic, transcendentals=0),
    )


def gather_rows(block, rows):
    parts = []
    for g in range(GROUPS):
        part = block[:, g * rows : (g + 1) * rows, :]
        if rows % 16:
            part = part.astype(jnp.float32)
        parts.append(part.reshape(ROWS * rows, LANES).astype(jnp.bfloat16))
    return jnp.concatenate(parts, axis=1)


def forward_rows_kernel(layout, *refs):
    x_ref, tables, out_ref = refs[0], refs[1:-1], refs[-1]
    edges = []
    for i, (n, first_in, first_out) in enumerate(layout):
        rows = n // ROWS
        slots = n // 8
        block = x_ref[:, first_in : first_in + GROUPS * rows, :]
        gathered = gather_rows(block, rows)
        result = dot(tables[i][...], gathered)
        half = result[:n].astype(jnp.bfloat16)
        edges.append(result[n:])
        half = half.reshape(COLS, 2, slots, GROUPS * LANES)
        for part in range(2):
            for g in range(GROUPS):
                at = first_out + (part * GROUPS + g) * slots
                out_ref[:, at : at + slots, :] = half[:, part, :, g * LANES : (g + 1) * LANES]
    for c in range(COLS):
        pieces = [
            edge[2 * c + part : 2 * c + part + 1, g * LANES : (g + 1) * LANES]
            for edge in edges
            for part in range(2)
            for g in range(GROUPS)
        ]
        pieces.append(jnp.zeros((EDGE_ROWS - len(pieces), LANES), jnp.float32))
        out_ref[c, FILTER_ROWS:, :] = jnp.concatenate(pieces, axis=0).astype(jnp.bfloat16)


def forward_rows(entries, sizes):
    layout, _, slots = layout_of(sizes)
    flops = sum(2 * n * n * GROUPS * LANES for n in sizes)
    return pl.pallas_call(
        functools.partial(forward_rows_kernel, layout),
        out_shape=jax.ShapeDtypeStruct((COLS, slots + EDGE_ROWS, LANES), jnp.bfloat16),
        name="forward_rows_" + "_".join(str(n) for n in sizes),
        **params(flops, 2 << 20),
    )(entries, *[constant(np.concatenate([row_table(n), edge_table(n)])) for n in sizes])


def inverse_rows_kernel(layout, *refs):
    x_ref, tables, out_ref = refs[0], refs[1:-1], refs[-1]
    for (n, first_out, first_in), table in zip(layout, tables):
        rows = n // ROWS
        slots = n // 8
        parts = []
        for g in range(GROUPS):
            both = []
            for part in range(2):
                at = first_in + (part * GROUPS + g) * slots
                both.append(x_ref[:, at : at + slots, :].reshape(COLS, 1, slots, LANES))
            parts.append(jnp.concatenate(both, axis=1).reshape(n, LANES))
        result = dot(table[...], jnp.concatenate(parts, axis=1))
        pieces = [
            result[:, g * LANES : (g + 1) * LANES].reshape(ROWS, rows, LANES)
            for g in range(GROUPS)
        ]
        out_ref[:, first_out : first_out + GROUPS * rows, :] = jnp.concatenate(
            pieces, axis=1
        ).astype(jnp.bfloat16)


def layout_of(sizes):
    layout, first_token, first_slot = [], 0, 0
    for n in sizes:
        layout.append((n, first_token, first_slot))
        first_token += GROUPS * n // ROWS
        first_slot += 2 * GROUPS * n // 8
    return tuple(layout), first_token, first_slot


def inverse_rows(entries, sizes):
    layout, tokens, _ = layout_of(sizes)
    flops = sum(2 * n * n * GROUPS * LANES for n in sizes)
    return pl.pallas_call(
        functools.partial(inverse_rows_kernel, layout),
        out_shape=jax.ShapeDtypeStruct((ROWS, tokens, LANES), jnp.bfloat16),
        name="inverse_rows_" + "_".join(str(n) for n in sizes),
        **params(flops, 2 << 20),
    )(entries, *[constant(row_table(n).T) for n in sizes])


def wide(ref, first, count):
    return jnp.concatenate([ref[q, first : first + count, :] for q in range(COLS)], axis=1)


def spectrum(ref, first, slots, special, cos, sin):
    count = GROUPS * slots
    real, imag = wide(ref, first, count), wide(ref, first + count, count)
    real_cos, real_sin = dot(real, cos), dot(real, sin)
    imag_cos, imag_sin = dot(imag, cos), dot(imag, sin)
    return (
        jnp.where(special, real_cos, real_cos + imag_sin),
        jnp.where(special, -real_sin, imag_cos - real_sin),
        jnp.where(special, imag_cos, real_cos - imag_sin),
        jnp.where(special, -imag_sin, -imag_cos - real_sin),
    )


def filters(near, kept_ref, recv_ref, first, slots):
    count = GROUPS * slots
    out = []
    for part in range(2):
        kept = wide(kept_ref, first + part * count, count).astype(jnp.float32)
        recv = wide(recv_ref, first + part * count, count).astype(jnp.float32)
        out.append((jnp.where(near, kept, recv), jnp.where(near, recv, kept)))
    return out


def put_inverse(out_ref, first, slots, special, up, down, cos, sin):
    count = GROUPS * slots
    (up_r, up_i), (down_r, down_i) = up, down
    bf16 = jnp.bfloat16
    sum_r = jnp.where(special, up_r, up_r + down_r).astype(bf16)
    sum_i = jnp.where(special, up_i, up_i + down_i).astype(bf16)
    dif_i = jnp.where(special, down_r, up_i - down_i).astype(bf16)
    dif_r = jnp.where(special, -down_i, up_r - down_r).astype(bf16)
    rot_real = (dot(sum_r, cos) - dot(sum_i, sin)).astype(bf16)
    rot_imag = (dot(dif_i, cos) + dot(dif_r, sin)).astype(bf16)
    for q in range(COLS):
        lanes = slice(q * LANES, (q + 1) * LANES)
        out_ref[q, first : first + count, :] = rot_real[:, lanes]
        out_ref[q, first + count : first + 2 * count, :] = rot_imag[:, lanes]


def masks(place_ref, slots):
    col = place_ref[0]
    row = lax.broadcasted_iota(jnp.int32, (GROUPS * slots, 512), 0)
    return (lax.rem(row, slots) + col * slots) == 0, col < 2


def apply_back(real, imag, grad):
    return [
        (
            real[side] * grad[2 * side] + imag[side] * grad[2 * side + 1],
            real[side] * grad[2 * side + 1] - imag[side] * grad[2 * side],
        )
        for side in range(2)
    ]


def mix_first_kernel(place_ref, x_ref, kept_ref, recv_ref, tables, out_ref):
    slots = H1 // 8
    special, near = masks(place_ref, slots)
    cos, sin = tables[0], tables[1]
    up_r, up_i, down_r, down_i = spectrum(x_ref, 0, slots, special, cos, sin)
    real, imag = filters(near, kept_ref, recv_ref, 0, slots)
    up = (real[0] * up_r - imag[0] * up_i, real[0] * up_i + imag[0] * up_r)
    down = (real[1] * down_r - imag[1] * down_i, real[1] * down_i + imag[1] * down_r)
    put_inverse(out_ref, 0, slots, special, up, down, cos, sin)

    first, slots = SECOND_SLOT, H2 // 8
    special, near = masks(place_ref, slots)
    cos, sin = tables[2], tables[3]
    grad = spectrum(x_ref, first, slots, special, cos, sin)
    real, imag = filters(near, kept_ref, recv_ref, first, slots)
    up, down = apply_back(real, imag, grad)
    put_inverse(out_ref, first, slots, special, up, down, cos, sin)


def put_terms(out_ref, first, slots, near, field, grad):
    count = GROUPS * slots
    terms = []
    for side in range(2):
        g_r, g_i = grad[2 * side], grad[2 * side + 1]
        s_r, s_i = field[2 * side], field[2 * side + 1]
        terms.append((g_r * s_r + g_i * s_i, g_i * s_r - g_r * s_i))
    for part in range(2):
        up, down = terms[0][part], terms[1][part]
        kept = jnp.where(near, up, down).astype(jnp.bfloat16)
        sent = jnp.where(near, down, up).astype(jnp.bfloat16)
        at = first + part * count
        for q in range(COLS):
            lanes = slice(q * LANES, (q + 1) * LANES)
            out_ref[q, at : at + count, :] = kept[:, lanes]
            out_ref[q, FILTER_ROWS + at : FILTER_ROWS + at + count, :] = sent[:, lanes]


def edge_spectrum(ref, first, tables):
    edges = wide(ref, FILTER_ROWS, EDGE_ROWS)
    with_cos, with_sin = dot(edges, tables[0]), dot(edges, tables[1])
    real, imag = slice(first, first + GROUPS), slice(first + GROUPS, first + 2 * GROUPS)
    return with_cos[real] - with_sin[imag], -with_cos[imag] - with_sin[real]


def edge_terms(field, grad):
    (s_r, s_i), (g_r, g_i) = field, grad
    return [g_r * s_r + g_i * s_i, g_i * s_r - g_r * s_i]


def mix_last_kernel(
    place_ref, x_ref, y_ref, kept_ref, recv_ref, tables_ref,
    out_ref, total_ref, terms_ref, sem,
):
    slots = H2 // 8
    special, near = masks(place_ref, slots)
    tables = tables_ref[2], tables_ref[3]
    grad = spectrum(x_ref, SECOND_SLOT, slots, special, *tables)
    field = spectrum(y_ref, SECOND_SLOT, slots, special, *tables)
    put_terms(terms_ref, SECOND_SLOT, slots, near, field, grad)
    at = 2 * GROUPS
    second_edges = edge_terms(
        edge_spectrum(y_ref, at, tables), edge_spectrum(x_ref, at, tables)
    )
    slots = H1 // 8
    special, near = masks(place_ref, slots)
    tables = tables_ref[0], tables_ref[1]
    field = spectrum(x_ref, 0, slots, special, *tables)
    grad = spectrum(y_ref, 0, slots, special, *tables)
    put_terms(terms_ref, 0, slots, near, field, grad)
    edges = edge_terms(edge_spectrum(x_ref, 0, tables), edge_spectrum(y_ref, 0, tables))
    filled = jnp.zeros((EDGE_ROWS - 4 * GROUPS, 512), jnp.float32)
    edges = jnp.concatenate(edges + second_edges + [filled], axis=0).astype(jnp.bfloat16)
    for q in range(COLS):
        terms_ref[q, 2 * FILTER_ROWS :, :] = edges[:, q * LANES : (q + 1) * LANES]
    copy = pltpu.make_async_copy(terms_ref, total_ref, sem)
    copy.start()
    real, imag = filters(near, kept_ref, recv_ref, 0, slots)
    up, down = apply_back(real, imag, grad)
    put_inverse(out_ref, 0, slots, special, up, down, *tables)
    copy.wait()


def smem():
    return pl.BlockSpec(memory_space=pltpu.SMEM)


def hbm(count):
    return [pl.BlockSpec(memory_space=pltpu.HBM)] * count


def vmem(count):
    return [pl.BlockSpec()] * count


def both_tables():
    return constant(np.stack(col_tables(H1) + col_tables(H2)))


def mix_first(place, entries, kept, recv):
    return pl.pallas_call(
        mix_first_kernel,
        out_shape=jax.ShapeDtypeStruct((COLS, FILTER_ROWS, LANES), jnp.bfloat16),
        in_specs=[smem()] + vmem(4),
        name="mix_first",
        **params(8 * FILTER_ROWS * 512 * 512, 6 << 20),
    )(place, entries, kept, recv, both_tables())


def mix_last(place, entries, later, kept, recv):
    total = (COLS, 2 * FILTER_ROWS + EDGE_ROWS, LANES)
    return pl.pallas_call(
        mix_last_kernel,
        out_shape=(
            jax.ShapeDtypeStruct((COLS, SECOND_SLOT, LANES), jnp.bfloat16),
            jax.ShapeDtypeStruct(total, jnp.bfloat16),
        ),
        in_specs=[smem()] + vmem(5),
        out_specs=tuple(vmem(1) + hbm(1)),
        scratch_shapes=[pltpu.VMEM(total, jnp.bfloat16), pltpu.SemaphoreType.DMA],
        name="mix_last",
        **params(12 * FILTER_ROWS * 512 * 512, 8 << 20),
    )(place, entries, later, kept, recv, both_tables())


def grid_of(rows, columns):
    shape = (rows, columns)
    return lax.broadcasted_iota(jnp.int32, shape, 0), lax.broadcasted_iota(jnp.int32, shape, 1)


def ones_at(mask):
    return jnp.where(mask, 1.0, 0.0).astype(jnp.bfloat16)


def kept_rows(near, slots):
    slot, local = grid_of(slots, 2 * slots)
    return ones_at(local == jnp.where(near, slot, slots - slot))


def sent_rows(near, slots):
    slot, local = grid_of(slots, 2 * slots)
    return ones_at(local == jnp.where(near, slots + slot, lax.rem(2 * slots - slot, 2 * slots)))


def quarter_lanes(quarter):
    wide_at, narrow_at = grid_of(512, LANES)
    return ones_at(
        wide_at == lax.div(narrow_at, 64) * 256 + 64 * quarter + lax.rem(narrow_at, 64)
    )


def second_pair(ref, part, g):
    pair = [ref[part, 2 * g + i].astype(jnp.bfloat16) for i in range(2)]
    return jnp.concatenate(pair, axis=1)


def send_filters_kernel(
    place_ref, quarter_ref, first_ref, second_ref, sent_ref, zero_ref, first_buf, second_buf, sems
):
    quarter = quarter_ref[0]
    at = pl.ds(pl.multiple_of(quarter * LANES, LANES), LANES)
    first_copy = pltpu.make_async_copy(first_ref.at[:, :, :, at], first_buf, sems.at[0])
    second_copy = pltpu.make_async_copy(second_ref, second_buf, sems.at[1])
    first_copy.start()
    second_copy.start()
    near = place_ref[0] < 2
    lanes = quarter_lanes(quarter)
    groups = [(part, g) for part in range(2) for g in range(GROUPS)]
    zeros = []
    first = 0
    for n in (H1, H2):
        slots = n // 8
        if n == H1:
            first_copy.wait()
            rows = [first_buf[part, g].astype(jnp.bfloat16) for part, g in groups]
        else:
            second_copy.wait()
            rows = [second_pair(second_buf, part, g) for part, g in groups]
            rows = dot(jnp.concatenate(rows, axis=0), lanes).astype(jnp.bfloat16)
            rows = [rows[2 * slots * i : 2 * slots * (i + 1)] for i in range(len(groups))]
        rows = dot(sent_rows(near, slots), jnp.concatenate(rows, axis=1))
        for i in range(len(groups)):
            picked = rows[:, i * LANES : (i + 1) * LANES]
            zeros.append(picked[:1])
            sent_ref[first : first + slots, :] = picked.astype(jnp.bfloat16)
            first += slots
    zeros.append(jnp.zeros((4, LANES), jnp.float32))
    zero_ref[...] = jnp.concatenate(zeros, axis=0).astype(jnp.bfloat16)


def keep_filters_kernel(place_ref, first_ref, second_ref, kept_ref):
    near = place_ref[0] < 2
    first = 0
    lanes = [quarter_lanes(q) for q in range(COLS)]
    for n in (H1, H2):
        slots = n // 8
        pick = kept_rows(near, slots)
        for part in range(2):
            for g in range(GROUPS):
                if n == H1:
                    rows = first_ref[part, g].astype(jnp.bfloat16)
                else:
                    rows = second_pair(second_ref, part, g)
                rows = dot(pick, rows).astype(jnp.bfloat16)
                for q in range(COLS):
                    if n == H1:
                        cut = rows[:, q * LANES : (q + 1) * LANES]
                    else:
                        cut = dot(rows, lanes[q]).astype(jnp.bfloat16)
                    kept_ref[q, first : first + slots, :] = cut
                first += slots


def send_filters(place, quarter, filter_first, filter_second):
    return pl.pallas_call(
        send_filters_kernel,
        out_shape=(
            jax.ShapeDtypeStruct((FILTER_ROWS, LANES), jnp.bfloat16),
            jax.ShapeDtypeStruct((16, LANES), jnp.bfloat16),
        ),
        in_specs=[smem()] * 2 + hbm(2),
        scratch_shapes=[
            pltpu.VMEM((2, GROUPS, H1 // 4, LANES), jnp.float32),
            pltpu.VMEM((2, 2 * GROUPS, H2 // 4, H2), jnp.float32),
            pltpu.SemaphoreType.DMA((2,)),
        ],
        name="send_filters",
        **params(12 * 64 * 512 * 128 * 2, 2 << 20, 60),
    )(place, quarter, filter_first, filter_second)


def keep_filters(place, filter_first, filter_second):
    return pl.pallas_call(
        keep_filters_kernel,
        out_shape=jax.ShapeDtypeStruct((COLS, FILTER_ROWS, LANES), jnp.bfloat16),
        in_specs=[smem()] + vmem(2),
        name="keep_filters",
        **params(12 * 64 * 512 * 512 * 2, 4 << 20),
    )(place, filter_first, filter_second)


def put_slot_zero(block, zero, take, slots):
    shaped = block.reshape(2 * GROUPS, slots, LANES)
    here = (jnp.arange(slots) == 0)[None, :, None] & take
    return jnp.where(here, zero[:, None, :], shaped).reshape(2 * GROUPS * slots, LANES)


def put_slots_zero(block, zero, take):
    split, groups = 2 * GROUPS * H1 // 8, 2 * GROUPS
    return (
        put_slot_zero(block[:split], zero[:groups], take, H1 // 8),
        put_slot_zero(block[split:], zero[groups : 2 * groups], take, H2 // 8),
    )


def swap_filters(sent, zero):
    return lax.ppermute(sent, "col", SWAP), lax.ppermute(zero, "col", ((2, 0), (3, 1)))


def patch_filters(recv, zero, col):
    recv = jnp.concatenate(put_slots_zero(recv, zero, col < 2), axis=0)
    return lax.all_gather(recv, "rep", axis=0, tiled=False)


def place_grads_kernel(
    place_ref, kept_first, recv_first, kept_second, recv_second, first_ref, second_ref
):
    near = place_ref[0] < 2
    wide_at, narrow_at = grid_of(LANES, LANES // 2)
    lanes = [ones_at(wide_at == narrow_at + 64 * i) for i in range(2)]
    groups = [(part, g) for part in range(2) for g in range(GROUPS)]
    for n, kept, recv in ((H1, kept_first, recv_first), (H2, kept_second, recv_second)):
        slots = n // 8
        local, slot = grid_of(2 * slots, slots)
        mirror = lax.rem(2 * slots - slot, 2 * slots)
        pick_kept = ones_at(local == jnp.where(near, slot, slots - slot))
        pick_recv = ones_at(local == jnp.where(near, slots + slot, mirror))
        kept, recv = [
            jnp.concatenate([ref[i * slots : (i + 1) * slots] for i in range(len(groups))], axis=1)
            for ref in (kept, recv)
        ]
        rows = dot(pick_kept, kept) + dot(pick_recv, recv)
        rows = [rows[:, i * LANES : (i + 1) * LANES] for i in range(len(groups))]
        if n == H1:
            for (part, g), block in zip(groups, rows):
                first_ref[part, g] = block
        else:
            rows = jnp.concatenate(rows, axis=0).astype(jnp.bfloat16)
            for i in range(2):
                half = dot(rows, lanes[i])
                for at, (part, g) in enumerate(groups):
                    second_ref[part, 2 * g + i] = half[at * 2 * slots : (at + 1) * 2 * slots]


def summed(terms):
    return lax.psum_scatter(terms, "rep", scatter_dimension=0, tiled=False)


def place_grads(place, kept, recv, edges, col):
    recv_first, recv_second = put_slots_zero(recv, edges, col >= 2)
    return pl.pallas_call(
        place_grads_kernel,
        out_shape=(
            jax.ShapeDtypeStruct((2, GROUPS, H1 // 4, LANES), jnp.float32),
            jax.ShapeDtypeStruct((2, 2 * GROUPS, H2 // 4, LANES // 2), jnp.float32),
        ),
        in_specs=[smem()] + vmem(4),
        name="place_grads",
        **params(12 * 128 * 128 * 128 * 2, 2 << 20),
    )(place, kept[:SECOND_SLOT], recv_first, kept[SECOND_SLOT:], recv_second)


def layer_normalize(entry_values, gains):
    center = entry_values - jnp.mean(entry_values, axis=1, keepdims=True)
    spread = jnp.mean(center * center, axis=1, keepdims=True)
    return center * lax.rsqrt(spread + epsilon) * gains[None, :, None, None]


def norm_pullback_step(entry_values, gains, upstream):
    _, pullback = jax.vjp(lambda inner_vals: layer_normalize(inner_vals, gains), entry_values)
    return pullback(upstream.astype(jnp.float32))[0]


def fold(values):
    total = jnp.broadcast_to(jnp.sum(values, axis=0, keepdims=True), (8, LANES))
    return (total + pltpu.roll(total, LANES // 2, 1))[:1]


def standardize(values):
    center = values - fold(values) / 192.0
    scale = lax.rsqrt(fold(center * center) / 192.0 + epsilon)
    return center * scale, scale


def pack_pairs(block):
    at, lane = grid_of(LANES, 192)
    mine = lax.rem(lane, 2) == lax.div(at, 64)
    fields = []
    for i in range(8):
        field = block[i].astype(jnp.float32)
        fields.append(jnp.where(mine, jnp.concatenate([field, field], axis=0), 0.0))
    at, lane = grid_of(96, 192)
    return lax.dot_general(
        ones_at(lax.div(lane, 2) == at),
        jnp.concatenate(fields, axis=0).astype(jnp.bfloat16),
        (((1,), (1,)), ((), ())),
        preferred_element_type=jnp.float32,
    )


def first_norm_kernel(
    x_ref, g_ref, gain_ref, out_ref, x_buf, g_buf, gain_buf, pack_buf, sems
):
    copies = [
        pltpu.make_async_copy(source, target, sems.at[i])
        for i, (source, target) in enumerate(
            ((x_ref, x_buf), (gain_ref, gain_buf), (g_ref, g_buf))
        )
    ]
    for copy in copies:
        copy.start()
    copies[0].wait()
    copies[1].wait()
    pixels = x_buf[...].astype(jnp.float32)
    center = pixels - jnp.sum(pixels, axis=0, keepdims=True) / 96.0
    scale = lax.rsqrt(jnp.sum(center * center, axis=0) / 96.0 + epsilon)
    for c in range(96):
        at = (c % GROUPS) * 16
        out_ref[c // GROUPS, at : at + 16, :] = (center[c] * scale * gain_buf[c]).astype(
            jnp.bfloat16
        )
    copies[2].wait()
    packed = pack_pairs(g_buf[...])
    for i in range(8):
        pack_buf[pl.ds(i, 96, stride=8), :] = packed[:, i * LANES : (i + 1) * LANES]
    packed = pack_buf[...].reshape(ROWS, GROUPS * 8, LANES)
    out_ref[:, GROUPS * 16 :, :] = packed.astype(jnp.bfloat16)


def first_norm(images, grad_out, gains):
    return pl.pallas_call(
        first_norm_kernel,
        out_shape=jax.ShapeDtypeStruct((ROWS, GROUPS * 24, LANES), jnp.bfloat16),
        in_specs=hbm(3),
        scratch_shapes=[
            pltpu.VMEM((96, 16, LANES), jnp.bfloat16),
            pltpu.VMEM((8, 64, 192), jnp.bfloat16),
            pltpu.SMEM((96,), jnp.float32),
            pltpu.VMEM((768, LANES), jnp.float32),
            pltpu.SemaphoreType.DMA((3,)),
        ],
        name="first_norm",
        **params(4 * 768 * 64 * 128, 2 << 20, 60),
    )(images, grad_out, gains)


def low_half():
    return lax.broadcasted_iota(jnp.int32, (96, LANES), 1) < LANES // 2


def token_kernel(
    x_ref, m_ref, g_ref, w_ref, wt_ref, gain_ref, out_ref, s_ref, n_ref, back_ref, o_ref
):
    at, lane = grid_of(LANES, 2 * LANES)
    spread_at = ones_at(at == 2 * lax.rem(lane, 64) + lax.div(lane, LANES))
    at, lane = grid_of(2 * LANES, 2 * LANES)
    here = LANES * lax.rem(lax.div(at, 64), 2) + 2 * lax.rem(at, 64) + lax.div(at, LANES)
    merge_at = ones_at(lane == here)
    mixed = m_ref[:, : GROUPS * 16, :].astype(jnp.float32).reshape(1536, LANES)
    back_ref[...] = m_ref[:, GROUPS * 16 :, :].astype(jnp.float32).reshape(768, LANES)
    section = x_ref[...].astype(jnp.float32).reshape(1536, LANES) + mixed
    spread = dot(section.astype(jnp.bfloat16), spread_at)
    for e in range(2):
        s_ref[e] = spread[:, e * LANES : (e + 1) * LANES]
    low = low_half()
    packed = pack_pairs(g_ref[...])
    for first in range(0, 8, 2):
        patches = [
            jnp.concatenate(
                [
                    s_ref[e, pl.ds(2 * i + a, 96, stride=16), :].astype(jnp.bfloat16)
                    for a in range(2)
                    for e in range(2)
                ],
                axis=0,
            )
            for i in (first, first + 1)
        ]
        both = dot(w_ref[...], jnp.concatenate(patches, axis=1))
        grads = []
        for i in range(2):
            block = both[:, i * LANES : (i + 1) * LANES]
            down = jnp.where(low, block[:96], block[96:]).astype(jnp.bfloat16)
            normed, scale = standardize(down.astype(jnp.float32))
            rows = pl.ds(first + i, 96, stride=8)
            n_ref[rows, :] = normed * gain_ref[...]
            upstream = back_ref[rows, :] * gain_ref[...]
            step = upstream - fold(upstream) / 192.0 - normed * (fold(upstream * normed) / 192.0)
            at = (first + i) * LANES
            total = packed[:, at : at + LANES] + scale * step
            total = total.astype(jnp.bfloat16).astype(jnp.float32)
            grads.append((total, pltpu.roll(total, LANES // 2, 1)))
        even = jnp.where(low, grads[0][0], grads[1][1])
        odd = jnp.where(low, grads[0][1], grads[1][0])
        both = jnp.concatenate([even, odd], axis=0).astype(jnp.bfloat16)
        patches = dot(wt_ref[...], both).astype(jnp.bfloat16)
        rows = [
            jnp.concatenate(
                [patches[(2 * a + e) * 96 : (2 * a + e + 1) * 96] for e in range(2)], axis=1
            )
            for a in range(2)
        ]
        merged = dot(jnp.concatenate(rows, axis=0), merge_at)
        for i in range(2):
            for a in range(2):
                o_ref[pl.ds(2 * (first + i) + a, 96, stride=16), :] = merged[
                    a * 96 : (a + 1) * 96, i * LANES : (i + 1) * LANES
                ]
    out_ref[:, : GROUPS * 16, :] = (
        o_ref[...].reshape(ROWS, GROUPS * 16, LANES).astype(jnp.bfloat16)
    )
    out_ref[:, GROUPS * 16 :, :] = (
        n_ref[...].reshape(ROWS, GROUPS * 8, LANES).astype(jnp.bfloat16)
    )


def token_step(images, back, grad_out, weight, gains):
    return pl.pallas_call(
        token_kernel,
        out_shape=jax.ShapeDtypeStruct((ROWS, GROUPS * 24, LANES), jnp.bfloat16),
        in_specs=vmem(6),
        scratch_shapes=[
            pltpu.VMEM((2, 1536, LANES), jnp.float32),
            pltpu.VMEM((768, LANES), jnp.float32),
            pltpu.VMEM((768, LANES), jnp.float32),
            pltpu.VMEM((1536, LANES), jnp.float32),
        ],
        name="token_step",
        **params(8 * 2 * 192 * 384 * 256, 4 << 20),
    )(images, back, grad_out, weight, weight.T, gains)


def unpack_first(blocks):
    return blocks.reshape(1, 96, 16, LANES)


def pack_second(field):
    pairs = field.reshape(96, 2, 8, 64).transpose(0, 2, 1, 3)
    return pairs.reshape(ROWS, GROUPS * 8, LANES)


def exchange(blocks, axis):
    return lax.all_to_all(blocks, axis, split_axis=0, concat_axis=0, tiled=True)


def shards(images, gain_first, filter_first, reduce_weight, gain_second, filter_second, grad_out):
    col = lax.axis_index("col")
    place = col.astype(jnp.int32).reshape(1)
    pixels = images.reshape(96, 16, LANES)
    upstream = grad_out.transpose(0, 2, 3, 1).reshape(8, 64, 192)
    weight = reduce_weight.reshape(96, 2, 384).transpose(1, 0, 2).reshape(192, 384)
    gains = jnp.repeat(gain_second.reshape(96, 2), 64, axis=1)

    quarter = lax.axis_index("rep").astype(jnp.int32).reshape(1)
    sent, zero = send_filters(place, quarter, filter_first, filter_second)
    swapped = swap_filters(sent, zero)
    kept = keep_filters(place, filter_first, filter_second)
    both = exchange(first_norm(pixels, upstream, gain_first), "row")
    half = forward_rows(both, (H1, H2))
    half, swapped = lax.optimization_barrier((half, swapped))
    recv = patch_filters(*swapped, col)
    both = exchange(half, "col")
    mixed = exchange(mix_first(place, both, kept, recv), "col")
    mixed = exchange(inverse_rows(mixed, (H1, H2)), "row")
    tokens = token_step(pixels, mixed, upstream, weight, gains)
    later = exchange(forward_rows(exchange(tokens, "row"), (H1, H2)), "col")
    dspec_one, terms = mix_last(place, both, later, kept, recv)
    terms = summed(terms)
    rot_one = exchange(dspec_one, "col")
    rot_one, terms = lax.optimization_barrier((rot_one, terms))
    swapped = lax.ppermute(terms[FILTER_ROWS : 2 * FILTER_ROWS], "col", SWAP)
    grad_norm_one = unpack_first(exchange(inverse_rows(rot_one, (H1,)), "row"))
    grad_images = (
        unpack_first(tokens[:, : GROUPS * 16]).astype(jnp.float32)
        + norm_pullback_step(images.astype(jnp.float32), gain_first, grad_norm_one)
    ).astype(jnp.bfloat16)
    grad_images, swapped = lax.optimization_barrier((grad_images, swapped))
    grad_first, grad_second = place_grads(
        place, terms[:FILTER_ROWS], swapped, terms[2 * FILTER_ROWS :], col
    )
    return (grad_images, grad_first, grad_second)


def solution(mesh):
    placed = (
        P("rep", None, "row", "col"),
        P(),
        P(None, "row", "col", None),
        P(),
        P(),
        P(None, "row", "col", None),
        P("rep", None, "row", "col"),
    )
    return jax.shard_map(
        shards,
        mesh=mesh,
        in_specs=placed,
        out_specs=(
            P("rep", None, "row", "col"),
            P(None, "row", "col", "rep"),
            P(None, "row", "col", "rep"),
        ),
        check_vma=False,
    )
```
